32 devices in a mesh: rows: 8 (over z, x), cols: 4 (over y, core).
Axes of the slice: x: 2, y: 2, z: 4, core: 2. Of those that a mesh axis runs over, the one named last changes fastest.
Arguments:
- warped: bfloat16 [64, 256, 2048], P(None, 'rows', 'cols'), may hold values from -6 to 6
- cotangent: bfloat16 [64, 256, 2048], P(None, 'rows', 'cols'), may hold values from -6 to 6
- w_first: bfloat16 [64, 64, 3, 3], replicated, may hold values from -0.25 to 0.25
- b_first: float32 [64], replicated, may hold values from -4 to 4
- w_second: bfloat16 [64, 64, 3, 3], replicated, may hold values from -0.25 to 0.25
- source_tile: int32 [16, 128], P('rows', 'cols'), may hold values from 0 to 31, as said below
- source_block: int32 [16, 128], P('rows', 'cols'), may hold values from 0 to 63
Outputs:
- frame_grad: float32 [64, 256, 2048], P(None, 'rows', 'cols')
- w_first_grad: float32 [64, 64, 3, 3], replicated
- b_first_grad: float32 [64], replicated
- w_second_grad: float32 [64, 64, 3, 3], replicated
- b_second_grad: float32 [64], replicated
The draws below stay inside these ranges and needn't reach their ends.
Inputs may be any that keep to these rules, and one draw needn't show every extreme that they name: `source_tile`: among the blocks of one tile, at most 2 name the same source tile; in every draw one source tile is named exactly 2 times by the blocks of every tile.
All inputs are finite; a program needn't handle non-finite values.
Results may differ from the reference program's by a relative error of at most 0.005.
Values may be sent and summed in bfloat16 or wider, within the bound.
No kernel may reach another device: no remote copies, remote signals or barrier semaphores. Data moves between devices by JAX's collectives and lax.ppermute only.
A program may use at most 128 MiB of HBM per device.

```python
import math
import jax
import jax.numpy as jnp
from jax import lax

CHANNELS = 64
BLOCK = 16
CAP = 2
HEIGHT = 256
WIDTH = 2048
BR_DEV = 2
BC_DEV = 32
BLK_DEV = 64
NBY = 16
NBX = 128
N_ROWS = 8
N_COLS = 4
DEVICES = 32


def draw_source_tile(key, part):
    tokens = DEVICES * CAP
    hottest = jax.random.randint(jax.random.fold_in(key, 11), (), 0, DEVICES)
    order_keys = jax.random.split(jax.random.fold_in(key, 12), DEVICES)
    orders = jax.vmap(lambda subkey: jax.random.permutation(subkey, tokens))(order_keys)
    tiles = orders // CAP
    scores = jnp.arange(tokens, dtype=jnp.int32)[None, :] + (tiles == hottest).astype(jnp.int32) * tokens
    picked = jnp.argsort(scores, axis=1)
    others = jnp.take_along_axis(tiles, picked, axis=1)[:, :BLK_DEV - CAP]
    chosen = jnp.concatenate([others, jnp.full((DEVICES, CAP), hottest, jnp.int32)], axis=1)
    shuffle_keys = jax.random.split(jax.random.fold_in(key, 13), DEVICES)
    shuffled = jax.vmap(lambda subkey, values: jax.random.permutation(subkey, values))(shuffle_keys, chosen)
    grid = shuffled.reshape(N_ROWS, N_COLS, BR_DEV, BC_DEV).transpose(0, 2, 1, 3).reshape(NBY, NBX)
    return grid.astype(jnp.int32)


def set_ends(drawn, own_key, low, high):
    longest = drawn.shape.index(max(drawn.shape))
    spots = []
    for shift in (0, 1):
        where = [jax.random.randint(jax.random.fold_in(own_key, axis), (), 0, length) for axis, length in enumerate(drawn.shape)]
        where[longest] = (where[longest] + shift) % drawn.shape[longest]
        spots.append(tuple(where))
    return drawn.at[spots[0]].set(low).at[spots[1]].set(high)


def levels(rng, extent, shards, smallest, top_value):
    loudness, own = 1.0, jax.random.fold_in(rng, 6)
    for axis_at, shards_of in shards:
        steps = jnp.exp(jax.random.uniform(jax.random.fold_in(own, axis_at), (shards_of,), jnp.float32, smallest / len(shards), top_value / len(shards)))
        loudness = loudness * jnp.repeat(steps, extent[axis_at] // shards_of).reshape([-1 if axis == axis_at else 1 for axis in range(len(extent))])
    return loudness


def gaussian(rng, extent, spread, reach, shards=(), kind=jnp.bfloat16):
    values = jax.random.normal(rng, extent, jnp.float32) * spread
    if len(shards) > 0:
        values = levels(rng, extent, shards, -0.22, 0.18) * values
    return jnp.clip(values, min=-reach, max=reach).astype(kind)


def setup_inputs(seed: int = 0) -> dict:
    splits = jax.random.split(jax.random.key(seed), 8)
    warped = gaussian(splits[0], (CHANNELS, HEIGHT, WIDTH), 1.0, 6.0, ((1, 8), (2, 4)))
    cotangent = gaussian(splits[1], (CHANNELS, HEIGHT, WIDTH), 1.0, 6.0, ((1, 8), (2, 4)))
    w_first = gaussian(splits[2], (CHANNELS, CHANNELS, 3, 3), (9 * CHANNELS) ** -0.5, 0.25)
    b_first = gaussian(splits[3], (CHANNELS,), 1.0, 4.0, (), jnp.float32)
    w_second = gaussian(splits[4], (CHANNELS, CHANNELS, 3, 3), (9 * CHANNELS) ** -0.5, 0.25)
    source_tile = draw_source_tile(jax.random.fold_in(splits[7], 71), 0)
    source_block = set_ends(jax.random.randint(splits[6], (NBY, NBX), 0, BLK_DEV), jax.random.fold_in(splits[6], 1), 0, BLK_DEV - 1).astype(jnp.int32)
    return {"warped": warped, "cotangent": cotangent, "w_first": w_first, "b_first": b_first, "w_second": w_second, "source_tile": source_tile, "source_block": source_block}


def conv_same(source, kernel):
    padded = jnp.pad(source, ((0, 0), (1, 1), (1, 1)))
    result = lax.conv_general_dilated(padded[None], kernel, (1, 1), 'VALID', dimension_numbers=('NCHW', 'OIHW', 'NCHW'), precision=lax.Precision.HIGHEST)
    return result[0]

def flipped(kernel):
    return jnp.transpose(kernel[:, :, ::-1, ::-1], (1, 0, 2, 3))

def silu_slope(value):
    sigma = jax.nn.sigmoid(value)
    return sigma * (1.0 + value * (1.0 - sigma))

def correlate(image, grads):
    padded = jnp.pad(image, ((0, 0), (1, 1), (1, 1)))
    height = grads.shape[1]
    breadth = grads.shape[2]
    columns = []
    for row_shift in range(3):
        for col_shift in range(3):
            window = padded[:, row_shift:row_shift + height, col_shift:col_shift + breadth]
            columns.append(jnp.einsum('ohw,ihw->oi', grads, window, precision=lax.Precision.HIGHEST))
    stacked = jnp.stack(columns, axis=-1)
    return stacked.reshape(grads.shape[0], image.shape[0], 3, 3)

def reference(warped, cotangent, w_first, b_first, w_second, source_tile, source_block):
    channels, height, breadth = warped.shape
    factor = 1.0 / math.sqrt(height * breadth)
    x_value = warped.astype(jnp.float32)
    act_in = lax.optimization_barrier(jax.nn.silu(x_value).astype(jnp.bfloat16)).astype(jnp.float32)
    kernel_one = w_first.astype(jnp.float32)
    kernel_two = w_second.astype(jnp.float32)
    a_mid = (x_value + conv_same(act_in, kernel_one) + b_first[:, None, None]).astype(jnp.bfloat16).astype(jnp.float32)
    act_mid = lax.optimization_barrier(jax.nn.silu(a_mid).astype(jnp.bfloat16)).astype(jnp.float32)
    grad_out = cotangent.astype(jnp.float32)
    w_second_grad = correlate(act_mid, grad_out) * factor
    b_second_grad = lax.optimization_barrier(jnp.sum(grad_out, axis=(1, 2))) * factor
    back_second = conv_same(grad_out, flipped(kernel_two))
    g_mid = lax.optimization_barrier((grad_out + silu_slope(a_mid) * back_second).astype(jnp.bfloat16)).astype(jnp.float32)
    w_first_grad = correlate(act_in, g_mid) * factor
    b_first_grad = lax.optimization_barrier(jnp.sum(g_mid, axis=(1, 2))) * factor
    back_first = conv_same(g_mid, flipped(kernel_one))
    g_warped = lax.optimization_barrier((g_mid + silu_slope(x_value) * back_first).astype(jnp.bfloat16)).astype(jnp.float32)
    pieces = g_warped.reshape(channels, NBY, BLOCK, NBX, BLOCK).transpose(1, 3, 0, 2, 4).reshape(NBY * NBX, channels * BLOCK * BLOCK)
    tile_row = source_tile // N_COLS
    tile_col = source_tile % N_COLS
    inner_row = source_block // BC_DEV
    inner_col = source_block % BC_DEV
    target = ((tile_row * BR_DEV + inner_row) * NBX + tile_col * BC_DEV + inner_col).reshape(NBY * NBX).astype(jnp.int32)
    summed = jax.ops.segment_sum(pieces, target, num_segments=NBY * NBX)
    frame_grad = summed.reshape(NBY, NBX, channels, BLOCK, BLOCK).transpose(2, 0, 3, 1, 4).reshape(channels, height, breadth)
    return (frame_grad, w_first_grad, b_first_grad, w_second_grad, b_second_grad)
```

```python
import functools
import math

import jax
import jax.numpy as jnp
from jax import lax
from jax.experimental import pallas as pl
from jax.experimental.pallas import tpu as pltpu
from jax.sharding import PartitionSpec as P

BLOCK = 16
CAP = 2
AXES = ("rows", "cols")
BF16 = jnp.bfloat16
F32 = jnp.float32
NT = (((1,), (1,)), ((), ()))
TN = (((0,), (0,)), ((), ()))
VMEM_BYTES = 60 * 2**20


def params(**extra):
    return pltpu.CompilerParams(vmem_limit_bytes=VMEM_BYTES, **extra)


def sigmoid(value):
    return 1.0 / (1.0 + jnp.exp(-value))


def one_hot(shape, pairs):
    row = lax.broadcasted_iota(jnp.int32, shape, 0)
    col = lax.broadcasted_iota(jnp.int32, shape, 1)
    hit = jnp.zeros(shape, jnp.bool_)
    for at_row, at_col in pairs:
        hit = hit | ((row == at_row) & (col == at_col))
    return hit.astype(F32).astype(BF16)


def reorder_kernel(w_ref, c_ref, xw_ref, xc_ref):
    channels, rows, _ = w_ref.shape
    for source, target in ((w_ref, xw_ref), (c_ref, xc_ref)):
        value = source[...].astype(F32)
        swapped = jnp.swapaxes(value, 0, 1)
        target[...] = swapped.reshape(rows * channels, value.shape[2]).astype(BF16)


def reorder(warped, cotangent):
    channels, height, breadth = warped.shape
    step = 16
    lanes = 128
    spec_in = pl.BlockSpec((channels, step, lanes), lambda h, x: (0, h, x))
    spec_out = pl.BlockSpec((step * channels, lanes), lambda h, x: (h, x))
    shape = jax.ShapeDtypeStruct((height * channels, breadth), BF16)
    return pl.pallas_call(
        reorder_kernel,
        grid=(height // step, breadth // lanes),
        in_specs=[spec_in, spec_in],
        out_specs=[spec_out, spec_out],
        out_shape=[shape, shape],
        compiler_params=params(),
        name="reorder",
    )(warped, cotangent)


def edges_kernel(wl_ref, cl_ref, wr_ref, cr_ref, to_right_ref, to_left_ref):
    lanes = wl_ref.shape[1]
    last = lanes - 1
    shape = (16, lanes)

    def pick(ref, pairs):
        return lax.dot_general(one_hot(shape, pairs), ref[...], NT, preferred_element_type=F32)

    to_right_ref[...] = (
        pick(wr_ref, ((0, last - 1), (1, last))) + pick(cr_ref, ((2, last - 1), (3, last)))
    ).astype(BF16)
    to_left_ref[...] = (pick(wl_ref, ((4, 0), (5, 1))) + pick(cl_ref, ((6, 0), (7, 1)))).astype(BF16)


def edges(xw, xc):
    count, breadth = xw.shape
    tiles = breadth // 128
    first = pl.BlockSpec((count, 128), lambda i: (0, 0))
    final = pl.BlockSpec((count, 128), lambda i: (0, tiles - 1))
    whole = pl.BlockSpec((16, count), lambda i: (0, 0))
    shape = jax.ShapeDtypeStruct((16, count), BF16)
    return pl.pallas_call(
        edges_kernel,
        grid=(1,),
        in_specs=[first, first, final, final],
        out_specs=[whole, whole],
        out_shape=[shape, shape],
        compiler_params=params(),
        name="edges",
    )(xw, xc, xw, xc)


def convs_kernel(
    channels, height, breadth,
    flags_ref,
    xw_ref, xc_ref, up_ref, down_ref, side_ref, side_up_ref, side_down_ref,
    w1_ref, w2f_ref, w1f_ref, bias_ref, target_ref,
    packed_ref, act_in_ref, act_mid_ref, g_mid_ref,
    wx, cx, sa, sc, sg, gw,
):
    ch = channels
    wide = breadth + 128
    core = slice(0, breadth)
    rim = slice(breadth, wide)
    body = height * ch

    for at, (target, up_at) in enumerate(((wx, 0), (cx, 1))):
        target[2 * ch : 2 * ch + body, core] = (xw_ref if at == 0 else xc_ref)[...]
        target[0 : 2 * ch, core] = up_ref[up_at * 2 * ch : (up_at + 1) * 2 * ch, :]
        target[2 * ch + body :, core] = down_ref[up_at * 2 * ch : (up_at + 1) * 2 * ch, :]
        low = 2 * at
        spread = one_hot((16, 128), ((low, 126), (low + 1, 127), (low + 4, 0), (low + 5, 1)))

        def side(ref):
            return lax.dot_general(ref[...], spread, TN, preferred_element_type=F32).astype(BF16)

        target[2 * ch : 2 * ch + body, rim] = side(side_ref)
        target[0 : 2 * ch, rim] = side(side_up_ref)
        target[2 * ch + body :, rim] = side(side_down_ref)

    def shifted(value):
        return (
            pltpu.roll(value, 1, 1).astype(BF16),
            value.astype(BF16),
            pltpu.roll(value, wide - 1, 1).astype(BF16),
        )

    def prepare(row, _):
        at = pl.multiple_of(row * ch, ch)
        out = pl.multiple_of(row * 3 * ch, ch)
        value = wx[pl.ds(at, ch), :].astype(F32)
        act = value * sigmoid(value)
        for shift, moved in enumerate(shifted(act)):
            sa[pl.ds(out + shift * ch, ch), :] = moved
        for shift, moved in enumerate(shifted(cx[pl.ds(at, ch), :].astype(F32))):
            sc[pl.ds(out + shift * ch, ch), :] = moved
        return 0

    lax.fori_loop(0, height + 4, prepare, 0)

    def keep_act(row, _):
        act_in_ref[pl.ds(pl.multiple_of(row * ch, ch), ch), :] = sa[
            pl.ds(pl.multiple_of((row + 1) * 3 * ch + ch, ch), ch), :
        ]
        return 0

    lax.fori_loop(0, height + 2, keep_act, 0)

    lane = lax.broadcasted_iota(jnp.int32, (2 * ch, wide), 1)
    sub = lax.broadcasted_iota(jnp.int32, (2 * ch, wide), 0)
    lane_ok = (
        (lane < breadth)
        | ((lane == breadth) & (flags_ref[3] == 1))
        | ((lane == wide - 1) & (flags_ref[2] == 1))
    )

    def middle(pair, _):
        row = pair * 2
        window = pl.ds(pl.multiple_of(row * 3 * ch, ch), 12 * ch)
        here = pl.ds(pl.multiple_of((row + 1) * ch, ch), 2 * ch)
        conv = jnp.dot(w1_ref[...], sa[window, :], preferred_element_type=F32)
        a_mid = (wx[here, :].astype(F32) + conv + bias_ref[:, 0:1]).astype(BF16).astype(F32)
        back = jnp.dot(w2f_ref[...], sc[window, :], preferred_element_type=F32)
        sigma = sigmoid(a_mid)
        slope = sigma * (1.0 + a_mid * (1.0 - sigma))
        grad = cx[here, :].astype(F32) + slope * back
        top_ok = (row > 0) | (flags_ref[0] == 1)
        low_ok = (row < height) | (flags_ref[1] == 1)
        good = lane_ok & (((sub < ch) & top_ok) | ((sub >= ch) & low_ok))
        act = jnp.where(good, a_mid * sigma, 0.0)
        grad = jnp.where(good, grad, 0.0)
        act_mid_ref[pl.ds(pl.multiple_of(row * ch, ch), 2 * ch), :] = act.astype(BF16)
        out = pl.multiple_of(row * 3 * ch, ch)
        for shift, moved in enumerate(shifted(grad)):
            sg[pl.ds(out + shift * ch, ch), :] = moved[:ch]
            sg[pl.ds(out + (3 + shift) * ch, ch), :] = moved[ch:]
        return 0

    lax.fori_loop(0, height // 2 + 1, middle, 0)

    def last(pair, _):
        row = pair * 2
        base = pl.multiple_of(row * 3 * ch, ch)
        back = jnp.dot(w1f_ref[...], sg[pl.ds(base, 12 * ch), core], preferred_element_type=F32)
        value = wx[pl.ds(pl.multiple_of((row + 2) * ch, ch), 2 * ch), core].astype(F32)
        sigma = sigmoid(value)
        slope = sigma * (1.0 + value * (1.0 - sigma))
        mid = jnp.concatenate(
            [sg[pl.ds(base + 4 * ch, ch), core], sg[pl.ds(base + 7 * ch, ch), core]], axis=0
        )
        at = pl.ds(pl.multiple_of(row * ch, ch), 2 * ch)
        g_mid_ref[at, :] = mid
        gw[at, :] = (mid.astype(F32) + slope * back).astype(BF16)
        return 0

    lax.fori_loop(0, height // 2, last, 0)

    size = 256
    strip = BLOCK * ch

    def pack(part, _):
        start = pl.multiple_of(part * size, size)
        row_at = lax.broadcasted_iota(jnp.int32, (size, breadth), 0) + start
        total = None
        for band in range(height // BLOCK):
            chosen = (row_at == target_ref[band : band + 1, :]).astype(F32).astype(BF16)
            term = lax.dot_general(
                chosen, gw[band * strip : (band + 1) * strip, :], NT, preferred_element_type=F32
            )
            total = term if total is None else total + term
        packed_ref[pl.ds(start, size), :] = total.astype(BF16)
        return 0

    lax.fori_loop(0, packed_ref.shape[0] // size, pack, 0)


def convs(sizes, flags, operands, slots):
    channels, height, breadth = sizes
    wide = breadth + 128
    vmem = pl.BlockSpec(memory_space=pltpu.VMEM)
    outs = [
        jax.ShapeDtypeStruct((slots * BLOCK, BLOCK * channels), BF16),
        jax.ShapeDtypeStruct(((height + 2) * channels, wide), BF16),
        jax.ShapeDtypeStruct(((height + 2) * channels, wide), BF16),
        jax.ShapeDtypeStruct((height * channels, breadth), BF16),
    ]
    return pl.pallas_call(
        functools.partial(convs_kernel, channels, height, breadth),
        in_specs=[pl.BlockSpec(memory_space=pltpu.SMEM)] + [vmem] * len(operands),
        out_specs=[vmem] * len(outs),
        out_shape=outs,
        scratch_shapes=[
            pltpu.VMEM(((height + 4) * channels, wide), BF16),
            pltpu.VMEM(((height + 4) * channels, wide), BF16),
            pltpu.VMEM(((height + 4) * 3 * channels, wide), BF16),
            pltpu.VMEM(((height + 4) * 3 * channels, wide), BF16),
            pltpu.VMEM(((height + 2) * 3 * channels, wide), BF16),
            pltpu.VMEM((height * channels, breadth), BF16),
        ],
        compiler_params=params(),
        name="convs",
    )(flags, *operands)


def correlate_kernel(
    channels, height, breadth,
    act_in_ref, act_mid_ref, g_mid_ref, xc_ref, out_ref, s1, s2, acc1, acc2, b1, b2,
):
    ch = channels
    wide = breadth + 128
    core = slice(0, breadth)

    def prepare(row, _):
        at = pl.multiple_of(row * ch, ch)
        out = pl.multiple_of(row * 3 * ch, ch)
        for source, target in ((act_in_ref, s1), (act_mid_ref, s2)):
            value = source[pl.ds(at, ch), :].astype(F32)
            target[pl.ds(out, ch), :] = pltpu.roll(value, 1, 1)[:, core].astype(BF16)
            target[pl.ds(out + ch, ch), :] = source[pl.ds(at, ch), core]
            target[pl.ds(out + 2 * ch, ch), :] = pltpu.roll(value, wide - 1, 1)[:, core].astype(BF16)
        return 0

    lax.fori_loop(0, height + 2, prepare, 0)
    for ref in (acc1, acc2, b1, b2):
        ref[...] = jnp.zeros_like(ref)
    ones = jnp.ones((16, breadth), BF16)

    def add(pair, _):
        window = pl.ds(pl.multiple_of(pair * 6 * ch, ch), 12 * ch)
        here = pl.ds(pl.multiple_of(pair * 2 * ch, ch), 2 * ch)
        for image, grads, acc, bias in ((s1, g_mid_ref, acc1, b1), (s2, xc_ref, acc2, b2)):
            grad = grads[here, :]
            acc[...] += lax.dot_general(image[window, :], grad, NT, preferred_element_type=F32)
            bias[...] += lax.dot_general(ones, grad, NT, preferred_element_type=F32)
        return 0

    lax.fori_loop(0, height // 2, add, 0)

    def fold(acc, bias):
        taps = acc[0 : 9 * ch, :] + pltpu.roll(acc[3 * ch : 12 * ch, :], ch, 1)
        return taps, bias[0:8, :] + pltpu.roll(bias[0:8, :], ch, 1)

    first, first_bias = fold(acc1, b1)
    second, second_bias = fold(acc2, b2)
    low = lax.broadcasted_iota(jnp.int32, (9 * ch, 2 * ch), 1) < ch
    out_ref[0 : 9 * ch, :] = jnp.where(low, first, pltpu.roll(second, ch, 1))
    out_ref[9 * ch :, :] = jnp.where(low[0:8], first_bias, pltpu.roll(second_bias, ch, 1))


def correlate(sizes, act_in, act_mid, g_mid, xc):
    channels, height, breadth = sizes
    vmem = pl.BlockSpec(memory_space=pltpu.VMEM)
    flops = 2 * 2 * 12 * channels * 2 * channels * breadth * (height // 2)
    return pl.pallas_call(
        functools.partial(correlate_kernel, channels, height, breadth),
        in_specs=[vmem] * 4,
        out_specs=vmem,
        out_shape=jax.ShapeDtypeStruct((9 * channels + 8, 2 * channels), F32),
        scratch_shapes=[
            pltpu.VMEM(((height + 2) * 3 * channels, breadth), BF16),
            pltpu.VMEM(((height + 2) * 3 * channels, breadth), BF16),
            pltpu.VMEM((12 * channels, 2 * channels), F32),
            pltpu.VMEM((12 * channels, 2 * channels), F32),
            pltpu.VMEM((16, 2 * channels), F32),
            pltpu.VMEM((16, 2 * channels), F32),
        ],
        compiler_params=params(),
        cost_estimate=pl.CostEstimate(flops=flops, bytes_accessed=10**7, transcendentals=0),
        name="correlate",
    )(act_in, act_mid, g_mid, xc)


def unpack_kernel(channels, block_rows, arrived_ref, owner_ref, out_ref, flat):
    rows, depth = arrived_ref.shape
    part = out_ref.shape[3]
    lanes = out_ref.shape[4]

    @pl.when(pl.program_id(1) == 0)
    def _():
        flat[...] = arrived_ref[...].T

    column = pl.program_id(1) * lanes + lax.broadcasted_iota(jnp.int32, (rows, lanes), 1)
    breadth = lanes * pl.num_programs(1)
    for band in range(block_rows):
        chosen = (owner_ref[...] == column + band * breadth).astype(F32).astype(BF16)
        summed = jnp.dot(flat[...], chosen, preferred_element_type=F32)
        cube = summed.reshape(part, channels, lanes)
        out_ref[:, band, 0, :, :] = jnp.swapaxes(cube, 0, 1)


def unpack(sizes, arrived, owner):
    channels, height, breadth = sizes
    block_rows = height // BLOCK
    rows = arrived.shape[0]
    part = 8
    lanes = 128
    return pl.pallas_call(
        functools.partial(unpack_kernel, channels, block_rows),
        grid=(BLOCK // part, breadth // lanes),
        in_specs=[
            pl.BlockSpec((rows, part * channels), lambda h, x: (0, h)),
            pl.BlockSpec((rows, 1), lambda h, x: (0, 0)),
        ],
        out_specs=pl.BlockSpec(
            (channels, block_rows, 1, part, lanes), lambda h, x: (0, 0, h, 0, x)
        ),
        out_shape=jax.ShapeDtypeStruct((channels, block_rows, BLOCK // part, part, breadth), F32),
        scratch_shapes=[pltpu.VMEM((part * channels, rows), BF16)],
        compiler_params=params(),
        name="unpack",
    )(arrived, owner)


def pair_weights(kernel):
    taps = jnp.transpose(kernel, (0, 2, 3, 1)).reshape(kernel.shape[0], -1)
    third = taps.shape[1] // 3
    return jnp.concatenate(
        [jnp.pad(taps, ((0, 0), (0, third))), jnp.pad(taps, ((0, 0), (third, 0)))], axis=0
    )


def flipped(kernel):
    return jnp.transpose(kernel[:, :, ::-1, ::-1], (1, 0, 2, 3))


def shift_pairs(axis, step):
    count = lax.axis_size(axis)
    return [(i, i + step) for i in range(count) if 0 <= i + step < count]


def total_over_devices(terms, devices):
    me = lax.axis_index(AXES)
    bit = me % 2
    halves = terms.reshape(2, terms.shape[0] // 2, terms.shape[1])
    swap = [(i, i ^ 1) for i in range(devices)]
    mine = lax.dynamic_index_in_dim(halves, bit, 0, keepdims=False)
    away = lax.dynamic_index_in_dim(halves, 1 - bit, 0, keepdims=False)
    total = mine + lax.ppermute(away, AXES, swap)
    step = 2
    while step < devices:
        total = total + lax.ppermute(total, AXES, [(i, i ^ step) for i in range(devices)])
        step *= 2
    other = lax.ppermute(total, AXES, swap)
    first = jnp.where(bit == 0, total, other)
    second = jnp.where(bit == 0, other, total)
    return jnp.concatenate([first, second], axis=0)


def body(warped, cotangent, w_first, b_first, w_second, source_tile, source_block):
    sizes = warped.shape
    channels, height, breadth = sizes
    row_count = lax.axis_size("rows")
    col_count = lax.axis_size("cols")
    devices = row_count * col_count
    slots = devices * CAP
    factor = 1.0 / math.sqrt(height * row_count * breadth * col_count)
    row_at = lax.axis_index("rows")
    col_at = lax.axis_index("cols")
    me = lax.axis_index(AXES)

    block_rows = height // BLOCK
    count = source_tile.size
    target = source_tile.reshape(count)
    same = target[:, None] == target[None, :]
    earlier = jnp.arange(count)[None, :] < jnp.arange(count)[:, None]
    ranking = jnp.sum((same & earlier).astype(jnp.int32), axis=1)
    places = target * CAP + ranking
    target_row = (
        places.reshape(block_rows, -1, 1) * BLOCK + jnp.arange(BLOCK, dtype=jnp.int32)
    ).reshape(block_rows, breadth)
    hits = places[:, None] == jnp.arange(slots, dtype=jnp.int32)[None, :]
    labels = jnp.sum(jnp.where(hits, source_block.reshape(count, 1) + 1, 0), axis=0) - 1

    xw, xc = reorder(warped, cotangent)
    to_right, to_left = edges(xw, xc)
    rim = 2 * channels
    to_down = jnp.concatenate([xw[-rim:], xc[-rim:]], axis=0)
    to_up = jnp.concatenate([xw[:rim], xc[:rim]], axis=0)
    side = lax.ppermute(to_right, "cols", shift_pairs("cols", 1)) + lax.ppermute(
        to_left, "cols", shift_pairs("cols", -1)
    )
    up = lax.ppermute(to_down, "rows", shift_pairs("rows", 1))
    down = lax.ppermute(to_up, "rows", shift_pairs("rows", -1))
    side_up = lax.ppermute(side[:, -rim:], "rows", shift_pairs("rows", 1))
    side_down = lax.ppermute(side[:, :rim], "rows", shift_pairs("rows", -1))

    flags = jnp.stack(
        [row_at > 0, row_at < row_count - 1, col_at > 0, col_at < col_count - 1]
    ).astype(jnp.int32)
    bias = jnp.broadcast_to(jnp.tile(b_first, 2)[:, None], (2 * channels, 128))
    packed, act_in, act_mid, g_mid = convs(
        sizes,
        flags,
        (
            xw, xc, up, down, side, side_up, side_down,
            pair_weights(w_first), pair_weights(flipped(w_second)), pair_weights(flipped(w_first)),
            bias, target_row,
        ),
        slots,
    )
    arrived = lax.all_to_all(
        packed.reshape(devices, CAP * BLOCK, BLOCK * channels),
        AXES,
        split_axis=0,
        concat_axis=0,
        tiled=True,
    )

    terms = correlate(sizes, act_in, act_mid, g_mid, xc)
    mine = jnp.arange(devices, dtype=jnp.int32)[:, None] == me
    table = jnp.where(mine, labels.astype(F32)[None, :], 0.0).reshape(-1, 128)
    used = terms.shape[0] + table.shape[0]
    fill = jnp.zeros((-used % 16, 128), F32)
    summed = total_over_devices(jnp.concatenate([terms, table, fill], axis=0), devices)
    owners = lax.dynamic_slice_in_dim(
        summed[terms.shape[0] : used].reshape(devices, slots), me * CAP, CAP, axis=1
    ).astype(jnp.int32)
    owner_row = (
        owners.reshape(slots, 1) * BLOCK + jnp.arange(BLOCK, dtype=jnp.int32)[None, :]
    ).reshape(slots * BLOCK, 1)
    owner_row = jnp.where(owner_row < 0, -(2**20), owner_row)

    frame = unpack(sizes, arrived.reshape(slots * BLOCK, BLOCK * channels), owner_row)
    taps = (
        summed[: 9 * channels].reshape(3, 3, channels, 2, channels).transpose(3, 4, 2, 0, 1) * factor
    )
    biases = summed[9 * channels].reshape(2, channels) * factor
    return (frame.reshape(sizes), taps[0], biases[0], taps[1], biases[1])


def solution(mesh):
    in_specs = (
        P(None, "rows", "cols"),
        P(None, "rows", "cols"),
        P(),
        P(),
        P(),
        P("rows", "cols"),
        P("rows", "cols"),
    )
    out_specs = (P(None, "rows", "cols"), P(), P(), P(), P())
    return jax.shard_map(body, mesh=mesh, in_specs=in_specs, out_specs=out_specs, check_vma=False)
```

```python
import functools
import math

import jax
import jax.numpy as jnp
from jax import lax
from jax.experimental import pallas as pl
from jax.experimental.pallas import tpu as pltpu
from jax.sharding import PartitionSpec as P

BLOCK = 16
CAP = 2
AXES = ("rows", "cols")
BF16 = jnp.bfloat16
F32 = jnp.float32
NT = (((1,), (1,)), ((), ()))
TN = (((0,), (0,)), ((), ()))
VMEM_BYTES = 60 * 2**20


def params(**extra):
    return pltpu.CompilerParams(vmem_limit_bytes=VMEM_BYTES, **extra)


def sigmoid(value):
    return 0.5 * jnp.tanh(0.5 * value) + 0.5


def one_hot(shape, pairs):
    row = lax.broadcasted_iota(jnp.int32, shape, 0)
    col = lax.broadcasted_iota(jnp.int32, shape, 1)
    hit = jnp.zeros(shape, jnp.bool_)
    for at_row, at_col in pairs:
        hit = hit | ((row == at_row) & (col == at_col))
    return hit.astype(F32).astype(BF16)


def shifted(value):
    wide = value.shape[1]
    return (
        pltpu.roll(value, 1, 1).astype(BF16),
        value.astype(BF16),
        pltpu.roll(value, wide - 1, 1).astype(BF16),
    )


def slope_of(value, sigma):
    return sigma * (1.0 + value * (1.0 - sigma))


def at_row(row, rows, channels):
    return pl.ds(pl.multiple_of(row * channels, channels), rows * channels)


def reorder_kernel(w_ref, c_ref, xw_ref, xc_ref, to_right_ref, to_left_ref, to_up_ref, to_down_ref):
    channels, rows, lanes = w_ref.shape
    rim = 2 * channels
    kept = []
    for source, target in ((w_ref, xw_ref), (c_ref, xc_ref)):
        value = source[...].astype(F32)
        swapped = jnp.swapaxes(value, 0, 1).reshape(rows * channels, lanes).astype(BF16)
        target[...] = swapped
        kept.append(swapped)

    @pl.when(pl.program_id(1) == 0)
    def _():
        to_up_ref[0:rim, :] = kept[0][0:rim]
        to_up_ref[rim:, :] = kept[1][0:rim]

    @pl.when(pl.program_id(1) == pl.num_programs(1) - 1)
    def _():
        to_down_ref[0:rim, :] = kept[0][rows * channels - rim :]
        to_down_ref[rim:, :] = kept[1][rows * channels - rim :]

    here = pl.ds(pl.multiple_of(pl.program_id(1) * rows * channels, 128), rows * channels)

    def pick(tile, w_pairs, c_pairs):
        return sum(
            lax.dot_general(
                one_hot((16, 128), pairs), value[:, tile], NT, preferred_element_type=F32
            )
            for value, pairs in zip(kept, (w_pairs, c_pairs))
        ).astype(BF16)

    @pl.when(pl.program_id(0) == pl.num_programs(0) - 1)
    def _():
        final = slice(lanes - 128, lanes)
        to_right_ref[:, here] = pick(final, ((0, 126), (1, 127)), ((2, 126), (3, 127)))

    @pl.when(pl.program_id(0) == 0)
    def _():
        to_left_ref[:, here] = pick(slice(0, 128), ((4, 0), (5, 1)), ((6, 0), (7, 1)))


def reorder(warped, cotangent):
    channels, height, breadth = warped.shape
    step = 16
    lanes = 256
    spec_in = pl.BlockSpec((channels, step, lanes), lambda x, h: (0, h, x))
    spec_out = pl.BlockSpec((step * channels, lanes), lambda x, h: (h, x))
    spec_edge = pl.BlockSpec((16, height * channels), lambda x, h: (0, 0))
    spec_rim = pl.BlockSpec((4 * channels, lanes), lambda x, h: (0, x))
    shape = jax.ShapeDtypeStruct((height * channels, breadth), BF16)
    edge = jax.ShapeDtypeStruct((16, height * channels), BF16)
    rim = jax.ShapeDtypeStruct((4 * channels, breadth), BF16)
    return pl.pallas_call(
        reorder_kernel,
        grid=(breadth // lanes, height // step),
        in_specs=[spec_in, spec_in],
        out_specs=[spec_out, spec_out, spec_edge, spec_edge, spec_rim, spec_rim],
        out_shape=[shape, shape, edge, edge, rim, rim],
        compiler_params=params(),
        name="reorder",
    )(warped, cotangent)


def spread_sides(side, first):
    spread = one_hot((16, 128), ((first, 126), (first + 1, 127), (first + 4, 0), (first + 5, 1)))
    return lax.dot_general(side, spread, TN, preferred_element_type=F32).astype(BF16)


def lane_mask(flags_ref, lane, breadth):
    wide = breadth + 128
    return (
        (lane < breadth)
        | ((lane == breadth) & (flags_ref[3] == 1))
        | ((lane == wide - 1) & (flags_ref[2] == 1))
    )


def middle_step(w1_ref, w2f_ref, bias_ref, value, cot, act_window, cot_window):
    conv = jnp.dot(w1_ref[...], act_window, preferred_element_type=F32)
    back = jnp.dot(w2f_ref[...], cot_window, preferred_element_type=F32)
    a_mid = (value.astype(F32) + conv + bias_ref[:, 0:1]).astype(BF16).astype(F32)
    sigma = sigmoid(a_mid)
    return a_mid * sigma, cot.astype(F32) + slope_of(a_mid, sigma) * back


def rim_masked(value, rim_ok, breadth):
    return jnp.concatenate(
        [value[:, :breadth], jnp.where(rim_ok, value[:, breadth:], 0.0)], axis=1
    )


def chosen_blocks(target_ref, band, start, size, breadth):
    row_at = lax.broadcasted_iota(jnp.int32, (size, breadth), 0) + start
    return (row_at == target_ref[band : band + 1, :]).astype(F32).astype(BF16)


def inner_kernel(
    channels, height, breadth,
    flags_ref, xw_ref, xc_ref, side_ref, w1_ref, w2f_ref, w1f_ref, bias_ref, target_ref,
    packed_ref, act_in_ref, act_mid_ref, g_ref, gw_mid_ref,
    wx, cx, sa, sc, sg, gw, act_in, act_mid, grads, packed, sem_in, sem_out,
):
    ch = channels
    wide = breadth + 128
    core = slice(0, breadth)
    rim = slice(breadth, wide)
    loads = [
        pltpu.make_async_copy(xw_ref, wx.at[:, core], sem_in.at[0]),
        pltpu.make_async_copy(xc_ref, cx.at[:, core], sem_in.at[1]),
    ]
    stores = [
        pltpu.make_async_copy(act_in, act_in_ref.at[ch : ch + height * ch, :], sem_out.at[0]),
        pltpu.make_async_copy(act_mid, act_mid_ref.at[2 * ch : height * ch, :], sem_out.at[1]),
        pltpu.make_async_copy(grads, g_ref.at[ch : (height - 1) * ch, :], sem_out.at[2]),
        pltpu.make_async_copy(packed, packed_ref.at[:, 2 * ch : (BLOCK - 2) * ch], sem_out.at[3]),
        pltpu.make_async_copy(
            gw.at[(BLOCK - 2) * ch : (BLOCK + 2) * ch, :], gw_mid_ref, sem_out.at[4]
        ),
    ]
    for load in loads:
        load.start()
    wx[:, rim] = spread_sides(side_ref[...], 0)
    cx[:, rim] = spread_sides(side_ref[...], 2)
    for load in loads:
        load.wait()

    def prepare(row, _):
        here = at_row(row, 1, ch)
        out = pl.multiple_of(row * 3 * ch, ch)
        value = wx[here, :].astype(F32)
        moved = shifted(value * sigmoid(value))
        act_in[here, :] = moved[1]
        for shift in range(3):
            sa[pl.ds(out + shift * ch, ch), :] = moved[shift]
        moved = shifted(cx[here, :].astype(F32))
        for shift in range(3):
            sc[pl.ds(out + shift * ch, ch), :] = moved[shift]
        return 0

    lax.fori_loop(0, height, prepare, 0, unroll=UNROLL_PREPARE)
    stores[0].start()
    lane = lax.broadcasted_iota(jnp.int32, (2 * ch, 128), 1) + breadth
    rim_ok = lane_mask(flags_ref, lane, breadth)

    def middle(pair, _):
        row = pair * 2
        window = at_row(row * 3, 12, ch)
        here = at_row(row + 1, 2, ch)
        act, grad = middle_step(
            w1_ref, w2f_ref, bias_ref, wx[here, :], cx[here, :], sa[window, :], sc[window, :]
        )
        out = at_row(row, 2, ch)
        act_mid[out, :] = rim_masked(act, rim_ok, breadth).astype(BF16)
        moved = shifted(rim_masked(grad, rim_ok, breadth))
        grads[out, :] = moved[1]
        for shift in range(3):
            sg[at_row(row * 3 + shift, 1, ch), :] = moved[shift][:ch]
            sg[at_row(row * 3 + 3 + shift, 1, ch), :] = moved[shift][ch:]
        return 0

    lax.fori_loop(0, height // 2 - 1, middle, 0, unroll=UNROLL_MIDDLE)
    stores[1].start()
    stores[2].start()

    def last(pair, _):
        row = pair * 2
        back = jnp.dot(w1f_ref[...], sg[at_row(row * 3, 12, ch), core], preferred_element_type=F32)
        here = at_row(row + 2, 2, ch)
        value = wx[here, core].astype(F32)
        mid = grads[at_row(row + 1, 2, ch), core].astype(F32)
        gw[here, :] = (mid + slope_of(value, sigmoid(value)) * back).astype(BF16)
        return 0

    lax.fori_loop(0, height // 2 - 2, last, 0, unroll=UNROLL_LAST)
    stores[4].start()

    size = 256
    strip = BLOCK * ch

    def pack(part, _):
        start = pl.multiple_of(part * size, size)
        total = None
        for band in range(height // BLOCK):
            chosen = chosen_blocks(target_ref, band, start, size, breadth)
            rows = slice(band * strip + 2 * ch, (band + 1) * strip - 2 * ch)
            term = lax.dot_general(chosen, gw[rows, :], NT, preferred_element_type=F32)
            total = term if total is None else total + term
        packed[pl.ds(start, size), :] = total.astype(BF16)
        return 0

    lax.fori_loop(0, packed.shape[0] // size, pack, 0)
    stores[3].start()
    for store in stores:
        store.wait()


UNROLL_PREPARE = 8
UNROLL_MIDDLE = 5
UNROLL_LAST = 7


def inner(sizes, flags, operands, slots):
    channels, height, breadth = sizes
    wide = breadth + 128
    vmem = pl.BlockSpec(memory_space=pltpu.VMEM)
    hbm = pl.BlockSpec(memory_space=pl.ANY)
    outs = [
        jax.ShapeDtypeStruct((slots * BLOCK, BLOCK * channels), BF16),
        jax.ShapeDtypeStruct(((height + 2) * channels, wide), BF16),
        jax.ShapeDtypeStruct(((height + 2) * channels, wide), BF16),
        jax.ShapeDtypeStruct((height * channels, wide), BF16),
        jax.ShapeDtypeStruct((4 * channels, breadth), BF16),
    ]
    flops = 2 * 3 * 12 * channels * 2 * channels * wide * (height // 2)
    return pl.pallas_call(
        functools.partial(inner_kernel, channels, height, breadth),
        in_specs=[pl.BlockSpec(memory_space=pltpu.SMEM), hbm, hbm] + [vmem] * (len(operands) - 2),
        out_specs=[hbm] * len(outs),
        out_shape=outs,
        scratch_shapes=[
            pltpu.VMEM((height * channels, wide), BF16),
            pltpu.VMEM((height * channels, wide), BF16),
            pltpu.VMEM((height * 3 * channels, wide), BF16),
            pltpu.VMEM((height * 3 * channels, wide), BF16),
            pltpu.VMEM(((height - 2) * 3 * channels, wide), BF16),
            pltpu.VMEM((height * channels, breadth), BF16),
            pltpu.VMEM((height * channels, wide), BF16),
            pltpu.VMEM(((height - 2) * channels, wide), BF16),
            pltpu.VMEM(((height - 2) * channels, wide), BF16),
            pltpu.VMEM((slots * BLOCK, (BLOCK - 4) * channels), BF16),
            pltpu.SemaphoreType.DMA((2,)),
            pltpu.SemaphoreType.DMA((5,)),
        ],
        compiler_params=params(),
        cost_estimate=pl.CostEstimate(flops=flops, bytes_accessed=2 * 10**7, transcendentals=10**6),
        name="inner",
    )(flags, *operands)


def outer_kernel(
    channels, height, breadth,
    flags_ref, xw_ref, xc_ref, up_ref, down_ref, side_ref, side_up_ref, side_down_ref,
    w1_ref, w2f_ref, w1f_ref, bias_ref, target_ref, gw_mid_ref,
    packed_in, act_in_in, act_mid_in, g_in,
    packed_ref, act_in_ref, act_mid_ref, g_ref,
    wx, cx, sa, sc, sg, near, gw, act_in, act_mid, grads, packed, sem_in, sem_out,
):
    ch = channels
    wide = breadth + 128
    core = slice(0, breadth)
    rim = slice(breadth, wide)
    body = height * ch
    rows2 = 2 * ch
    loads = []

    def load(source, target):
        copy = pltpu.make_async_copy(source, target, sem_in.at[len(loads)])
        copy.start()
        loads.append(copy)

    load(xw_ref.at[0:rows2, :], wx.at[rows2 : 2 * rows2, core])
    load(xc_ref.at[0:rows2, :], cx.at[rows2 : 2 * rows2, core])
    load(xw_ref.at[body - rows2 : body, :], wx.at[2 * rows2 : 3 * rows2, core])
    load(xc_ref.at[body - rows2 : body, :], cx.at[2 * rows2 : 3 * rows2, core])
    load(up_ref.at[0:rows2, :], wx.at[0:rows2, core])
    load(up_ref.at[rows2 : 2 * rows2, :], cx.at[0:rows2, core])
    load(down_ref.at[0:rows2, :], wx.at[3 * rows2 : 4 * rows2, core])
    load(down_ref.at[rows2 : 2 * rows2, :], cx.at[3 * rows2 : 4 * rows2, core])
    load(g_in.at[ch : 3 * ch, :], near.at[0:rows2, :])
    load(g_in.at[body - 3 * ch : body - ch, :], near.at[rows2 : 2 * rows2, :])
    for target, first in ((wx, 0), (cx, 2)):
        target[0:rows2, rim] = spread_sides(side_up_ref[...], first)
        target[rows2 : 2 * rows2, rim] = spread_sides(side_ref[:, 0:rows2], first)
        target[2 * rows2 : 3 * rows2, rim] = spread_sides(side_ref[:, body - rows2 : body], first)
        target[3 * rows2 : 4 * rows2, rim] = spread_sides(side_down_ref[...], first)
    for copy in loads:
        copy.wait()
    lane = lax.broadcasted_iota(jnp.int32, (2 * ch, 128), 1) + breadth
    rim_ok = lane_mask(flags_ref, lane, breadth)
    sub = lax.broadcasted_iota(jnp.int32, (2 * ch, wide), 0)

    for half in range(2):
        base = half * 2 * rows2
        for row in range(4):
            here = slice(base + row * ch, base + (row + 1) * ch)
            value = wx[here, :].astype(F32)
            moved = shifted(value * sigmoid(value))
            if row == 1 + half:
                act_in[half * ch : (half + 1) * ch, :] = moved[1]
            for shift in range(3):
                sa[(row * 3 + shift) * ch : (row * 3 + shift + 1) * ch, :] = moved[shift]
            moved = shifted(cx[here, :].astype(F32))
            for shift in range(3):
                sc[(row * 3 + shift) * ch : (row * 3 + shift + 1) * ch, :] = moved[shift]
        here = slice(base + ch, base + 3 * ch)
        act, grad = middle_step(
            w1_ref, w2f_ref, bias_ref, wx[here, :], cx[here, :], sa[...], sc[...]
        )
        good = ((sub >= ch) if half == 0 else (sub < ch)) | (flags_ref[half] == 1)
        act = jnp.where(good, rim_masked(act, rim_ok, breadth), 0.0)
        grad = jnp.where(good, rim_masked(grad, rim_ok, breadth), 0.0)
        act_mid[half * rows2 : (half + 1) * rows2, :] = act.astype(BF16)
        mine = shifted(grad)
        other = shifted(near[half * rows2 : (half + 1) * rows2, :].astype(F32))
        own = mine[1][ch:] if half == 0 else mine[1][:ch]
        grads[half * ch : (half + 1) * ch, :] = own
        order = (mine, other) if half == 0 else (other, mine)
        for pair in range(2):
            for row in range(2):
                for shift in range(3):
                    out = ((pair * 2 + row) * 3 + shift) * ch
                    sg[out : out + ch, :] = order[pair][shift][row * ch : (row + 1) * ch]
        back = jnp.dot(w1f_ref[...], sg[:, core], preferred_element_type=F32)
        inside = slice(rows2, 2 * rows2) if half == 0 else slice(2 * rows2, 3 * rows2)
        value = wx[inside, core].astype(F32)
        mid = jnp.concatenate([order[0][1][ch:, core], order[1][1][:ch, core]], axis=0).astype(F32)
        gw[half * rows2 : (half + 1) * rows2, :] = (
            mid + slope_of(value, sigmoid(value)) * back
        ).astype(BF16)

    stores = [
        (act_in.at[0:ch, :], act_in_ref.at[0:ch, :]),
        (act_in.at[ch : 2 * ch, :], act_in_ref.at[body + ch : body + 2 * ch, :]),
        (act_mid.at[0:rows2, :], act_mid_ref.at[0:rows2, :]),
        (act_mid.at[rows2 : 2 * rows2, :], act_mid_ref.at[body : body + 2 * ch, :]),
        (grads.at[0:ch, :], g_ref.at[0:ch, :]),
        (grads.at[ch : 2 * ch, :], g_ref.at[body - ch : body, :]),
        (packed.at[:, 0:rows2], packed_ref.at[:, 0:rows2]),
        (packed.at[:, rows2 : 2 * rows2], packed_ref.at[:, (BLOCK - 2) * ch : BLOCK * ch]),
    ]
    stores = [
        pltpu.make_async_copy(source, target, sem_out.at[at])
        for at, (source, target) in enumerate(stores)
    ]
    for store in stores[:6]:
        store.start()
    first = jnp.concatenate([gw[0:rows2, :], gw_mid_ref[0:rows2, :]], axis=0)
    second = jnp.concatenate([gw_mid_ref[rows2 : 2 * rows2, :], gw[rows2 : 2 * rows2, :]], axis=0)
    size = 256

    def pack(part, _):
        start = pl.multiple_of(part * size, size)
        total = sum(
            lax.dot_general(
                chosen_blocks(target_ref, band, start, size, breadth),
                rows,
                NT,
                preferred_element_type=F32,
            )
            for band, rows in enumerate((first, second))
        )
        packed[pl.ds(start, size), :] = total.astype(BF16)
        return 0

    lax.fori_loop(0, packed.shape[0] // size, pack, 0)
    for store in stores[6:]:
        store.start()
    for store in stores:
        store.wait()


def outer(sizes, flags, operands, state, slots):
    channels, height, breadth = sizes
    wide = breadth + 128
    vmem = pl.BlockSpec(memory_space=pltpu.VMEM)
    hbm = pl.BlockSpec(memory_space=pl.ANY)
    inputs = 1 + len(operands)
    return pl.pallas_call(
        functools.partial(outer_kernel, channels, height, breadth),
        in_specs=[pl.BlockSpec(memory_space=pltpu.SMEM)]
        + [hbm] * 4
        + [vmem] * (len(operands) - 4)
        + [hbm] * len(state),
        out_specs=[hbm] * len(state),
        out_shape=[jax.ShapeDtypeStruct(item.shape, item.dtype) for item in state],
        input_output_aliases={inputs + at: at for at in range(len(state))},
        scratch_shapes=[
            pltpu.VMEM((8 * channels, wide), BF16),
            pltpu.VMEM((8 * channels, wide), BF16),
            pltpu.VMEM((12 * channels, wide), BF16),
            pltpu.VMEM((12 * channels, wide), BF16),
            pltpu.VMEM((12 * channels, wide), BF16),
            pltpu.VMEM((4 * channels, wide), BF16),
            pltpu.VMEM((4 * channels, breadth), BF16),
            pltpu.VMEM((2 * channels, wide), BF16),
            pltpu.VMEM((4 * channels, wide), BF16),
            pltpu.VMEM((2 * channels, wide), BF16),
            pltpu.VMEM((slots * BLOCK, 4 * channels), BF16),
            pltpu.SemaphoreType.DMA((10,)),
            pltpu.SemaphoreType.DMA((8,)),
        ],
        compiler_params=params(),
        name="outer",
    )(flags, *operands, *state)


def correlate_kernel(
    channels, height, breadth,
    act_in_ref, act_mid_ref, g_ref, xc_ref, out_ref,
    image1, image2, g, c, s1, s2, acc1, acc2, sum1, sum2, sem,
):
    ch = channels
    wide = breadth + 128
    core = slice(0, breadth)
    loads = [
        pltpu.make_async_copy(source, target, sem.at[at])
        for at, (source, target) in enumerate(
            ((g_ref.at[:, core], g), (xc_ref, c), (act_in_ref, image1), (act_mid_ref, image2))
        )
    ]
    for load in loads:
        load.start()
    for ref in (acc1, acc2, sum1, sum2):
        ref[...] = jnp.zeros_like(ref)
    empty = jnp.zeros((ch, wide - breadth), F32)

    def prepare(row, source, target, total):
        value = source[at_row(row, 1, ch), :].astype(F32)
        total[...] += value
        right, here, left = shifted(jnp.concatenate([value, empty], axis=1))
        for shift, moved in enumerate((left, here, right)):
            target[at_row(row * 3 + shift, 1, ch), :] = moved

    def add(pair, image, grads, acc):
        acc[...] += lax.dot_general(
            grads[at_row(pair * 6, 6, ch), :],
            image[at_row(pair * 2, 4, ch), :],
            NT,
            preferred_element_type=F32,
        )

    loads[0].wait()
    loads[1].wait()

    def step(row, _):
        prepare(row, g, s1, sum1)
        prepare(row, c, s2, sum2)
        return 0

    def products(pair, _):
        add(pair, image1, s1, acc1)
        add(pair, image2, s2, acc2)
        return 0

    lax.fori_loop(0, height, step, 0, unroll=4)
    loads[2].wait()
    loads[3].wait()
    lax.fori_loop(0, height // 2, products, 0, unroll=4)

    first, second = (
        acc[0 : 3 * ch, :] + pltpu.roll(acc[3 * ch : 6 * ch, :], 3 * ch, 1) for acc in (acc1, acc2)
    )
    second = pltpu.roll(second, ch, 1)
    low = lax.broadcasted_iota(jnp.int32, (3 * ch, 128), 1) < ch
    out_ref[0 : 3 * ch, :] = first[:, 0:128]
    out_ref[3 * ch : 6 * ch, :] = jnp.where(low, first[:, 128:256], second[:, 0:128])
    out_ref[6 * ch : 9 * ch, :] = second[:, 128:256]
    sums = jnp.concatenate(
        [jnp.sum(total[...], axis=1, keepdims=True) for total in (sum1, sum2)], axis=0
    )
    out_ref[9 * ch :, :] = jnp.broadcast_to(sums, (2 * ch, 2 * ch)).T[0:8, :]


def correlate(sizes, act_in, act_mid, g_mid, xc):
    channels, height, breadth = sizes
    wide = breadth + 128
    hbm = pl.BlockSpec(memory_space=pl.ANY)
    flops = 2 * 2 * 12 * channels * 2 * channels * breadth * (height // 2)
    return pl.pallas_call(
        functools.partial(correlate_kernel, channels, height, breadth),
        in_specs=[hbm] * 4,
        out_specs=pl.BlockSpec(memory_space=pltpu.VMEM),
        out_shape=jax.ShapeDtypeStruct((9 * channels + 8, 2 * channels), F32),
        scratch_shapes=[
            pltpu.VMEM(((height + 2) * channels, wide), BF16),
            pltpu.VMEM(((height + 2) * channels, wide), BF16),
            pltpu.VMEM((height * channels, breadth), BF16),
            pltpu.VMEM((height * channels, breadth), BF16),
            pltpu.VMEM((height * 3 * channels, wide), BF16),
            pltpu.VMEM((height * 3 * channels, wide), BF16),
            pltpu.VMEM((6 * channels, 4 * channels), F32),
            pltpu.VMEM((6 * channels, 4 * channels), F32),
            pltpu.VMEM((channels, breadth), F32),
            pltpu.VMEM((channels, breadth), F32),
            pltpu.SemaphoreType.DMA((4,)),
        ],
        compiler_params=params(),
        cost_estimate=pl.CostEstimate(flops=flops, bytes_accessed=10**7, transcendentals=0),
        name="correlate",
    )(act_in, act_mid, g_mid, xc)


def unpack_kernel(channels, devices, me_ref, table_ref, arrived_ref, out_ref, chosen):
    block_rows, part, breadth = out_ref.shape[1], out_ref.shape[3], out_ref.shape[4]

    @pl.when(pl.program_id(0) == 0)
    def _():
        shape = (CAP * BLOCK, block_rows * breadth)
        sub = lax.broadcasted_iota(jnp.int32, shape, 0)
        place = lax.broadcasted_iota(jnp.int32, shape, 1) - sub % BLOCK
        second = sub >= BLOCK

        def select(source, _):
            at = (source * devices + me_ref[0]) * CAP
            owners = [
                table_ref[(at + rank) // 128, (at + rank) % 128] * BLOCK for rank in range(CAP)
            ]
            wanted = jnp.where(second, owners[1], owners[0])
            chosen[pl.ds(pl.multiple_of(source * CAP * BLOCK, CAP * BLOCK), CAP * BLOCK), :] = (
                (place == wanted).astype(F32).astype(BF16)
            )
            return 0

        lax.fori_loop(0, devices, select, 0, unroll=4)

    flat = arrived_ref[...].T
    for band in range(block_rows):
        summed = jnp.dot(
            flat, chosen[:, band * breadth : (band + 1) * breadth], preferred_element_type=F32
        )
        cube = summed.reshape(part, channels, breadth)
        out_ref[:, band, 0, :, :] = jnp.swapaxes(cube, 0, 1)


def unpack(sizes, me, table, arrived, devices):
    channels, height, breadth = sizes
    block_rows = height // BLOCK
    rows = arrived.shape[0]
    part = 8
    smem = pl.BlockSpec(memory_space=pltpu.SMEM)
    return pl.pallas_call(
        functools.partial(unpack_kernel, channels, devices),
        grid=(BLOCK // part,),
        in_specs=[smem, smem, pl.BlockSpec((rows, part * channels), lambda h: (0, h))],
        out_specs=pl.BlockSpec((channels, block_rows, 1, part, breadth), lambda h: (0, 0, h, 0, 0)),
        out_shape=jax.ShapeDtypeStruct((channels, block_rows, BLOCK // part, part, breadth), F32),
        scratch_shapes=[pltpu.VMEM((rows, block_rows * breadth), BF16)],
        compiler_params=params(),
        name="unpack",
    )(me, table, arrived)


def pair_weights(kernel):
    taps = jnp.transpose(kernel, (0, 2, 3, 1)).reshape(kernel.shape[0], -1)
    third = taps.shape[1] // 3
    return jnp.concatenate(
        [jnp.pad(taps, ((0, 0), (0, third))), jnp.pad(taps, ((0, 0), (third, 0)))], axis=0
    )


def flipped(kernel):
    return jnp.transpose(kernel[:, :, ::-1, ::-1], (1, 0, 2, 3))


def shift_pairs(axis, step):
    count = lax.axis_size(axis)
    return [(i, i + step) for i in range(count) if 0 <= i + step < count]


def total_over_devices(terms, devices):
    me = lax.axis_index(AXES)
    swap = lambda value, step: lax.ppermute(value, AXES, [(i, i ^ step) for i in range(devices)])
    total = terms
    for step in (1, 2):
        bit = (me // step) % 2
        half = total.shape[0] // 2
        mine = lax.dynamic_slice_in_dim(total, bit * half, half, 0)
        away = lax.dynamic_slice_in_dim(total, (1 - bit) * half, half, 0)
        total = mine + swap(away, step)
    step = 4
    while step < devices:
        total = total + swap(total, step)
        step *= 2
    for step in (2, 1):
        bit = (me // step) % 2
        other = swap(total, step)
        total = jnp.concatenate(
            [jnp.where(bit == 0, total, other), jnp.where(bit == 0, other, total)], axis=0
        )
    return total


def body(warped, cotangent, w_first, b_first, w_second, source_tile, source_block):
    sizes = warped.shape
    channels, height, breadth = sizes
    row_count = lax.axis_size("rows")
    col_count = lax.axis_size("cols")
    devices = row_count * col_count
    slots = devices * CAP
    factor = 1.0 / math.sqrt(height * row_count * breadth * col_count)
    row_at = lax.axis_index("rows")
    col_at = lax.axis_index("cols")
    me = lax.axis_index(AXES)

    block_rows = height // BLOCK
    count = source_tile.size
    target = source_tile.reshape(count)
    same = target[:, None] == target[None, :]
    earlier = jnp.arange(count)[None, :] < jnp.arange(count)[:, None]
    ranking = jnp.sum((same & earlier).astype(jnp.int32), axis=1)
    places = target * CAP + ranking
    target_row = (
        places.reshape(block_rows, -1, 1) * BLOCK + jnp.arange(BLOCK, dtype=jnp.int32)
    ).reshape(block_rows, breadth)
    hits = places[:, None] == jnp.arange(slots, dtype=jnp.int32)[None, :]
    labels = jnp.sum(jnp.where(hits, source_block.reshape(count, 1) + 1, 0), axis=0) - 1

    xw, xc, to_right, to_left, to_up, to_down = reorder(warped, cotangent)
    rim = 2 * channels
    side = lax.ppermute(to_right, "cols", shift_pairs("cols", 1)) + lax.ppermute(
        to_left, "cols", shift_pairs("cols", -1)
    )
    up = lax.ppermute(to_down, "rows", shift_pairs("rows", 1))
    down = lax.ppermute(to_up, "rows", shift_pairs("rows", -1))
    side_up = lax.ppermute(side[:, -rim:], "rows", shift_pairs("rows", 1))
    side_down = lax.ppermute(side[:, :rim], "rows", shift_pairs("rows", -1))

    flags = jnp.stack(
        [row_at > 0, row_at < row_count - 1, col_at > 0, col_at < col_count - 1]
    ).astype(jnp.int32)
    bias = jnp.broadcast_to(jnp.tile(b_first, 2)[:, None], (2 * channels, 128))
    first = pair_weights(w_first)
    second_back = pair_weights(flipped(w_second))
    first_back = pair_weights(flipped(w_first))
    *state, gw_mid = inner(
        sizes, flags, (xw, xc, side, first, second_back, first_back, bias, target_row), slots
    )
    packed, act_in, act_mid, g_mid = outer(
        sizes,
        flags,
        (
            xw, xc, up, down, side, side_up, side_down,
            first, second_back, first_back, bias, target_row, gw_mid,
        ),
        state,
        slots,
    )
    arrived = lax.all_to_all(
        packed.reshape(devices, CAP * BLOCK, BLOCK * channels),
        AXES,
        split_axis=0,
        concat_axis=0,
        tiled=True,
    )

    terms = correlate(sizes, act_in, act_mid, g_mid, xc)
    mine = jnp.arange(devices, dtype=jnp.int32)[:, None] == me
    table = jnp.where(mine, labels.astype(F32)[None, :], 0.0).reshape(-1, 128)
    used = terms.shape[0] + table.shape[0]
    fill = jnp.zeros((-used % 32, 128), F32)
    summed = total_over_devices(jnp.concatenate([terms, table, fill], axis=0), devices)
    owners = summed[terms.shape[0] : used].astype(jnp.int32)
    frame = unpack(
        sizes, me.reshape(1), owners, arrived.reshape(slots * BLOCK, BLOCK * channels), devices
    )
    tiles = summed[: 9 * channels].reshape(3, 3 * channels, 128)
    taps = (
        jnp.concatenate([tiles[0], tiles[1], tiles[2]], axis=1)
        .reshape(3, channels, 2, 3, channels)
        .transpose(2, 1, 4, 3, 0)
        * factor
    )
    biases = summed[9 * channels].reshape(2, channels) * factor
    return (frame.reshape(sizes), taps[0], biases[0], taps[1], biases[1])


def solution(mesh):
    in_specs = (
        P(None, "rows", "cols"),
        P(None, "rows", "cols"),
        P(),
        P(),
        P(),
        P("rows", "cols"),
        P("rows", "cols"),
    )
    out_specs = (P(None, "rows", "cols"), P(), P(), P(), P())
    return jax.shard_map(body, mesh=mesh, in_specs=in_specs, out_specs=out_specs, check_vma=False)
```

```python
import functools
import math

import jax
import jax.numpy as jnp
from jax import lax
from jax.experimental import pallas as pl
from jax.experimental.pallas import tpu as pltpu
from jax.sharding import PartitionSpec as P

BLOCK = 16
CAP = 2
AXES = ("rows", "cols")
BF16 = jnp.bfloat16
F32 = jnp.float32
NT = (((1,), (1,)), ((), ()))
TN = (((0,), (0,)), ((), ()))
VMEM_BYTES = 63 * 2**20


def params(**extra):
    return pltpu.CompilerParams(vmem_limit_bytes=VMEM_BYTES, **extra)


def sigmoid(value):
    return 0.5 * jnp.tanh(0.5 * value) + 0.5


def one_hot(shape, pairs):
    row = lax.broadcasted_iota(jnp.int32, shape, 0)
    col = lax.broadcasted_iota(jnp.int32, shape, 1)
    hit = jnp.zeros(shape, jnp.bool_)
    for at_row, at_col in pairs:
        hit = hit | ((row == at_row) & (col == at_col))
    return hit.astype(F32).astype(BF16)


def shifted(value):
    wide = value.shape[1]
    return (
        pltpu.roll(value, 1, 1).astype(BF16),
        value.astype(BF16),
        pltpu.roll(value, wide - 1, 1).astype(BF16),
    )


def slope_of(value, sigma):
    return sigma * (1.0 + value * (1.0 - sigma))


def at_row(row, rows, channels):
    return pl.ds(pl.multiple_of(row * channels, channels), rows * channels)


def pair_weights(taps_ref, out_ref, flip):
    ch = taps_ref.shape[2]
    out_ref[...] = jnp.zeros_like(out_ref)
    for row in range(3):
        for col in range(3):
            if flip:
                tap = taps_ref[2 - row, 2 - col].astype(F32).T.astype(BF16)
            else:
                tap = taps_ref[row, col]
            at = (row * 3 + col) * ch
            out_ref[0:ch, at : at + ch] = tap
            out_ref[ch : 2 * ch, at + 3 * ch : at + 4 * ch] = tap


def reorder_kernel(
    w_ref, c_ref, first_ref, second_ref, b_ref,
    xw_ref, xc_ref, to_right_ref, to_left_ref, to_up_ref, to_down_ref,
    w1_ref, w2f_ref, w1f_ref, bias_ref,
):
    channels, rows, lanes = w_ref.shape

    @pl.when((pl.program_id(0) == 0) & (pl.program_id(1) == 1))
    def _():
        pair_weights(first_ref, w1_ref, False)
        pair_weights(second_ref, w2f_ref, True)
        pair_weights(first_ref, w1f_ref, True)
        column = jnp.broadcast_to(b_ref[...], (2 * channels, channels)).T
        bias_ref[0:channels, :] = column
        bias_ref[channels:, :] = column

    rim = 2 * channels
    kept = []
    for source, target in ((w_ref, xw_ref), (c_ref, xc_ref)):
        value = source[...].astype(F32)
        swapped = jnp.swapaxes(value, 0, 1).reshape(rows * channels, lanes).astype(BF16)
        target[...] = swapped
        kept.append(swapped)

    @pl.when(pl.program_id(1) == 0)
    def _():
        to_up_ref[0:rim, :] = kept[0][0:rim]
        to_up_ref[rim:, :] = kept[1][0:rim]

    @pl.when(pl.program_id(1) == pl.num_programs(1) - 1)
    def _():
        to_down_ref[0:rim, :] = kept[0][rows * channels - rim :]
        to_down_ref[rim:, :] = kept[1][rows * channels - rim :]

    here = pl.ds(pl.multiple_of(pl.program_id(1) * rows * channels, 128), rows * channels)

    def pick(tile, w_pairs, c_pairs):
        return sum(
            lax.dot_general(
                one_hot((16, 128), pairs), value[:, tile], NT, preferred_element_type=F32
            )
            for value, pairs in zip(kept, (w_pairs, c_pairs))
        ).astype(BF16)

    @pl.when(pl.program_id(0) == pl.num_programs(0) - 1)
    def _():
        final = slice(lanes - 128, lanes)
        to_right_ref[:, here] = pick(final, ((0, 126), (1, 127)), ((2, 126), (3, 127)))

    @pl.when(pl.program_id(0) == 0)
    def _():
        to_left_ref[:, here] = pick(slice(0, 128), ((4, 0), (5, 1)), ((6, 0), (7, 1)))


def reorder(warped, cotangent, w_first, w_second, b_first):
    channels, height, breadth = warped.shape
    whole = lambda shape: pl.BlockSpec(shape, lambda x, h: (0,) * len(shape))
    step = 16
    lanes = 256
    spec_in = pl.BlockSpec((channels, step, lanes), lambda x, h: (0, h, x))
    spec_out = pl.BlockSpec((step * channels, lanes), lambda x, h: (h, x))
    spec_edge = pl.BlockSpec((16, height * channels), lambda x, h: (0, 0))
    spec_rim = pl.BlockSpec((4 * channels, lanes), lambda x, h: (0, x))
    shape = jax.ShapeDtypeStruct((height * channels, breadth), BF16)
    edge = jax.ShapeDtypeStruct((16, height * channels), BF16)
    rim = jax.ShapeDtypeStruct((4 * channels, breadth), BF16)
    weights = jax.ShapeDtypeStruct((2 * channels, 12 * channels), BF16)
    bias = jax.ShapeDtypeStruct((2 * channels, 2 * channels), F32)
    return pl.pallas_call(
        reorder_kernel,
        grid=(breadth // lanes, height // step),
        in_specs=[spec_in, spec_in]
        + [whole(w_first.shape[2:] + w_first.shape[:2])] * 2
        + [whole((1, channels))],
        out_specs=[spec_out, spec_out, spec_edge, spec_edge, spec_rim, spec_rim]
        + [whole(weights.shape)] * 3
        + [whole(bias.shape)],
        out_shape=[shape, shape, edge, edge, rim, rim, weights, weights, weights, bias],
        compiler_params=params(),
        name="reorder",
    )(
        warped,
        cotangent,
        jnp.transpose(w_first, (2, 3, 0, 1)),
        jnp.transpose(w_second, (2, 3, 0, 1)),
        b_first[None, :],
    )


def spread_sides(side, first):
    spread = one_hot((16, 128), ((first, 126), (first + 1, 127), (first + 4, 0), (first + 5, 1)))
    return lax.dot_general(side, spread, TN, preferred_element_type=F32).astype(BF16)


def rim_mask(channels):
    lane = lax.broadcasted_iota(jnp.int32, (2 * channels, 128), 1)
    col = lax.axis_index("cols")
    right = jnp.where(col < lax.axis_size("cols") - 1, 0, -1)
    left = jnp.where(col > 0, 127, -1)
    return (lane == right) | (lane == left)


def middle_step(w1_ref, w2f_ref, bias_ref, value, cot, act_window, cot_window):
    conv = jnp.dot(w1_ref[...], act_window, preferred_element_type=F32)
    back = jnp.dot(w2f_ref[...], cot_window, preferred_element_type=F32)
    a_mid = (value.astype(F32) + conv + bias_ref[:, 0:1]).astype(BF16).astype(F32)
    sigma = sigmoid(a_mid)
    return a_mid * sigma, cot.astype(F32) + slope_of(a_mid, sigma) * back


def rim_masked(value, rim_ok, breadth):
    return jnp.concatenate(
        [value[:, :breadth], jnp.where(rim_ok, value[:, breadth:], 0.0)], axis=1
    )


def chosen_blocks(target_ref, band, start, size, breadth):
    row_at = lax.broadcasted_iota(jnp.int32, (size, breadth), 0) + start
    return (row_at == target_ref[band : band + 1, :]).astype(F32).astype(BF16)


def inner_kernel(
    channels, height, breadth,
    xw_ref, xc_ref, side_ref, w1_ref, w2f_ref, w1f_ref, bias_ref, target_ref, label_ref,
    packed_ref, act_in_ref, act_mid_ref, g_ref, gw_mid_ref,
    wx, cx, sa, sc, sg, gw, act_in, act_mid, grads, packed, sem_in, sem_out,
):
    ch = channels
    wide = breadth + 128
    core = slice(0, breadth)
    rim = slice(breadth, wide)
    step = height * ch // 4
    loads = [
        pltpu.make_async_copy(
            source.at[at * step : (at + 1) * step, :],
            target.at[at * step : (at + 1) * step, core],
            sem_in.at[2 * at + which],
        )
        for at in range(4)
        for which, (source, target) in enumerate(((xw_ref, wx), (xc_ref, cx)))
    ]
    stores = [
        pltpu.make_async_copy(act_in, act_in_ref.at[ch : ch + height * ch, :], sem_out.at[0]),
        pltpu.make_async_copy(act_mid, act_mid_ref.at[2 * ch : height * ch, :], sem_out.at[1]),
        pltpu.make_async_copy(grads, g_ref.at[ch : (height - 1) * ch, :], sem_out.at[2]),
        pltpu.make_async_copy(
            label_ref, packed_ref.at[:, DEPTH * CAP * BLOCK : DEPTH * CAP * BLOCK + 16, :], sem_out.at[3]
        ),
        pltpu.make_async_copy(
            gw.at[(BLOCK - 2) * ch : (BLOCK + 2) * ch, :], gw_mid_ref, sem_out.at[4]
        ),
    ]
    for load in loads:
        load.start()
    stores[3].start()
    wx[:, rim] = spread_sides(side_ref[...], 0)
    cx[:, rim] = spread_sides(side_ref[...], 2)

    def prepare(row, _):
        here = at_row(row, 1, ch)
        out = pl.multiple_of(row * 3 * ch, ch)
        value = wx[here, :].astype(F32)
        moved = shifted(value * sigmoid(value))
        act_in[here, :] = moved[1]
        for shift in range(3):
            sa[pl.ds(out + shift * ch, ch), :] = moved[shift]
        moved = shifted(cx[here, :].astype(F32))
        for shift in range(3):
            sc[pl.ds(out + shift * ch, ch), :] = moved[shift]
        return 0

    for at in range(4):
        loads[2 * at].wait()
        loads[2 * at + 1].wait()
        lax.fori_loop(at * height // 4, (at + 1) * height // 4, prepare, 0, unroll=UNROLL_PREPARE)
    stores[0].start()
    rim_ok = rim_mask(ch)

    def middle(pair, _):
        row = pair * 2
        window = at_row(row * 3, 12, ch)
        here = at_row(row + 1, 2, ch)
        act, grad = middle_step(
            w1_ref, w2f_ref, bias_ref, wx[here, :], cx[here, :], sa[window, :], sc[window, :]
        )
        out = at_row(row, 2, ch)
        act_mid[out, :] = rim_masked(act, rim_ok, breadth).astype(BF16)
        moved = shifted(rim_masked(grad, rim_ok, breadth))
        grads[out, :] = moved[1]
        for shift in range(3):
            sg[at_row(row * 3 + shift, 1, ch), :] = moved[shift][:ch]
            sg[at_row(row * 3 + 3 + shift, 1, ch), :] = moved[shift][ch:]
        return 0

    lax.fori_loop(0, height // 2 - 1, middle, 0, unroll=UNROLL_MIDDLE)
    stores[1].start()
    stores[2].start()

    def last(pair, _):
        row = pair * 2
        back = jnp.dot(w1f_ref[...], sg[at_row(row * 3, 12, ch), core], preferred_element_type=F32)
        here = at_row(row + 2, 2, ch)
        value = wx[here, core].astype(F32)
        mid = grads[at_row(row + 1, 2, ch), core].astype(F32)
        gw[here, :] = (mid + slope_of(value, sigmoid(value)) * back).astype(BF16)
        return 0

    lax.fori_loop(0, height // 2 - 2, last, 0, unroll=UNROLL_LAST)
    stores[4].start()

    size = 256
    strip = BLOCK * ch

    def pack(part, _):
        start = pl.multiple_of(part * size, size)
        total = None
        for band in range(height // BLOCK):
            chosen = chosen_blocks(target_ref, band, start, size, breadth)
            rows = slice(band * strip + 2 * ch, (band + 1) * strip - 2 * ch)
            term = lax.dot_general(chosen, gw[rows, :], NT, preferred_element_type=F32)
            total = term if total is None else total + term
        total = total.astype(BF16).reshape(size // rows_to, rows_to, total.shape[1])
        packed[pl.ds(part * (size // rows_to), size // rows_to), :, :] = total
        return 0

    rows_to = CAP * BLOCK
    lax.fori_loop(0, packed.shape[0] * rows_to // size, pack, 0)
    for at in range(1, DEPTH - 1):
        stores.append(
            pltpu.make_async_copy(
                packed.at[:, :, (at - 1) * 128 : at * 128],
                packed_ref.at[:, at * rows_to : (at + 1) * rows_to, :],
                sem_out.at[4 + at],
            )
        )
        stores[-1].start()
    for store in stores:
        store.wait()


DEPTH = 8
UNROLL_PREPARE = 8
UNROLL_MIDDLE = 5
UNROLL_LAST = 7


def inner(sizes, operands, slots):
    channels, height, breadth = sizes
    wide = breadth + 128
    vmem = pl.BlockSpec(memory_space=pltpu.VMEM)
    hbm = pl.BlockSpec(memory_space=pl.ANY)
    outs = [
        jax.ShapeDtypeStruct((slots // CAP, DEPTH * CAP * BLOCK + 16, 128), BF16),
        jax.ShapeDtypeStruct(((height + 2) * channels, wide), BF16),
        jax.ShapeDtypeStruct(((height + 2) * channels, wide), BF16),
        jax.ShapeDtypeStruct((height * channels, wide), BF16),
        jax.ShapeDtypeStruct((4 * channels, breadth), BF16),
    ]
    flops = 2 * 3 * 12 * channels * 2 * channels * wide * (height // 2)
    return pl.pallas_call(
        functools.partial(inner_kernel, channels, height, breadth),
        in_specs=[hbm, hbm] + [vmem] * (len(operands) - 3) + [hbm],
        out_specs=[hbm] * len(outs),
        out_shape=outs,
        scratch_shapes=[
            pltpu.VMEM((height * channels, wide), BF16),
            pltpu.VMEM((height * channels, wide), BF16),
            pltpu.VMEM((height * 3 * channels, wide), BF16),
            pltpu.VMEM((height * 3 * channels, wide), BF16),
            pltpu.VMEM(((height - 2) * 3 * channels, wide), BF16),
            pltpu.VMEM((height * channels, breadth), BF16),
            pltpu.VMEM((height * channels, wide), BF16),
            pltpu.VMEM(((height - 2) * channels, wide), BF16),
            pltpu.VMEM(((height - 2) * channels, wide), BF16),
            pltpu.VMEM((slots // CAP, CAP * BLOCK, (BLOCK - 4) * channels), BF16),
            pltpu.SemaphoreType.DMA((8,)),
            pltpu.SemaphoreType.DMA((3 + DEPTH,)),
        ],
        compiler_params=params(),
        cost_estimate=pl.CostEstimate(flops=flops, bytes_accessed=2 * 10**7, transcendentals=10**6),
        name="inner",
    )(*operands)


def outer_kernel(
    channels, height, breadth,
    xw_ref, xc_ref, up_ref, down_ref, side_ref,
    w1_ref, w2f_ref, w1f_ref, bias_ref, target_ref, gw_mid_ref,
    packed_in, act_in_in, act_mid_in, g_in,
    packed_ref, act_in_ref, act_mid_ref, g_ref,
    wx, cx, sa_both, sc_both, sg_both, near, gw, act_in, act_mid, grads, packed, chosen, corner,
    sem_in, sem_out,
):
    ch = channels
    wide = breadth + 128
    core = slice(0, breadth)
    rim = slice(breadth, wide)
    body = height * ch
    rows2 = 2 * ch
    loads = []

    def load(source, target):
        copy = pltpu.make_async_copy(source, target, sem_in.at[len(loads)])
        copy.start()
        loads.append(copy)

    load(up_ref.at[2 * rows2 : 2 * rows2 + 16, 0:rows2], corner.at[0])
    load(down_ref.at[2 * rows2 : 2 * rows2 + 16, 0:rows2], corner.at[1])
    load(xw_ref.at[0:rows2, :], wx.at[rows2 : 2 * rows2, core])
    load(xc_ref.at[0:rows2, :], cx.at[rows2 : 2 * rows2, core])
    load(xw_ref.at[body - rows2 : body, :], wx.at[2 * rows2 : 3 * rows2, core])
    load(xc_ref.at[body - rows2 : body, :], cx.at[2 * rows2 : 3 * rows2, core])
    load(up_ref.at[0:rows2, :], wx.at[0:rows2, core])
    load(up_ref.at[rows2 : 2 * rows2, :], cx.at[0:rows2, core])
    load(down_ref.at[0:rows2, :], wx.at[3 * rows2 : 4 * rows2, core])
    load(down_ref.at[rows2 : 2 * rows2, :], cx.at[3 * rows2 : 4 * rows2, core])
    load(g_in.at[ch : 3 * ch, :], near.at[0:rows2, :])
    load(g_in.at[body - 3 * ch : body - ch, :], near.at[rows2 : 2 * rows2, :])
    for target, first in ((wx, 0), (cx, 2)):
        target[rows2 : 2 * rows2, rim] = spread_sides(side_ref[:, 0:rows2], first)
        target[2 * rows2 : 3 * rows2, rim] = spread_sides(side_ref[:, body - rows2 : body], first)
    size = 256

    def choose(part, _):
        start = pl.multiple_of(part * size, size)
        for band in range(2):
            chosen[pl.ds(start, size), band * breadth : (band + 1) * breadth] = chosen_blocks(
                target_ref, band, start, size, breadth
            )
        return 0

    lax.fori_loop(0, chosen.shape[0] // size, choose, 0)
    for copy in loads:
        copy.wait()
    for target, first in ((wx, 0), (cx, 2)):
        target[0:rows2, rim] = spread_sides(corner[0], first)
        target[3 * rows2 : 4 * rows2, rim] = spread_sides(corner[1], first)
    rim_ok = rim_mask(ch)
    sub = lax.broadcasted_iota(jnp.int32, (2 * ch, wide), 0)

    for half in range(2):
        base = half * 2 * rows2
        sa, sc, sg = sa_both.at[half], sc_both.at[half], sg_both.at[half]
        for row in range(4):
            here = slice(base + row * ch, base + (row + 1) * ch)
            value = wx[here, :].astype(F32)
            moved = shifted(value * sigmoid(value))
            if row == 1 + half:
                act_in[half * ch : (half + 1) * ch, :] = moved[1]
            for shift in range(3):
                sa[(row * 3 + shift) * ch : (row * 3 + shift + 1) * ch, :] = moved[shift]
            moved = shifted(cx[here, :].astype(F32))
            for shift in range(3):
                sc[(row * 3 + shift) * ch : (row * 3 + shift + 1) * ch, :] = moved[shift]
        here = slice(base + ch, base + 3 * ch)
        act, grad = middle_step(
            w1_ref, w2f_ref, bias_ref, wx[here, :], cx[here, :], sa[...], sc[...]
        )
        inside_at = 0 if half == 0 else lax.axis_size("rows") - 1
        limit = jnp.where(lax.axis_index("rows") == inside_at, ch, 0 if half == 0 else 2 * ch)
        good = (sub >= limit) if half == 0 else (sub < limit)
        act = jnp.where(good, rim_masked(act, rim_ok, breadth), 0.0)
        grad = jnp.where(good, rim_masked(grad, rim_ok, breadth), 0.0)
        act_mid[half * rows2 : (half + 1) * rows2, :] = act.astype(BF16)
        mine = shifted(grad)
        other = shifted(near[half * rows2 : (half + 1) * rows2, :].astype(F32))
        own = mine[1][ch:] if half == 0 else mine[1][:ch]
        grads[half * ch : (half + 1) * ch, :] = own
        order = (mine, other) if half == 0 else (other, mine)
        for pair in range(2):
            for row in range(2):
                for shift in range(3):
                    out = ((pair * 2 + row) * 3 + shift) * ch
                    sg[out : out + ch, :] = order[pair][shift][row * ch : (row + 1) * ch]
        back = jnp.dot(w1f_ref[...], sg[:, core], preferred_element_type=F32)
        inside = slice(rows2, 2 * rows2) if half == 0 else slice(2 * rows2, 3 * rows2)
        value = wx[inside, core].astype(F32)
        mid = jnp.concatenate([order[0][1][ch:, core], order[1][1][:ch, core]], axis=0).astype(F32)
        gw[half * rows2 : (half + 1) * rows2, :] = (
            mid + slope_of(value, sigmoid(value)) * back
        ).astype(BF16)

    rows_to = CAP * BLOCK
    stores = [
        (act_in.at[0:ch, :], act_in_ref.at[0:ch, :]),
        (act_in.at[ch : 2 * ch, :], act_in_ref.at[body + ch : body + 2 * ch, :]),
        (act_mid.at[0:rows2, :], act_mid_ref.at[0:rows2, :]),
        (act_mid.at[rows2 : 2 * rows2, :], act_mid_ref.at[body : body + 2 * ch, :]),
        (grads.at[0:ch, :], g_ref.at[0:ch, :]),
        (grads.at[ch : 2 * ch, :], g_ref.at[body - ch : body, :]),
        (packed.at[:, :, 0:rows2], packed_ref.at[:, 0:rows_to, :]),
        (
            packed.at[:, :, rows2 : 2 * rows2],
            packed_ref.at[:, (DEPTH - 1) * rows_to : DEPTH * rows_to, :],
        ),
    ]
    stores = [
        pltpu.make_async_copy(source, target, sem_out.at[at])
        for at, (source, target) in enumerate(stores)
    ]
    for store in stores[:6]:
        store.start()
    both = (
        jnp.concatenate([gw[0:rows2, :], gw_mid_ref[0:rows2, :]], axis=0),
        jnp.concatenate([gw_mid_ref[rows2 : 2 * rows2, :], gw[rows2 : 2 * rows2, :]], axis=0),
    )

    def pack(part, _):
        rows = pl.ds(pl.multiple_of(part * size, size), size)
        total = sum(
            lax.dot_general(
                chosen[rows, band * breadth : (band + 1) * breadth],
                both[band],
                NT,
                preferred_element_type=F32,
            )
            for band in range(2)
        ).astype(BF16)
        packed[pl.ds(part * (size // rows_to), size // rows_to), :, :] = total.reshape(
            size // rows_to, rows_to, total.shape[1]
        )
        return 0

    lax.fori_loop(0, chosen.shape[0] // size, pack, 0)
    for store in stores[6:]:
        store.start()
    for store in stores:
        store.wait()


def outer(sizes, operands, state, slots):
    channels, height, breadth = sizes
    wide = breadth + 128
    vmem = pl.BlockSpec(memory_space=pltpu.VMEM)
    hbm = pl.BlockSpec(memory_space=pl.ANY)
    inputs = len(operands)
    return pl.pallas_call(
        functools.partial(outer_kernel, channels, height, breadth),
        in_specs=[hbm] * 4
        + [vmem] * (len(operands) - 4)
        + [hbm] * len(state),
        out_specs=[hbm] * len(state),
        out_shape=[jax.ShapeDtypeStruct(item.shape, item.dtype) for item in state],
        input_output_aliases={inputs + at: at for at in range(len(state))},
        scratch_shapes=[
            pltpu.VMEM((8 * channels, wide), BF16),
            pltpu.VMEM((8 * channels, wide), BF16),
            pltpu.VMEM((2, 12 * channels, wide), BF16),
            pltpu.VMEM((2, 12 * channels, wide), BF16),
            pltpu.VMEM((2, 12 * channels, wide), BF16),
            pltpu.VMEM((4 * channels, wide), BF16),
            pltpu.VMEM((4 * channels, breadth), BF16),
            pltpu.VMEM((2 * channels, wide), BF16),
            pltpu.VMEM((4 * channels, wide), BF16),
            pltpu.VMEM((2 * channels, wide), BF16),
            pltpu.VMEM((slots // CAP, CAP * BLOCK, 4 * channels), BF16),
            pltpu.VMEM((slots * BLOCK, 2 * breadth), BF16),
            pltpu.VMEM((2, 16, 2 * channels), BF16),
            pltpu.SemaphoreType.DMA((12,)),
            pltpu.SemaphoreType.DMA((8,)),
        ],
        compiler_params=params(),
        name="outer",
    )(*operands, *state)


def correlate_kernel(
    channels, height, breadth,
    act_in_ref, act_mid_ref, g_ref, xc_ref, out_ref,
    image1, image2, g, c, s1, s2, acc1, acc2, sum1, sum2, sem,
):
    ch = channels
    wide = breadth + 128
    core = slice(0, breadth)
    loads = [
        pltpu.make_async_copy(source, target, sem.at[at])
        for at, (source, target) in enumerate(
            ((g_ref.at[:, core], g), (xc_ref, c), (act_in_ref, image1), (act_mid_ref, image2))
        )
    ]
    for load in loads:
        load.start()
    for ref in (acc1, acc2, sum1, sum2):
        ref[...] = jnp.zeros_like(ref)
    empty = jnp.zeros((ch, wide - breadth), F32)

    def prepare(row, source, target, total):
        value = source[at_row(row, 1, ch), :].astype(F32)
        total[...] += value
        right, here, left = shifted(jnp.concatenate([value, empty], axis=1))
        for shift, moved in enumerate((left, here, right)):
            target[at_row(row * 3 + shift, 1, ch), :] = moved

    def add(pair, image, grads, acc):
        acc[...] += lax.dot_general(
            grads[at_row(pair * 6, 6, ch), :],
            image[at_row(pair * 2, 4, ch), :],
            NT,
            preferred_element_type=F32,
        )

    loads[0].wait()
    loads[1].wait()

    def step(row, _):
        prepare(row, g, s1, sum1)
        prepare(row, c, s2, sum2)
        return 0

    def products(pair, _):
        add(pair, image1, s1, acc1)
        add(pair, image2, s2, acc2)
        return 0

    lax.fori_loop(0, height, step, 0, unroll=4)
    loads[2].wait()
    loads[3].wait()
    lax.fori_loop(0, height // 2, products, 0, unroll=4)

    first, second = (
        acc[0 : 3 * ch, :] + pltpu.roll(acc[3 * ch : 6 * ch, :], 3 * ch, 1) for acc in (acc1, acc2)
    )
    second = pltpu.roll(second, ch, 1)
    low = lax.broadcasted_iota(jnp.int32, (3 * ch, 128), 1) < ch
    out_ref[0 : 3 * ch, :] = first[:, 0:128]
    out_ref[3 * ch : 6 * ch, :] = jnp.where(low, first[:, 128:256], second[:, 0:128])
    out_ref[6 * ch : 9 * ch, :] = second[:, 128:256]
    sums = jnp.concatenate(
        [jnp.sum(total[...], axis=1, keepdims=True) for total in (sum1, sum2)], axis=0
    )
    out_ref[9 * ch :, :] = jnp.broadcast_to(sums, (2 * ch, 2 * ch)).T[0:8, :]


def correlate(sizes, act_in, act_mid, g_mid, xc):
    channels, height, breadth = sizes
    wide = breadth + 128
    hbm = pl.BlockSpec(memory_space=pl.ANY)
    flops = 2 * 2 * 12 * channels * 2 * channels * breadth * (height // 2)
    return pl.pallas_call(
        functools.partial(correlate_kernel, channels, height, breadth),
        in_specs=[hbm] * 4,
        out_specs=pl.BlockSpec(memory_space=pltpu.VMEM),
        out_shape=jax.ShapeDtypeStruct((9 * channels + 8, 2 * channels), F32),
        scratch_shapes=[
            pltpu.VMEM(((height + 2) * channels, wide), BF16),
            pltpu.VMEM(((height + 2) * channels, wide), BF16),
            pltpu.VMEM((height * channels, breadth), BF16),
            pltpu.VMEM((height * channels, breadth), BF16),
            pltpu.VMEM((height * 3 * channels, wide), BF16),
            pltpu.VMEM((height * 3 * channels, wide), BF16),
            pltpu.VMEM((6 * channels, 4 * channels), F32),
            pltpu.VMEM((6 * channels, 4 * channels), F32),
            pltpu.VMEM((channels, breadth), F32),
            pltpu.VMEM((channels, breadth), F32),
            pltpu.SemaphoreType.DMA((4,)),
        ],
        compiler_params=params(),
        cost_estimate=pl.CostEstimate(flops=flops, bytes_accessed=10**7, transcendentals=0),
        name="correlate",
    )(act_in, act_mid, g_mid, xc)


def unpack_kernel(channels, arrived_ref, label_ref, out_ref, chosen, flat):
    devices = arrived_ref.shape[0]
    block_rows, part, breadth = out_ref.shape[1], out_ref.shape[3], out_ref.shape[4]
    rows_to = CAP * BLOCK

    @pl.when(pl.program_id(0) == 0)
    def _():
        shape = (BLOCK, block_rows * breadth)
        place = lax.broadcasted_iota(jnp.int32, shape, 1) - lax.broadcasted_iota(jnp.int32, shape, 0)
        place = place.astype(F32)

        def select(source, _):
            label = label_ref[source].astype(F32) * BLOCK
            for rank in range(CAP):
                at = rank * (128 // CAP)
                hit = (place == label[:, at : at + 1]).astype(F32).astype(BF16)
                row = pl.multiple_of(source * rows_to + rank * BLOCK, BLOCK)
                chosen[pl.ds(row, BLOCK), :] = hit
            return 0

        lax.fori_loop(0, devices, select, 0, unroll=4)

    for at in range(arrived_ref.shape[1] // rows_to):
        tile = arrived_ref[:, at * rows_to : (at + 1) * rows_to, :]
        flat[at * 128 : (at + 1) * 128, :] = tile.reshape(devices * rows_to, 128).T
    for band in range(block_rows):
        summed = jnp.dot(
            flat[...], chosen[:, band * breadth : (band + 1) * breadth], preferred_element_type=F32
        )
        cube = summed.reshape(part, channels, breadth)
        out_ref[:, band, 0, :, :] = jnp.swapaxes(cube, 0, 1)


def unpack(sizes, arrived):
    channels, height, breadth = sizes
    block_rows = height // BLOCK
    devices = arrived.shape[0]
    rows_to = CAP * BLOCK
    part = 8
    tiles = DEPTH * part // BLOCK
    return pl.pallas_call(
        functools.partial(unpack_kernel, channels),
        grid=(BLOCK // part,),
        in_specs=[
            pl.BlockSpec((devices, tiles * rows_to, 128), lambda h: (0, h, 0)),
            pl.BlockSpec((devices, 16, 128), lambda h: (0, DEPTH * rows_to // 16, 0)),
        ],
        out_specs=pl.BlockSpec((channels, block_rows, 1, part, breadth), lambda h: (0, 0, h, 0, 0)),
        out_shape=jax.ShapeDtypeStruct((channels, block_rows, BLOCK // part, part, breadth), F32),
        scratch_shapes=[
            pltpu.VMEM((devices * rows_to, block_rows * breadth), BF16),
            pltpu.VMEM((part * channels, devices * rows_to), BF16),
        ],
        compiler_params=params(),
        name="unpack",
    )(arrived, arrived)


def shift_pairs(axis, step):
    count = lax.axis_size(axis)
    return [(i, i + step) for i in range(count) if 0 <= i + step < count]


def finish_kernel(channels, factor, total_ref, other_ref, w1_ref, w2_ref, b1_ref, b2_ref, terms):
    ch = channels
    half = total_ref.shape[0]
    bit = lax.rem(lax.axis_index("rows") * lax.axis_size("cols") + lax.axis_index("cols"), 2)
    terms[pl.ds(pl.multiple_of(bit * half, 8), half), :] = total_ref[...] * factor
    terms[pl.ds(pl.multiple_of((1 - bit) * half, 8), half), :] = other_ref[...] * factor
    tile = lambda at: terms[at * 3 * ch : (at + 1) * 3 * ch, :]
    for out, parts in ((w1_ref, ((0, 0), (0, 1), (1, 0))), (w2_ref, ((1, 1), (2, 0), (2, 1)))):
        for row, (at, side) in enumerate(parts):
            value = pltpu.roll(tile(at), ch, 1) if side else tile(at)
            for col in range(3):
                out[row, col] = value[col * ch : (col + 1) * ch, 0:ch]
    bias = terms[9 * ch : 9 * ch + 8, :]
    b1_ref[...] = bias[0:1, 0:ch]
    b2_ref[...] = pltpu.roll(bias, ch, 1)[0:1, 0:ch]


def finish(channels, factor, total, other):
    vmem = pl.BlockSpec(memory_space=pltpu.VMEM)
    kernel = jax.ShapeDtypeStruct((3, 3, channels, channels), F32)
    bias = jax.ShapeDtypeStruct((1, channels), F32)
    w1, w2, b1, b2 = pl.pallas_call(
        functools.partial(finish_kernel, channels, factor),
        in_specs=[vmem, vmem],
        out_specs=[vmem] * 4,
        out_shape=[kernel, kernel, bias, bias],
        scratch_shapes=[pltpu.VMEM((2 * total.shape[0], 128), F32)],
        compiler_params=params(),
        name="finish",
    )(total, other)
    order = (2, 3, 0, 1)
    return jnp.transpose(w1, order), b1[0], jnp.transpose(w2, order), b2[0]


def total_over_devices(terms, devices, frame_of):
    me = lax.axis_index(AXES)
    swap = lambda value, step: lax.ppermute(value, AXES, [(i, i ^ step) for i in range(devices)])
    bit = me % 2
    half = terms.shape[0] // 2
    mine = lax.dynamic_slice_in_dim(terms, bit * half, half, 0)
    away = lax.dynamic_slice_in_dim(terms, (1 - bit) * half, half, 0)
    total = mine + swap(away, 1)
    step = 2
    while 2 * step < devices:
        total = total + swap(total, step)
        step *= 2
    other = swap(total, step)
    frame = frame_of()
    other, frame = lax.optimization_barrier((other, frame))
    total = total + other
    return total, swap(total, 1), frame


def body(warped, cotangent, w_first, b_first, w_second, source_tile, source_block):
    sizes = warped.shape
    channels, height, breadth = sizes
    row_count = lax.axis_size("rows")
    col_count = lax.axis_size("cols")
    devices = row_count * col_count
    slots = devices * CAP
    factor = 1.0 / math.sqrt(height * row_count * breadth * col_count)
    me = lax.axis_index(AXES)

    block_rows = height // BLOCK
    count = source_tile.size
    target = source_tile.reshape(count)
    same = target[:, None] == target[None, :]
    earlier = jnp.arange(count)[None, :] < jnp.arange(count)[:, None]
    ranking = jnp.sum((same & earlier).astype(jnp.int32), axis=1)
    places = target * CAP + ranking
    target_row = (
        places.reshape(block_rows, -1, 1) * BLOCK + jnp.arange(BLOCK, dtype=jnp.int32)
    ).reshape(block_rows, breadth)
    hits = places[:, None] == jnp.arange(slots, dtype=jnp.int32)[None, :]
    labels = jnp.sum(jnp.where(hits, source_block.reshape(count, 1) + 1, 0), axis=0) - 1
    labels = jnp.broadcast_to(
        jnp.repeat(labels.reshape(devices, 1, CAP), 128 // CAP, axis=2), (devices, 16, 128)
    ).astype(BF16)

    xw, xc, to_right, to_left, to_up, to_down, first, second_back, first_back, bias = reorder(
        warped, cotangent, w_first, w_second, b_first
    )
    rim = 2 * channels
    side = lax.ppermute(to_right, "cols", shift_pairs("cols", 1)) + lax.ppermute(
        to_left, "cols", shift_pairs("cols", -1)
    )
    fill = ((0, 0), (0, breadth - rim))
    to_down = jnp.concatenate([to_down, jnp.pad(side[:, -rim:], fill)], axis=0)
    to_up = jnp.concatenate([to_up, jnp.pad(side[:, :rim], fill)], axis=0)
    up = lax.ppermute(to_down, "rows", shift_pairs("rows", 1))
    down = lax.ppermute(to_up, "rows", shift_pairs("rows", -1))

    *state, gw_mid = inner(
        sizes, (xw, xc, side, first, second_back, first_back, bias, target_row, labels), slots
    )
    packed, act_in, act_mid, g_mid = outer(
        sizes,
        (
            xw, xc, up, down, side,
            first, second_back, first_back, bias, target_row, gw_mid,
        ),
        state,
        slots,
    )
    arrived = lax.all_to_all(packed, AXES, split_axis=0, concat_axis=0, tiled=True)

    terms = correlate(sizes, act_in, act_mid, g_mid, xc)
    fill = jnp.zeros((-terms.shape[0] % 16, 128), F32)
    total, other, frame = total_over_devices(
        jnp.concatenate([terms, fill], axis=0),
        devices,
        lambda: unpack(sizes, arrived),
    )
    return (frame.reshape(sizes), *finish(channels, factor, total, other))


def solution(mesh):
    in_specs = (
        P(None, "rows", "cols"),
        P(None, "rows", "cols"),
        P(),
        P(),
        P(),
        P("rows", "cols"),
        P("rows", "cols"),
    )
    out_specs = (P(None, "rows", "cols"), P(), P(), P(), P())
    return jax.shard_map(body, mesh=mesh, in_specs=in_specs, out_specs=out_specs, check_vma=False)
```

```python
import functools
import math

import jax
import jax.numpy as jnp
from jax import lax
from jax.experimental import pallas as pl
from jax.experimental.pallas import tpu as pltpu
from jax.sharding import PartitionSpec as P

BLOCK = 16
CAP = 2
AXES = ("rows", "cols")
BF16 = jnp.bfloat16
F32 = jnp.float32
NT = (((1,), (1,)), ((), ()))
TN = (((0,), (0,)), ((), ()))
VMEM_BYTES = 63 * 2**20


def params(**extra):
    return pltpu.CompilerParams(vmem_limit_bytes=VMEM_BYTES, **extra)


def sigmoid(value):
    return 0.5 * jnp.tanh(0.5 * value) + 0.5


def one_hot(shape, pairs):
    row = lax.broadcasted_iota(jnp.int32, shape, 0)
    col = lax.broadcasted_iota(jnp.int32, shape, 1)
    hit = jnp.zeros(shape, jnp.bool_)
    for at_row, at_col in pairs:
        hit = hit | ((row == at_row) & (col == at_col))
    return hit.astype(F32).astype(BF16)


def shifted(value):
    value = value.astype(BF16)
    return pltpu.roll(value, 1, 1), value, pltpu.roll(value, value.shape[1] - 1, 1)


def slope_of(value, sigma):
    return sigma + value * sigma * (1.0 - sigma)


def at_row(row, rows, channels):
    return pl.ds(pl.multiple_of(row * channels, channels), rows * channels)


def pair_weights(taps_ref, out_ref, flip):
    ch = taps_ref.shape[2]
    out_ref[...] = jnp.zeros_like(out_ref)
    for row in range(3):
        for col in range(3):
            if flip:
                tap = taps_ref[2 - row, 2 - col].astype(F32).T.astype(BF16)
            else:
                tap = taps_ref[row, col]
            at = (row * 3 + col) * ch
            out_ref[0:ch, at : at + ch] = tap
            out_ref[ch : 2 * ch, at + 3 * ch : at + 4 * ch] = tap


def reorder_kernel(
    w_ref, c_ref, first_ref, second_ref, b_ref,
    xw_ref, xc_ref, to_right_ref, to_left_ref, to_up_ref, to_down_ref,
    w1_ref, w2f_ref, w1f_ref, bias_ref,
):
    channels, rows, lanes = w_ref.shape

    @pl.when((pl.program_id(0) == 0) & (pl.program_id(1) == 1))
    def _():
        pair_weights(first_ref, w1_ref, False)
        pair_weights(second_ref, w2f_ref, True)
        pair_weights(first_ref, w1f_ref, True)
        column = jnp.broadcast_to(b_ref[...], (2 * channels, channels)).T
        bias_ref[0:channels, :] = column
        bias_ref[channels:, :] = column

    rim = 2 * channels
    kept = []
    for source, target in ((w_ref, xw_ref), (c_ref, xc_ref)):
        value = source[...].astype(F32)
        swapped = jnp.swapaxes(value, 0, 1).reshape(rows * channels, lanes).astype(BF16)
        target[...] = swapped
        kept.append(swapped)

    @pl.when(pl.program_id(1) == 0)
    def _():
        to_up_ref[0:rim, :] = kept[0][0:rim]
        to_up_ref[rim : 2 * rim, :] = kept[1][0:rim]
        to_up_ref[2 * rim :, :] = jnp.zeros((16, lanes), BF16)

    @pl.when(pl.program_id(1) == pl.num_programs(1) - 1)
    def _():
        to_down_ref[0:rim, :] = kept[0][rows * channels - rim :]
        to_down_ref[rim : 2 * rim, :] = kept[1][rows * channels - rim :]
        to_down_ref[2 * rim :, :] = jnp.zeros((16, lanes), BF16)

    here = pl.ds(pl.multiple_of(pl.program_id(1) * rows * channels, 128), rows * channels)

    def pick(tile, w_pairs, c_pairs):
        return sum(
            lax.dot_general(
                one_hot((16, 128), pairs), value[:, tile], NT, preferred_element_type=F32
            )
            for value, pairs in zip(kept, (w_pairs, c_pairs))
        ).astype(BF16)

    @pl.when(pl.program_id(0) == pl.num_programs(0) - 1)
    def _():
        final = slice(lanes - 128, lanes)
        to_right_ref[:, here] = pick(final, ((0, 126), (1, 127)), ((2, 126), (3, 127)))

    @pl.when(pl.program_id(0) == 0)
    def _():
        to_left_ref[:, here] = pick(slice(0, 128), ((4, 0), (5, 1)), ((6, 0), (7, 1)))


def reorder(warped, cotangent, w_first, w_second, b_first):
    channels, height, breadth = warped.shape
    whole = lambda shape: pl.BlockSpec(shape, lambda x, h: (0,) * len(shape))
    step = 16
    lanes = breadth
    spec_in = pl.BlockSpec((channels, step, lanes), lambda x, h: (0, h, x))
    spec_out = pl.BlockSpec((step * channels, lanes), lambda x, h: (h, x))
    spec_edge = pl.BlockSpec((16, height * channels), lambda x, h: (0, 0))
    spec_rim = pl.BlockSpec((4 * channels + 16, lanes), lambda x, h: (0, x))
    shape = jax.ShapeDtypeStruct((height * channels, breadth), BF16)
    edge = jax.ShapeDtypeStruct((16, height * channels), BF16)
    rim = jax.ShapeDtypeStruct((4 * channels + 16, breadth), BF16)
    weights = jax.ShapeDtypeStruct((2 * channels, 12 * channels), BF16)
    bias = jax.ShapeDtypeStruct((2 * channels, 2 * channels), F32)
    return pl.pallas_call(
        reorder_kernel,
        grid=(breadth // lanes, height // step),
        in_specs=[spec_in, spec_in]
        + [whole(w_first.shape[2:] + w_first.shape[:2])] * 2
        + [whole((1, channels))],
        out_specs=[spec_out, spec_out, spec_edge, spec_edge, spec_rim, spec_rim]
        + [whole(weights.shape)] * 3
        + [whole(bias.shape)],
        out_shape=[shape, shape, edge, edge, rim, rim, weights, weights, weights, bias],
        compiler_params=params(),
        name="reorder",
    )(
        warped,
        cotangent,
        jnp.transpose(w_first, (2, 3, 0, 1)),
        jnp.transpose(w_second, (2, 3, 0, 1)),
        b_first[None, :],
    )


def spread_sides(side, first):
    spread = one_hot((16, 128), ((first, 126), (first + 1, 127), (first + 4, 0), (first + 5, 1)))
    return lax.dot_general(side, spread, TN, preferred_element_type=F32).astype(BF16)


def rim_mask(channels):
    lane = lax.broadcasted_iota(jnp.int32, (2 * channels, 128), 1)
    col = lax.axis_index("cols")
    right = jnp.where(col < lax.axis_size("cols") - 1, 0, -1)
    left = jnp.where(col > 0, 127, -1)
    return (lane == right) | (lane == left)


def middle_step(w1_ref, w2f_ref, bias_ref, value, cot, act_window, cot_window):
    conv = jnp.dot(w1_ref[...], act_window, preferred_element_type=F32)
    back = jnp.dot(w2f_ref[...], cot_window, preferred_element_type=F32)
    a_mid = (value.astype(F32) + conv + bias_ref[:, 0:1]).astype(BF16).astype(F32)
    sigma = sigmoid(a_mid)
    return a_mid * sigma, cot.astype(F32) + slope_of(a_mid, sigma) * back


def rim_masked(value, rim_ok, breadth):
    return jnp.concatenate(
        [value[:, :breadth], jnp.where(rim_ok, value[:, breadth:], 0.0)], axis=1
    )


def chosen_blocks(target_ref, band, start, size, breadth):
    row_at = lax.broadcasted_iota(jnp.int32, (size, breadth), 0) + start
    return (row_at == target_ref[band : band + 1, :]).astype(F32).astype(BF16)


def inner_kernel(
    channels, height, breadth,
    xw_ref, xc_ref, side_ref, w1_ref, w2f_ref, w1f_ref, bias_ref, target_ref, label_ref,
    packed_ref, act_in_ref, act_mid_ref, g_ref, gw_mid_ref,
    wx, cx, sa, sc, sg, gw, act_in, act_mid, grads, packed, label_rows, sem_in, sem_out,
):
    ch = channels
    wide = breadth + 128
    core = slice(0, breadth)
    rim = slice(breadth, wide)
    step = height * ch // 4
    loads = [
        pltpu.make_async_copy(
            source.at[at * step : (at + 1) * step, :],
            target.at[at * step : (at + 1) * step, core],
            sem_in.at[2 * at + which],
        )
        for at in range(4)
        for which, (source, target) in enumerate(((xw_ref, wx), (xc_ref, cx)))
    ]
    stores = [
        pltpu.make_async_copy(act_in, act_in_ref.at[ch : ch + height * ch, :], sem_out.at[0]),
        pltpu.make_async_copy(act_mid, act_mid_ref.at[2 * ch : height * ch, :], sem_out.at[1]),
        pltpu.make_async_copy(grads, g_ref.at[ch : (height - 1) * ch, :], sem_out.at[2]),
        pltpu.make_async_copy(
            label_rows, packed_ref.at[:, DEPTH * CAP * BLOCK : DEPTH * CAP * BLOCK + 16, :], sem_out.at[3]
        ),
        pltpu.make_async_copy(
            gw.at[(BLOCK - 2) * ch : (BLOCK + 2) * ch, :], gw_mid_ref, sem_out.at[4]
        ),
    ]
    for load in loads:
        load.start()
    upper = lax.broadcasted_iota(jnp.int32, (16, 128), 1) >= 128 // CAP

    def label(device, _):
        owner = jnp.where(upper, label_ref[device * CAP + 1], label_ref[device * CAP])
        label_rows[device] = owner.astype(F32).astype(BF16)
        return 0

    lax.fori_loop(0, label_rows.shape[0], label, 0, unroll=4)
    stores[3].start()
    wx[:, rim] = spread_sides(side_ref[...], 0)
    cx[:, rim] = spread_sides(side_ref[...], 2)

    def prepare(row, _):
        here = at_row(row, 1, ch)
        out = pl.multiple_of(row * 3 * ch, ch)
        value = wx[here, :].astype(F32)
        moved = shifted(value * sigmoid(value))
        act_in[here, :] = moved[1]
        for shift in range(3):
            sa[pl.ds(out + shift * ch, ch), :] = moved[shift]
        moved = shifted(cx[here, :])
        for shift in range(3):
            sc[pl.ds(out + shift * ch, ch), :] = moved[shift]
        return 0

    rim_ok = rim_mask(ch)

    def middle(pair, _):
        row = pair * 2
        window = at_row(row * 3, 12, ch)
        here = at_row(row + 1, 2, ch)
        act, grad = middle_step(
            w1_ref, w2f_ref, bias_ref, wx[here, :], cx[here, :], sa[window, :], sc[window, :]
        )
        out = at_row(row, 2, ch)
        act_mid[out, :] = rim_masked(act, rim_ok, breadth).astype(BF16)
        moved = shifted(rim_masked(grad, rim_ok, breadth))
        grads[out, :] = moved[1]
        for shift in range(3):
            sg[at_row(row * 3 + shift, 1, ch), :] = moved[shift][:ch]
            sg[at_row(row * 3 + 3 + shift, 1, ch), :] = moved[shift][ch:]
        return 0

    quarter = height // 4
    done = 0
    for at in range(4):
        loads[2 * at].wait()
        loads[2 * at + 1].wait()
        lax.fori_loop(at * quarter, (at + 1) * quarter, prepare, 0, unroll=UNROLL_PREPARE)
        if at == 3:
            stores[0].start()
        ready = (at + 1) * quarter // 2 - 1
        lax.fori_loop(done, ready, middle, 0, unroll=True)
        done = ready
    stores[1].start()
    stores[2].start()

    def last(pair, _):
        row = pair * 2
        back = jnp.dot(w1f_ref[...], sg[at_row(row * 3, 12, ch), core], preferred_element_type=F32)
        here = at_row(row + 2, 2, ch)
        value = wx[here, core].astype(F32)
        mid = grads[at_row(row + 1, 2, ch), core].astype(F32)
        gw[here, :] = (mid + slope_of(value, sigmoid(value)) * back).astype(BF16)
        return 0

    lax.fori_loop(0, height // 2 - 2, last, 0, unroll=UNROLL_LAST)
    stores[4].start()

    size = 256
    strip = BLOCK * ch

    def pack(part, _):
        start = pl.multiple_of(part * size, size)
        total = None
        for band in range(height // BLOCK):
            chosen = chosen_blocks(target_ref, band, start, size, breadth)
            rows = slice(band * strip + 2 * ch, (band + 1) * strip - 2 * ch)
            term = lax.dot_general(chosen, gw[rows, :], NT, preferred_element_type=F32)
            total = term if total is None else total + term
        total = total.astype(BF16).reshape(size // rows_to, rows_to, total.shape[1])
        packed[pl.ds(part * (size // rows_to), size // rows_to), :, :] = total
        return 0

    rows_to = CAP * BLOCK
    lax.fori_loop(0, packed.shape[0] * rows_to // size, pack, 0, unroll=4)
    for at in range(1, DEPTH - 1):
        stores.append(
            pltpu.make_async_copy(
                packed.at[:, :, (at - 1) * 128 : at * 128],
                packed_ref.at[:, at * rows_to : (at + 1) * rows_to, :],
                sem_out.at[4 + at],
            )
        )
        stores[-1].start()
    for store in stores:
        store.wait()


DEPTH = 8
UNROLL_PREPARE = 8
UNROLL_MIDDLE = 5
UNROLL_LAST = 14


def inner(sizes, operands, slots):
    channels, height, breadth = sizes
    wide = breadth + 128
    vmem = pl.BlockSpec(memory_space=pltpu.VMEM)
    hbm = pl.BlockSpec(memory_space=pl.ANY)
    outs = [
        jax.ShapeDtypeStruct((slots // CAP, DEPTH * CAP * BLOCK + 16, 128), BF16),
        jax.ShapeDtypeStruct(((height + 2) * channels, wide), BF16),
        jax.ShapeDtypeStruct(((height + 2) * channels, wide), BF16),
        jax.ShapeDtypeStruct((height * channels, wide), BF16),
        jax.ShapeDtypeStruct((4 * channels, breadth), BF16),
    ]
    flops = 2 * 3 * 12 * channels * 2 * channels * wide * (height // 2)
    return pl.pallas_call(
        functools.partial(inner_kernel, channels, height, breadth),
        in_specs=[hbm, hbm]
        + [vmem] * (len(operands) - 3)
        + [pl.BlockSpec(memory_space=pltpu.SMEM)],
        out_specs=[hbm] * len(outs),
        out_shape=outs,
        scratch_shapes=[
            pltpu.VMEM((height * channels, wide), BF16),
            pltpu.VMEM((height * channels, wide), BF16),
            pltpu.VMEM((height * 3 * channels, wide), BF16),
            pltpu.VMEM((height * 3 * channels, wide), BF16),
            pltpu.VMEM(((height - 2) * 3 * channels, wide), BF16),
            pltpu.VMEM((height * channels, breadth), BF16),
            pltpu.VMEM((height * channels, wide), BF16),
            pltpu.VMEM(((height - 2) * channels, wide), BF16),
            pltpu.VMEM(((height - 2) * channels, wide), BF16),
            pltpu.VMEM((slots // CAP, CAP * BLOCK, (BLOCK - 4) * channels), BF16),
            pltpu.VMEM((slots // CAP, 16, 128), BF16),
            pltpu.SemaphoreType.DMA((8,)),
            pltpu.SemaphoreType.DMA((3 + DEPTH,)),
        ],
        compiler_params=params(),
        cost_estimate=pl.CostEstimate(flops=flops, bytes_accessed=2 * 10**7, transcendentals=10**6),
        name="inner",
    )(*operands)


def outer_kernel(
    channels, height, breadth,
    xw_ref, xc_ref, up_ref, down_ref, side_hbm,
    w1_hbm, w2f_hbm, w1f_hbm, bias_hbm, target_hbm, gw_mid_hbm,
    packed_in, act_in_in, act_mid_in, g_in,
    packed_ref, act_in_ref, act_mid_ref, g_ref,
    wx, cx, sa_both, sc_both, sg_both, near, gw, act_in, act_mid, grads, packed, chosen, corner,
    side_ref, w1_ref, w2f_ref, w1f_ref, bias_ref, target_ref, gw_mid_ref, sem_in, sem_out,
):
    ch = channels
    wide = breadth + 128
    core = slice(0, breadth)
    rim = slice(breadth, wide)
    body = height * ch
    rows2 = 2 * ch
    loads = []

    def load(source, target):
        copy = pltpu.make_async_copy(source, target, sem_in.at[len(loads)])
        copy.start()
        loads.append(copy)

    load(target_hbm, target_ref)
    load(side_hbm, side_ref)
    load(up_ref.at[2 * rows2 : 2 * rows2 + 16, 0:rows2], corner.at[0])
    load(down_ref.at[2 * rows2 : 2 * rows2 + 16, 0:rows2], corner.at[1])
    load(xw_ref.at[0:rows2, :], wx.at[rows2 : 2 * rows2, core])
    load(xc_ref.at[0:rows2, :], cx.at[rows2 : 2 * rows2, core])
    load(xw_ref.at[body - rows2 : body, :], wx.at[2 * rows2 : 3 * rows2, core])
    load(xc_ref.at[body - rows2 : body, :], cx.at[2 * rows2 : 3 * rows2, core])
    load(up_ref.at[0:rows2, :], wx.at[0:rows2, core])
    load(up_ref.at[rows2 : 2 * rows2, :], cx.at[0:rows2, core])
    load(down_ref.at[0:rows2, :], wx.at[3 * rows2 : 4 * rows2, core])
    load(down_ref.at[rows2 : 2 * rows2, :], cx.at[3 * rows2 : 4 * rows2, core])
    load(g_in.at[ch : 3 * ch, :], near.at[0:rows2, :])
    load(g_in.at[body - 3 * ch : body - ch, :], near.at[rows2 : 2 * rows2, :])
    load(w1_hbm, w1_ref)
    load(w2f_hbm, w2f_ref)
    load(bias_hbm, bias_ref)
    load(w1f_hbm, w1f_ref)
    load(gw_mid_hbm, gw_mid_ref)
    loads[0].wait()
    loads[1].wait()
    for target, first in ((wx, 0), (cx, 2)):
        target[rows2 : 2 * rows2, rim] = spread_sides(side_ref[:, 0:rows2], first)
        target[2 * rows2 : 3 * rows2, rim] = spread_sides(side_ref[:, body - rows2 : body], first)
    size = 256

    def choose(part, _):
        start = pl.multiple_of(part * size, size)
        for band in range(2):
            chosen[pl.ds(start, size), band * breadth : (band + 1) * breadth] = chosen_blocks(
                target_ref, band, start, size, breadth
            )
        return 0

    lax.fori_loop(0, chosen.shape[0] // size, choose, 0, unroll=4)
    for copy in loads[2:]:
        copy.wait()
    for target, first in ((wx, 0), (cx, 2)):
        target[0:rows2, rim] = spread_sides(corner[0], first)
        target[3 * rows2 : 4 * rows2, rim] = spread_sides(corner[1], first)
    rim_ok = rim_mask(ch)
    sub = lax.broadcasted_iota(jnp.int32, (2 * ch, wide), 0)

    for half in range(2):
        base = half * 2 * rows2
        sa, sc, sg = sa_both.at[half], sc_both.at[half], sg_both.at[half]
        for row in range(4):
            here = slice(base + row * ch, base + (row + 1) * ch)
            value = wx[here, :].astype(F32)
            moved = shifted(value * sigmoid(value))
            if row == 1 + half:
                act_in[half * ch : (half + 1) * ch, :] = moved[1]
            for shift in range(3):
                sa[(row * 3 + shift) * ch : (row * 3 + shift + 1) * ch, :] = moved[shift]
            moved = shifted(cx[here, :])
            for shift in range(3):
                sc[(row * 3 + shift) * ch : (row * 3 + shift + 1) * ch, :] = moved[shift]
        here = slice(base + ch, base + 3 * ch)
        act, grad = middle_step(
            w1_ref, w2f_ref, bias_ref, wx[here, :], cx[here, :], sa[...], sc[...]
        )
        inside_at = 0 if half == 0 else lax.axis_size("rows") - 1
        limit = jnp.where(lax.axis_index("rows") == inside_at, ch, 0 if half == 0 else 2 * ch)
        good = (sub >= limit) if half == 0 else (sub < limit)
        act = jnp.where(good, rim_masked(act, rim_ok, breadth), 0.0)
        grad = jnp.where(good, rim_masked(grad, rim_ok, breadth), 0.0)
        act_mid[half * rows2 : (half + 1) * rows2, :] = act.astype(BF16)
        mine = shifted(grad)
        other = shifted(near[half * rows2 : (half + 1) * rows2, :].astype(F32))
        own = mine[1][ch:] if half == 0 else mine[1][:ch]
        grads[half * ch : (half + 1) * ch, :] = own
        order = (mine, other) if half == 0 else (other, mine)
        for pair in range(2):
            for row in range(2):
                for shift in range(3):
                    out = ((pair * 2 + row) * 3 + shift) * ch
                    sg[out : out + ch, :] = order[pair][shift][row * ch : (row + 1) * ch]
        back = jnp.dot(w1f_ref[...], sg[:, core], preferred_element_type=F32)
        inside = slice(rows2, 2 * rows2) if half == 0 else slice(2 * rows2, 3 * rows2)
        value = wx[inside, core].astype(F32)
        mid = jnp.concatenate([order[0][1][ch:, core], order[1][1][:ch, core]], axis=0).astype(F32)
        gw[half * rows2 : (half + 1) * rows2, :] = (
            mid + slope_of(value, sigmoid(value)) * back
        ).astype(BF16)

    rows_to = CAP * BLOCK
    stores = [
        (act_in.at[0:ch, :], act_in_ref.at[0:ch, :]),
        (act_in.at[ch : 2 * ch, :], act_in_ref.at[body + ch : body + 2 * ch, :]),
        (act_mid.at[0:rows2, :], act_mid_ref.at[0:rows2, :]),
        (act_mid.at[rows2 : 2 * rows2, :], act_mid_ref.at[body : body + 2 * ch, :]),
        (grads.at[0:ch, :], g_ref.at[0:ch, :]),
        (grads.at[ch : 2 * ch, :], g_ref.at[body - ch : body, :]),
        (packed.at[:, :, 0:rows2], packed_ref.at[:, 0:rows_to, :]),
        (
            packed.at[:, :, rows2 : 2 * rows2],
            packed_ref.at[:, (DEPTH - 1) * rows_to : DEPTH * rows_to, :],
        ),
    ]
    stores = [
        pltpu.make_async_copy(source, target, sem_out.at[at])
        for at, (source, target) in enumerate(stores)
    ]
    for store in stores[:6]:
        store.start()
    both = (
        jnp.concatenate([gw[0:rows2, :], gw_mid_ref[0:rows2, :]], axis=0),
        jnp.concatenate([gw_mid_ref[rows2 : 2 * rows2, :], gw[rows2 : 2 * rows2, :]], axis=0),
    )

    def pack(part, _):
        rows = pl.ds(pl.multiple_of(part * size, size), size)
        total = sum(
            lax.dot_general(
                chosen[rows, band * breadth : (band + 1) * breadth],
                both[band],
                NT,
                preferred_element_type=F32,
            )
            for band in range(2)
        ).astype(BF16)
        packed[pl.ds(part * (size // rows_to), size // rows_to), :, :] = total.reshape(
            size // rows_to, rows_to, total.shape[1]
        )
        return 0

    lax.fori_loop(0, chosen.shape[0] // size, pack, 0, unroll=4)
    for store in stores[6:]:
        store.start()
    for store in stores:
        store.wait()


def outer(sizes, operands, state, slots):
    channels, height, breadth = sizes
    wide = breadth + 128
    hbm = pl.BlockSpec(memory_space=pl.ANY)
    inputs = len(operands)
    return pl.pallas_call(
        functools.partial(outer_kernel, channels, height, breadth),
        in_specs=[hbm] * (inputs + len(state)),
        out_specs=[hbm] * len(state),
        out_shape=[jax.ShapeDtypeStruct(item.shape, item.dtype) for item in state],
        input_output_aliases={inputs + at: at for at in range(len(state))},
        scratch_shapes=[
            pltpu.VMEM((8 * channels, wide), BF16),
            pltpu.VMEM((8 * channels, wide), BF16),
            pltpu.VMEM((2, 12 * channels, wide), BF16),
            pltpu.VMEM((2, 12 * channels, wide), BF16),
            pltpu.VMEM((2, 12 * channels, wide), BF16),
            pltpu.VMEM((4 * channels, wide), BF16),
            pltpu.VMEM((4 * channels, breadth), BF16),
            pltpu.VMEM((2 * channels, wide), BF16),
            pltpu.VMEM((4 * channels, wide), BF16),
            pltpu.VMEM((2 * channels, wide), BF16),
            pltpu.VMEM((slots // CAP, CAP * BLOCK, 4 * channels), BF16),
            pltpu.VMEM((slots * BLOCK, 2 * breadth), BF16),
            pltpu.VMEM((2, 16, 2 * channels), BF16),
            *[pltpu.VMEM(item.shape, item.dtype) for item in operands[4:]],
            pltpu.SemaphoreType.DMA((19,)),
            pltpu.SemaphoreType.DMA((8,)),
        ],
        compiler_params=params(),
        name="outer",
    )(*operands, *state)


def correlate_kernel(
    channels, height, breadth,
    act_in_ref, act_mid_ref, g_ref, xc_ref, out_ref,
    image1, image2, g, c, s1, s2, acc1, acc2, sum1, sum2, sem,
):
    ch = channels
    wide = breadth + 128
    core = slice(0, breadth)
    loads = [
        pltpu.make_async_copy(source, target, sem.at[at])
        for at, (source, target) in enumerate(
            ((g_ref.at[:, core], g), (xc_ref, c), (act_in_ref, image1), (act_mid_ref, image2))
        )
    ]
    for load in loads:
        load.start()
    for ref in (acc1, acc2, sum1, sum2):
        ref[...] = jnp.zeros_like(ref)
    empty = jnp.zeros((ch, wide - breadth), F32)

    def prepare(row, source, target, total):
        value = source[at_row(row, 1, ch), :].astype(F32)
        total[...] += value
        right, here, left = shifted(jnp.concatenate([value, empty], axis=1))
        for shift, moved in enumerate((left, here, right)):
            target[at_row(row * 3 + shift, 1, ch), :] = moved

    def add(pair, image, grads, acc):
        acc[...] += lax.dot_general(
            grads[at_row(pair * 6, 6, ch), :],
            image[at_row(pair * 2, 4, ch), :],
            NT,
            preferred_element_type=F32,
        )

    loads[0].wait()
    loads[1].wait()

    def step(row, _):
        prepare(row, g, s1, sum1)
        prepare(row, c, s2, sum2)
        return 0

    def products(pair, _):
        add(pair, image1, s1, acc1)
        add(pair, image2, s2, acc2)
        return 0

    lax.fori_loop(0, height, step, 0, unroll=4)
    loads[2].wait()
    loads[3].wait()
    lax.fori_loop(0, height // 2, products, 0, unroll=4)

    first, second = (
        acc[0 : 3 * ch, :] + pltpu.roll(acc[3 * ch : 6 * ch, :], 3 * ch, 1) for acc in (acc1, acc2)
    )
    second = pltpu.roll(second, ch, 1)
    low = lax.broadcasted_iota(jnp.int32, (3 * ch, 128), 1) < ch
    out_ref[0 : 3 * ch, :] = first[:, 0:128]
    out_ref[3 * ch : 6 * ch, :] = jnp.where(low, first[:, 128:256], second[:, 0:128])
    out_ref[6 * ch : 9 * ch, :] = second[:, 128:256]
    sums = jnp.concatenate(
        [jnp.sum(total[...], axis=1, keepdims=True) for total in (sum1, sum2)], axis=0
    )
    out_ref[9 * ch :, :] = jnp.broadcast_to(sums, (2 * ch, 2 * ch)).T[0:8, :]


def correlate(sizes, act_in, act_mid, g_mid, xc):
    channels, height, breadth = sizes
    wide = breadth + 128
    hbm = pl.BlockSpec(memory_space=pl.ANY)
    flops = 2 * 2 * 12 * channels * 2 * channels * breadth * (height // 2)
    return pl.pallas_call(
        functools.partial(correlate_kernel, channels, height, breadth),
        in_specs=[hbm] * 4,
        out_specs=pl.BlockSpec(memory_space=pltpu.VMEM),
        out_shape=jax.ShapeDtypeStruct((9 * channels + 8, 2 * channels), F32),
        scratch_shapes=[
            pltpu.VMEM(((height + 2) * channels, wide), BF16),
            pltpu.VMEM(((height + 2) * channels, wide), BF16),
            pltpu.VMEM((height * channels, breadth), BF16),
            pltpu.VMEM((height * channels, breadth), BF16),
            pltpu.VMEM((height * 3 * channels, wide), BF16),
            pltpu.VMEM((height * 3 * channels, wide), BF16),
            pltpu.VMEM((6 * channels, 4 * channels), F32),
            pltpu.VMEM((6 * channels, 4 * channels), F32),
            pltpu.VMEM((channels, breadth), F32),
            pltpu.VMEM((channels, breadth), F32),
            pltpu.SemaphoreType.DMA((4,)),
        ],
        compiler_params=params(),
        cost_estimate=pl.CostEstimate(flops=flops, bytes_accessed=10**7, transcendentals=0),
        name="correlate",
    )(act_in, act_mid, g_mid, xc)


def unpack_kernel(channels, arrived_ref, label_ref, out_ref, chosen, flat):
    devices = arrived_ref.shape[0]
    block_rows, part, breadth = out_ref.shape[1], out_ref.shape[3], out_ref.shape[4]
    rows_to = CAP * BLOCK

    @pl.when(pl.program_id(0) == 0)
    def _():
        shape = (BLOCK, block_rows * breadth)
        place = lax.broadcasted_iota(jnp.int32, shape, 1) - lax.broadcasted_iota(jnp.int32, shape, 0)
        place = place.astype(F32)

        def select(source, _):
            label = label_ref[source].astype(F32) * BLOCK
            for rank in range(CAP):
                at = rank * (128 // CAP)
                hit = (place == label[:, at : at + 1]).astype(F32).astype(BF16)
                row = pl.multiple_of(source * rows_to + rank * BLOCK, BLOCK)
                chosen[pl.ds(row, BLOCK), :] = hit
            return 0

        lax.fori_loop(0, devices, select, 0, unroll=4)

    for at in range(arrived_ref.shape[1] // rows_to):
        tile = arrived_ref[:, at * rows_to : (at + 1) * rows_to, :]
        flat[at * 128 : (at + 1) * 128, :] = tile.reshape(devices * rows_to, 128).T
    for band in range(block_rows):
        summed = jnp.dot(
            flat[...], chosen[:, band * breadth : (band + 1) * breadth], preferred_element_type=F32
        )
        cube = summed.reshape(part, channels, breadth)
        out_ref[:, band, 0, :, :] = jnp.swapaxes(cube, 0, 1)


def unpack(sizes, arrived):
    channels, height, breadth = sizes
    block_rows = height // BLOCK
    devices = arrived.shape[0]
    rows_to = CAP * BLOCK
    part = 8
    tiles = DEPTH * part // BLOCK
    return pl.pallas_call(
        functools.partial(unpack_kernel, channels),
        grid=(BLOCK // part,),
        in_specs=[
            pl.BlockSpec((devices, tiles * rows_to, 128), lambda h: (0, h, 0)),
            pl.BlockSpec((devices, 16, 128), lambda h: (0, DEPTH * rows_to // 16, 0)),
        ],
        out_specs=pl.BlockSpec((channels, block_rows, 1, part, breadth), lambda h: (0, 0, h, 0, 0)),
        out_shape=jax.ShapeDtypeStruct((channels, block_rows, BLOCK // part, part, breadth), F32),
        scratch_shapes=[
            pltpu.VMEM((devices * rows_to, block_rows * breadth), BF16),
            pltpu.VMEM((part * channels, devices * rows_to), BF16),
        ],
        compiler_params=params(),
        name="unpack",
    )(arrived, arrived)


def shift_pairs(axis, step):
    count = lax.axis_size(axis)
    return [(i, i + step) for i in range(count) if 0 <= i + step < count]


def finish_kernel(channels, factor, total_ref, other_ref, w1_ref, w2_ref, b1_ref, b2_ref, terms):
    ch = channels
    half = total_ref.shape[0]
    bit = lax.rem(lax.axis_index("rows") * lax.axis_size("cols") + lax.axis_index("cols"), 2)
    terms[pl.ds(pl.multiple_of(bit * half, 8), half), :] = total_ref[...] * factor
    terms[pl.ds(pl.multiple_of((1 - bit) * half, 8), half), :] = other_ref[...] * factor
    tile = lambda at: terms[at * 3 * ch : (at + 1) * 3 * ch, :]
    for out, parts in ((w1_ref, ((0, 0), (0, 1), (1, 0))), (w2_ref, ((1, 1), (2, 0), (2, 1)))):
        for row, (at, side) in enumerate(parts):
            value = pltpu.roll(tile(at), ch, 1) if side else tile(at)
            for col in range(3):
                out[row, col] = value[col * ch : (col + 1) * ch, 0:ch]
    bias = terms[9 * ch : 9 * ch + 8, :]
    b1_ref[...] = bias[0:1, 0:ch]
    b2_ref[...] = pltpu.roll(bias, ch, 1)[0:1, 0:ch]


def finish(channels, factor, total, other):
    vmem = pl.BlockSpec(memory_space=pltpu.VMEM)
    kernel = jax.ShapeDtypeStruct((3, 3, channels, channels), F32)
    bias = jax.ShapeDtypeStruct((1, channels), F32)
    w1, w2, b1, b2 = pl.pallas_call(
        functools.partial(finish_kernel, channels, factor),
        in_specs=[vmem, vmem],
        out_specs=[vmem] * 4,
        out_shape=[kernel, kernel, bias, bias],
        scratch_shapes=[pltpu.VMEM((2 * total.shape[0], 128), F32)],
        compiler_params=params(),
        name="finish",
    )(total, other)
    order = (2, 3, 0, 1)
    return jnp.transpose(w1, order), b1[0], jnp.transpose(w2, order), b2[0]


def total_over_devices(terms, devices, frame_of):
    me = lax.axis_index(AXES)
    swap = lambda value, step: lax.ppermute(value, AXES, [(i, i ^ step) for i in range(devices)])
    bit = me % 2
    half = terms.shape[0] // 2
    mine = lax.dynamic_slice_in_dim(terms, bit * half, half, 0)
    away = lax.dynamic_slice_in_dim(terms, (1 - bit) * half, half, 0)
    total = mine + swap(away, 1)
    step = 2
    while 2 * step < devices:
        total = total + swap(total, step)
        step *= 2
    other = swap(total, step)
    frame = frame_of()
    other, frame = lax.optimization_barrier((other, frame))
    total = total + other
    return total, swap(total, 1), frame


def body(warped, cotangent, w_first, b_first, w_second, source_tile, source_block):
    sizes = warped.shape
    channels, height, breadth = sizes
    row_count = lax.axis_size("rows")
    col_count = lax.axis_size("cols")
    devices = row_count * col_count
    slots = devices * CAP
    factor = 1.0 / math.sqrt(height * row_count * breadth * col_count)
    me = lax.axis_index(AXES)

    block_rows = height // BLOCK
    count = source_tile.size
    target = source_tile.reshape(count)
    same = target[:, None] == target[None, :]
    earlier = jnp.arange(count)[None, :] < jnp.arange(count)[:, None]
    ranking = jnp.sum((same & earlier).astype(jnp.int32), axis=1)
    places = target * CAP + ranking
    target_row = (
        places.reshape(block_rows, -1, 1) * BLOCK + jnp.arange(BLOCK, dtype=jnp.int32)
    ).reshape(block_rows, breadth)
    hits = places[:, None] == jnp.arange(slots, dtype=jnp.int32)[None, :]
    labels = jnp.sum(jnp.where(hits, source_block.reshape(count, 1) + 1, 0), axis=0) - 1
    xw, xc, to_right, to_left, to_up, to_down, first, second_back, first_back, bias = reorder(
        warped, cotangent, w_first, w_second, b_first
    )
    rim = 2 * channels
    side = lax.ppermute(to_right, "cols", shift_pairs("cols", 1)) + lax.ppermute(
        to_left, "cols", shift_pairs("cols", -1)
    )
    to_down = lax.dynamic_update_slice(to_down, side[:, -rim:], (2 * rim, 0))
    to_up = lax.dynamic_update_slice(to_up, side[:, :rim], (2 * rim, 0))
    up = lax.ppermute(to_down, "rows", shift_pairs("rows", 1))
    down = lax.ppermute(to_up, "rows", shift_pairs("rows", -1))

    *state, gw_mid = inner(
        sizes, (xw, xc, side, first, second_back, first_back, bias, target_row, labels), slots
    )
    packed, act_in, act_mid, g_mid = outer(
        sizes,
        (
            xw, xc, up, down, side,
            first, second_back, first_back, bias, target_row, gw_mid,
        ),
        state,
        slots,
    )
    arrived = lax.all_to_all(packed, AXES, split_axis=0, concat_axis=0, tiled=True)

    terms = correlate(sizes, act_in, act_mid, g_mid, xc)
    fill = jnp.zeros((-terms.shape[0] % 16, 128), F32)
    total, other, frame = total_over_devices(
        jnp.concatenate([terms, fill], axis=0),
        devices,
        lambda: unpack(sizes, arrived),
    )
    return (frame.reshape(sizes), *finish(channels, factor, total, other))


def solution(mesh):
    in_specs = (
        P(None, "rows", "cols"),
        P(None, "rows", "cols"),
        P(),
        P(),
        P(),
        P("rows", "cols"),
        P("rows", "cols"),
    )
    out_specs = (P(None, "rows", "cols"), P(), P(), P(), P())
    return jax.shard_map(body, mesh=mesh, in_specs=in_specs, out_specs=out_specs, check_vma=False)
```

```python
import functools
import math

import jax
import jax.numpy as jnp
from jax import lax
from jax.experimental import pallas as pl
from jax.experimental.pallas import tpu as pltpu
from jax.sharding import PartitionSpec as P

BLOCK = 16
CAP = 2
AXES = ("rows", "cols")
BF16 = jnp.bfloat16
F32 = jnp.float32
NT = (((1,), (1,)), ((), ()))
TN = (((0,), (0,)), ((), ()))
VMEM_BYTES = 63 * 2**20


def params(**extra):
    return pltpu.CompilerParams(vmem_limit_bytes=VMEM_BYTES, **extra)


def sigmoid(value):
    return 0.5 * jnp.tanh(0.5 * value) + 0.5


def one_hot(shape, pairs):
    row = lax.broadcasted_iota(jnp.int32, shape, 0)
    col = lax.broadcasted_iota(jnp.int32, shape, 1)
    hit = jnp.zeros(shape, jnp.bool_)
    for at_row, at_col in pairs:
        hit = hit | ((row == at_row) & (col == at_col))
    return hit.astype(F32).astype(BF16)


def shifted(value):
    value = value.astype(BF16)
    return pltpu.roll(value, 1, 1), value, pltpu.roll(value, value.shape[1] - 1, 1)


def slope_of(value, sigma):
    return sigma + value * sigma * (1.0 - sigma)


def at_row(row, rows, channels):
    return pl.ds(pl.multiple_of(row * channels, channels), rows * channels)


def pair_weights(taps_ref, out_ref, flip):
    ch = taps_ref.shape[2]
    out_ref[...] = jnp.zeros_like(out_ref)
    for row in range(3):
        for col in range(3):
            if flip:
                tap = taps_ref[2 - row, 2 - col].astype(F32).T.astype(BF16)
            else:
                tap = taps_ref[row, col]
            at = (row * 3 + col) * ch
            out_ref[0:ch, at : at + ch] = tap
            out_ref[ch : 2 * ch, at + 3 * ch : at + 4 * ch] = tap


def reorder_kernel(
    w_ref, c_ref, first_ref, second_ref, b_ref,
    xw_ref, xc_ref, to_right_ref, to_left_ref, to_up_ref, to_down_ref,
    w1_ref, w2f_ref, w1f_ref, bias_ref,
):
    channels, rows, lanes = w_ref.shape

    @pl.when((pl.program_id(0) == 0) & (pl.program_id(1) == 1))
    def _():
        pair_weights(first_ref, w1_ref, False)
        pair_weights(second_ref, w2f_ref, True)
        pair_weights(first_ref, w1f_ref, True)
        column = jnp.broadcast_to(b_ref[...], (2 * channels, channels)).T
        bias_ref[0:channels, :] = column
        bias_ref[channels:, :] = column

    rim = 2 * channels
    kept = []
    for source, target in ((w_ref, xw_ref), (c_ref, xc_ref)):
        value = source[...].astype(F32)
        swapped = jnp.swapaxes(value, 0, 1).reshape(rows * channels, lanes).astype(BF16)
        target[...] = swapped
        kept.append(swapped)

    @pl.when(pl.program_id(1) == 0)
    def _():
        to_up_ref[0:rim, :] = kept[0][0:rim]
        to_up_ref[rim : 2 * rim, :] = kept[1][0:rim]
        to_up_ref[2 * rim :, :] = jnp.zeros((16, lanes), BF16)

    @pl.when(pl.program_id(1) == pl.num_programs(1) - 1)
    def _():
        to_down_ref[0:rim, :] = kept[0][rows * channels - rim :]
        to_down_ref[rim : 2 * rim, :] = kept[1][rows * channels - rim :]
        to_down_ref[2 * rim :, :] = jnp.zeros((16, lanes), BF16)

    here = pl.ds(pl.multiple_of(pl.program_id(1) * rows * channels, 128), rows * channels)

    def pick(tile, w_pairs, c_pairs):
        return sum(
            lax.dot_general(
                one_hot((16, 128), pairs), value[:, tile], NT, preferred_element_type=F32
            )
            for value, pairs in zip(kept, (w_pairs, c_pairs))
        ).astype(BF16)

    @pl.when(pl.program_id(0) == pl.num_programs(0) - 1)
    def _():
        final = slice(lanes - 128, lanes)
        to_right_ref[:, here] = pick(final, ((0, 126), (1, 127)), ((2, 126), (3, 127)))

    @pl.when(pl.program_id(0) == 0)
    def _():
        to_left_ref[:, here] = pick(slice(0, 128), ((4, 0), (5, 1)), ((6, 0), (7, 1)))


def reorder(warped, cotangent, w_first, w_second, b_first):
    channels, height, breadth = warped.shape
    whole = lambda shape: pl.BlockSpec(shape, lambda x, h: (0,) * len(shape))
    step = 16
    lanes = breadth
    spec_in = pl.BlockSpec((channels, step, lanes), lambda x, h: (0, h, x))
    spec_out = pl.BlockSpec((step * channels, lanes), lambda x, h: (h, x))
    spec_edge = pl.BlockSpec((16, height * channels), lambda x, h: (0, 0))
    spec_rim = pl.BlockSpec((4 * channels + 16, lanes), lambda x, h: (0, x))
    shape = jax.ShapeDtypeStruct((height * channels, breadth), BF16)
    edge = jax.ShapeDtypeStruct((16, height * channels), BF16)
    rim = jax.ShapeDtypeStruct((4 * channels + 16, breadth), BF16)
    weights = jax.ShapeDtypeStruct((2 * channels, 12 * channels), BF16)
    bias = jax.ShapeDtypeStruct((2 * channels, 2 * channels), F32)
    return pl.pallas_call(
        reorder_kernel,
        grid=(breadth // lanes, height // step),
        in_specs=[spec_in, spec_in]
        + [whole(w_first.shape[2:] + w_first.shape[:2])] * 2
        + [whole((1, channels))],
        out_specs=[spec_out, spec_out, spec_edge, spec_edge, spec_rim, spec_rim]
        + [whole(weights.shape)] * 3
        + [whole(bias.shape)],
        out_shape=[shape, shape, edge, edge, rim, rim, weights, weights, weights, bias],
        compiler_params=params(),
        name="reorder",
    )(
        warped,
        cotangent,
        jnp.transpose(w_first, (2, 3, 0, 1)),
        jnp.transpose(w_second, (2, 3, 0, 1)),
        b_first[None, :],
    )


def spread_sides(side, first):
    spread = one_hot((16, 128), ((first, 126), (first + 1, 127), (first + 4, 0), (first + 5, 1)))
    return lax.dot_general(side, spread, TN, preferred_element_type=F32).astype(BF16)


def rim_mask(channels):
    lane = lax.broadcasted_iota(jnp.int32, (2 * channels, 128), 1)
    col = lax.axis_index("cols")
    right = jnp.where(col < lax.axis_size("cols") - 1, 0, -1)
    left = jnp.where(col > 0, 127, -1)
    return (lane == right) | (lane == left)


def middle_step(w1_ref, w2f_ref, bias_ref, value, cot, act_window, cot_window):
    conv = jnp.dot(w1_ref[...], act_window, preferred_element_type=F32)
    back = jnp.dot(w2f_ref[...], cot_window, preferred_element_type=F32)
    a_mid = (value.astype(F32) + conv + bias_ref[:, 0:1]).astype(BF16).astype(F32)
    sigma = sigmoid(a_mid)
    return a_mid * sigma, cot.astype(F32) + slope_of(a_mid, sigma) * back


def rim_masked(value, rim_ok, breadth):
    return jnp.concatenate(
        [value[:, :breadth], jnp.where(rim_ok, value[:, breadth:], 0.0)], axis=1
    )


def chosen_blocks(target_ref, band, start, size, breadth):
    row_at = lax.broadcasted_iota(jnp.int32, (size, breadth), 0) + start
    return (row_at == target_ref[band : band + 1, :]).astype(F32).astype(BF16)


def inner_kernel(
    channels, height, breadth,
    xw_ref, xc_ref, side_ref, w1_ref, w2f_ref, w1f_ref, bias_ref, target_ref, label_ref,
    packed_ref, act_in_ref, act_mid_ref, g_ref, gw_mid_ref,
    wx, cx, sa, sc, sg, gw, act_in, act_mid, grads, packed, label_rows, sem_in, sem_out,
):
    ch = channels
    wide = breadth + 128
    core = slice(0, breadth)
    rim = slice(breadth, wide)
    step = height * ch // 4
    loads = [
        pltpu.make_async_copy(
            source.at[at * step : (at + 1) * step, :],
            target.at[at * step : (at + 1) * step, core],
            sem_in.at[2 * at + which],
        )
        for at in range(4)
        for which, (source, target) in enumerate(((xw_ref, wx), (xc_ref, cx)))
    ]
    stores = [
        pltpu.make_async_copy(act_in, act_in_ref.at[ch : ch + height * ch, :], sem_out.at[0]),
        pltpu.make_async_copy(act_mid, act_mid_ref.at[2 * ch : height * ch, :], sem_out.at[1]),
        pltpu.make_async_copy(grads, g_ref.at[ch : (height - 1) * ch, :], sem_out.at[2]),
        pltpu.make_async_copy(
            label_rows, packed_ref.at[:, DEPTH * CAP * BLOCK : DEPTH * CAP * BLOCK + 16, :], sem_out.at[3]
        ),
        pltpu.make_async_copy(
            gw.at[(BLOCK - 2) * ch : (BLOCK + 2) * ch, :], gw_mid_ref, sem_out.at[4]
        ),
    ]
    for load in loads:
        load.start()
    upper = lax.broadcasted_iota(jnp.int32, (16, 128), 1) >= 128 // CAP

    def label(device, _):
        owner = jnp.where(upper, label_ref[device * CAP + 1], label_ref[device * CAP])
        label_rows[device] = owner.astype(F32).astype(BF16)
        return 0

    lax.fori_loop(0, label_rows.shape[0], label, 0, unroll=4)
    stores[3].start()
    wx[:, rim] = spread_sides(side_ref[...], 0)
    cx[:, rim] = spread_sides(side_ref[...], 2)

    def prepare(row, _):
        here = at_row(row, 1, ch)
        out = pl.multiple_of(row * 3 * ch, ch)
        value = wx[here, :].astype(F32)
        moved = shifted(value * sigmoid(value))
        act_in[here, :] = moved[1]
        for shift in range(3):
            sa[pl.ds(out + shift * ch, ch), :] = moved[shift]
        moved = shifted(cx[here, :])
        for shift in range(3):
            sc[pl.ds(out + shift * ch, ch), :] = moved[shift]
        return 0

    rim_ok = rim_mask(ch)

    def middle(pair, _):
        row = pair * 2
        window = at_row(row * 3, 12, ch)
        here = at_row(row + 1, 2, ch)
        act, grad = middle_step(
            w1_ref, w2f_ref, bias_ref, wx[here, :], cx[here, :], sa[window, :], sc[window, :]
        )
        out = at_row(row, 2, ch)
        act_mid[out, :] = rim_masked(act, rim_ok, breadth).astype(BF16)
        moved = shifted(rim_masked(grad, rim_ok, breadth))
        grads[out, :] = moved[1]
        for shift in range(3):
            sg[at_row(row * 3 + shift, 1, ch), :] = moved[shift][:ch]
            sg[at_row(row * 3 + 3 + shift, 1, ch), :] = moved[shift][ch:]
        return 0

    quarter = height // 4
    done = 0
    for at in range(4):
        loads[2 * at].wait()
        loads[2 * at + 1].wait()
        lax.fori_loop(at * quarter, (at + 1) * quarter, prepare, 0, unroll=UNROLL_PREPARE)
        if at == 3:
            stores[0].start()
        ready = (at + 1) * quarter // 2 - 1
        lax.fori_loop(done, ready, middle, 0, unroll=True)
        done = ready
    stores[1].start()
    stores[2].start()

    def last(pair, _):
        row = pair * 2
        back = jnp.dot(w1f_ref[...], sg[at_row(row * 3, 12, ch), core], preferred_element_type=F32)
        here = at_row(row + 2, 2, ch)
        value = wx[here, core].astype(F32)
        mid = grads[at_row(row + 1, 2, ch), core].astype(F32)
        gw[here, :] = (mid + slope_of(value, sigmoid(value)) * back).astype(BF16)
        return 0

    lax.fori_loop(0, height // 2 - 2, last, 0, unroll=UNROLL_LAST)
    stores[4].start()

    size = 256
    strip = BLOCK * ch

    def pack(part, _):
        start = pl.multiple_of(part * size, size)
        total = None
        for band in range(height // BLOCK):
            chosen = chosen_blocks(target_ref, band, start, size, breadth)
            rows = slice(band * strip + 2 * ch, (band + 1) * strip - 2 * ch)
            term = lax.dot_general(chosen, gw[rows, :], NT, preferred_element_type=F32)
            total = term if total is None else total + term
        total = total.astype(BF16).reshape(size // rows_to, rows_to, total.shape[1])
        packed[pl.ds(part * (size // rows_to), size // rows_to), :, :] = total
        return 0

    rows_to = CAP * BLOCK
    lax.fori_loop(0, packed.shape[0] * rows_to // size, pack, 0, unroll=4)
    for at in range(1, DEPTH - 1):
        stores.append(
            pltpu.make_async_copy(
                packed.at[:, :, (at - 1) * 128 : at * 128],
                packed_ref.at[:, at * rows_to : (at + 1) * rows_to, :],
                sem_out.at[4 + at],
            )
        )
        stores[-1].start()
    for store in stores:
        store.wait()


DEPTH = 8
UNROLL_PREPARE = 8
UNROLL_MIDDLE = 5
UNROLL_LAST = 14


def inner(sizes, operands, slots):
    channels, height, breadth = sizes
    wide = breadth + 128
    vmem = pl.BlockSpec(memory_space=pltpu.VMEM)
    hbm = pl.BlockSpec(memory_space=pl.ANY)
    outs = [
        jax.ShapeDtypeStruct((slots // CAP, DEPTH * CAP * BLOCK + 16, 128), BF16),
        jax.ShapeDtypeStruct(((height + 2) * channels, wide), BF16),
        jax.ShapeDtypeStruct(((height + 2) * channels, wide), BF16),
        jax.ShapeDtypeStruct((height * channels, wide), BF16),
        jax.ShapeDtypeStruct((4 * channels, breadth), BF16),
    ]
    flops = 2 * 3 * 12 * channels * 2 * channels * wide * (height // 2)
    return pl.pallas_call(
        functools.partial(inner_kernel, channels, height, breadth),
        in_specs=[hbm, hbm]
        + [vmem] * (len(operands) - 3)
        + [pl.BlockSpec(memory_space=pltpu.SMEM)],
        out_specs=[hbm] * len(outs),
        out_shape=outs,
        scratch_shapes=[
            pltpu.VMEM((height * channels, wide), BF16),
            pltpu.VMEM((height * channels, wide), BF16),
            pltpu.VMEM((height * 3 * channels, wide), BF16),
            pltpu.VMEM((height * 3 * channels, wide), BF16),
            pltpu.VMEM(((height - 2) * 3 * channels, wide), BF16),
            pltpu.VMEM((height * channels, breadth), BF16),
            pltpu.VMEM((height * channels, wide), BF16),
            pltpu.VMEM(((height - 2) * channels, wide), BF16),
            pltpu.VMEM(((height - 2) * channels, wide), BF16),
            pltpu.VMEM((slots // CAP, CAP * BLOCK, (BLOCK - 4) * channels), BF16),
            pltpu.VMEM((slots // CAP, 16, 128), BF16),
            pltpu.SemaphoreType.DMA((8,)),
            pltpu.SemaphoreType.DMA((3 + DEPTH,)),
        ],
        compiler_params=params(),
        cost_estimate=pl.CostEstimate(flops=flops, bytes_accessed=2 * 10**7, transcendentals=10**6),
        name="inner",
    )(*operands)


def outer_kernel(
    channels, height, breadth,
    xw_ref, xc_ref, up_ref, down_ref, side_hbm,
    w1_hbm, w2f_hbm, w1f_hbm, bias_hbm, target_hbm, gw_mid_hbm,
    packed_in, act_in_in, act_mid_in, g_in,
    packed_ref, act_in_ref, act_mid_ref, g_ref,
    wx, cx, sa_both, sc_both, sg_both, near, gw, act_in, act_mid, grads, packed, chosen, corner,
    side_ref, w1_ref, w2f_ref, w1f_ref, bias_ref, target_ref, gw_mid_ref, sem_in, sem_out,
):
    ch = channels
    wide = breadth + 128
    core = slice(0, breadth)
    rim = slice(breadth, wide)
    body = height * ch
    rows2 = 2 * ch
    loads = []

    def load(source, target):
        copy = pltpu.make_async_copy(source, target, sem_in.at[len(loads)])
        copy.start()
        loads.append(copy)

    load(target_hbm, target_ref)
    load(side_hbm, side_ref)
    load(up_ref.at[2 * rows2 : 2 * rows2 + 16, 0:rows2], corner.at[0])
    load(down_ref.at[2 * rows2 : 2 * rows2 + 16, 0:rows2], corner.at[1])
    load(xw_ref.at[0:rows2, :], wx.at[rows2 : 2 * rows2, core])
    load(xc_ref.at[0:rows2, :], cx.at[rows2 : 2 * rows2, core])
    load(xw_ref.at[body - rows2 : body, :], wx.at[2 * rows2 : 3 * rows2, core])
    load(xc_ref.at[body - rows2 : body, :], cx.at[2 * rows2 : 3 * rows2, core])
    load(up_ref.at[0:rows2, :], wx.at[0:rows2, core])
    load(up_ref.at[rows2 : 2 * rows2, :], cx.at[0:rows2, core])
    load(down_ref.at[0:rows2, :], wx.at[3 * rows2 : 4 * rows2, core])
    load(down_ref.at[rows2 : 2 * rows2, :], cx.at[3 * rows2 : 4 * rows2, core])
    load(g_in.at[ch : 3 * ch, :], near.at[0:rows2, :])
    load(g_in.at[body - 3 * ch : body - ch, :], near.at[rows2 : 2 * rows2, :])
    load(w1_hbm, w1_ref)
    load(w2f_hbm, w2f_ref)
    load(bias_hbm, bias_ref)
    load(w1f_hbm, w1f_ref)
    load(gw_mid_hbm, gw_mid_ref)
    loads[0].wait()
    loads[1].wait()
    for target, first in ((wx, 0), (cx, 2)):
        target[rows2 : 2 * rows2, rim] = spread_sides(side_ref[:, 0:rows2], first)
        target[2 * rows2 : 3 * rows2, rim] = spread_sides(side_ref[:, body - rows2 : body], first)
    size = 256

    def choose(part, _):
        start = pl.multiple_of(part * size, size)
        for band in range(2):
            chosen[pl.ds(start, size), band * breadth : (band + 1) * breadth] = chosen_blocks(
                target_ref, band, start, size, breadth
            )
        return 0

    lax.fori_loop(0, chosen.shape[0] // size, choose, 0, unroll=4)
    for copy in loads[2:]:
        copy.wait()
    for target, first in ((wx, 0), (cx, 2)):
        target[0:rows2, rim] = spread_sides(corner[0], first)
        target[3 * rows2 : 4 * rows2, rim] = spread_sides(corner[1], first)
    rim_ok = rim_mask(ch)
    sub = lax.broadcasted_iota(jnp.int32, (2 * ch, wide), 0)

    for half in range(2):
        base = half * 2 * rows2
        sa, sc, sg = sa_both.at[half], sc_both.at[half], sg_both.at[half]
        for row in range(4):
            here = slice(base + row * ch, base + (row + 1) * ch)
            value = wx[here, :].astype(F32)
            moved = shifted(value * sigmoid(value))
            if row == 1 + half:
                act_in[half * ch : (half + 1) * ch, :] = moved[1]
            for shift in range(3):
                sa[(row * 3 + shift) * ch : (row * 3 + shift + 1) * ch, :] = moved[shift]
            moved = shifted(cx[here, :])
            for shift in range(3):
                sc[(row * 3 + shift) * ch : (row * 3 + shift + 1) * ch, :] = moved[shift]
        here = slice(base + ch, base + 3 * ch)
        act, grad = middle_step(
            w1_ref, w2f_ref, bias_ref, wx[here, :], cx[here, :], sa[...], sc[...]
        )
        inside_at = 0 if half == 0 else lax.axis_size("rows") - 1
        limit = jnp.where(lax.axis_index("rows") == inside_at, ch, 0 if half == 0 else 2 * ch)
        good = (sub >= limit) if half == 0 else (sub < limit)
        act = jnp.where(good, rim_masked(act, rim_ok, breadth), 0.0)
        grad = jnp.where(good, rim_masked(grad, rim_ok, breadth), 0.0)
        act_mid[half * rows2 : (half + 1) * rows2, :] = act.astype(BF16)
        mine = shifted(grad)
        other = shifted(near[half * rows2 : (half + 1) * rows2, :].astype(F32))
        own = mine[1][ch:] if half == 0 else mine[1][:ch]
        grads[half * ch : (half + 1) * ch, :] = own
        order = (mine, other) if half == 0 else (other, mine)
        for pair in range(2):
            for row in range(2):
                for shift in range(3):
                    out = ((pair * 2 + row) * 3 + shift) * ch
                    sg[out : out + ch, :] = order[pair][shift][row * ch : (row + 1) * ch]
        back = jnp.dot(w1f_ref[...], sg[:, core], preferred_element_type=F32)
        inside = slice(rows2, 2 * rows2) if half == 0 else slice(2 * rows2, 3 * rows2)
        value = wx[inside, core].astype(F32)
        mid = jnp.concatenate([order[0][1][ch:, core], order[1][1][:ch, core]], axis=0).astype(F32)
        gw[half * rows2 : (half + 1) * rows2, :] = (
            mid + slope_of(value, sigmoid(value)) * back
        ).astype(BF16)

    rows_to = CAP * BLOCK
    stores = [
        (act_in.at[0:ch, :], act_in_ref.at[0:ch, :]),
        (act_in.at[ch : 2 * ch, :], act_in_ref.at[body + ch : body + 2 * ch, :]),
        (act_mid.at[0:rows2, :], act_mid_ref.at[0:rows2, :]),
        (act_mid.at[rows2 : 2 * rows2, :], act_mid_ref.at[body : body + 2 * ch, :]),
        (grads.at[0:ch, :], g_ref.at[0:ch, :]),
        (grads.at[ch : 2 * ch, :], g_ref.at[body - ch : body, :]),
        (packed.at[:, :, 0:rows2], packed_ref.at[:, 0:rows_to, :]),
        (
            packed.at[:, :, rows2 : 2 * rows2],
            packed_ref.at[:, (DEPTH - 1) * rows_to : DEPTH * rows_to, :],
        ),
    ]
    stores = [
        pltpu.make_async_copy(source, target, sem_out.at[at])
        for at, (source, target) in enumerate(stores)
    ]
    for store in stores[:6]:
        store.start()
    both = (
        jnp.concatenate([gw[0:rows2, :], gw_mid_ref[0:rows2, :]], axis=0),
        jnp.concatenate([gw_mid_ref[rows2 : 2 * rows2, :], gw[rows2 : 2 * rows2, :]], axis=0),
    )

    def pack(part, _):
        rows = pl.ds(pl.multiple_of(part * size, size), size)
        total = sum(
            lax.dot_general(
                chosen[rows, band * breadth : (band + 1) * breadth],
                both[band],
                NT,
                preferred_element_type=F32,
            )
            for band in range(2)
        ).astype(BF16)
        packed[pl.ds(part * (size // rows_to), size // rows_to), :, :] = total.reshape(
            size // rows_to, rows_to, total.shape[1]
        )
        return 0

    lax.fori_loop(0, chosen.shape[0] // size, pack, 0, unroll=4)
    for store in stores[6:]:
        store.start()
    for store in stores:
        store.wait()


def outer(sizes, operands, state, slots):
    channels, height, breadth = sizes
    wide = breadth + 128
    hbm = pl.BlockSpec(memory_space=pl.ANY)
    inputs = len(operands)
    return pl.pallas_call(
        functools.partial(outer_kernel, channels, height, breadth),
        in_specs=[hbm] * (inputs + len(state)),
        out_specs=[hbm] * len(state),
        out_shape=[jax.ShapeDtypeStruct(item.shape, item.dtype) for item in state],
        input_output_aliases={inputs + at: at for at in range(len(state))},
        scratch_shapes=[
            pltpu.VMEM((8 * channels, wide), BF16),
            pltpu.VMEM((8 * channels, wide), BF16),
            pltpu.VMEM((2, 12 * channels, wide), BF16),
            pltpu.VMEM((2, 12 * channels, wide), BF16),
            pltpu.VMEM((2, 12 * channels, wide), BF16),
            pltpu.VMEM((4 * channels, wide), BF16),
            pltpu.VMEM((4 * channels, breadth), BF16),
            pltpu.VMEM((2 * channels, wide), BF16),
            pltpu.VMEM((4 * channels, wide), BF16),
            pltpu.VMEM((2 * channels, wide), BF16),
            pltpu.VMEM((slots // CAP, CAP * BLOCK, 4 * channels), BF16),
            pltpu.VMEM((slots * BLOCK, 2 * breadth), BF16),
            pltpu.VMEM((2, 16, 2 * channels), BF16),
            *[pltpu.VMEM(item.shape, item.dtype) for item in operands[4:]],
            pltpu.SemaphoreType.DMA((19,)),
            pltpu.SemaphoreType.DMA((8,)),
        ],
        compiler_params=params(),
        name="outer",
    )(*operands, *state)


def correlate_kernel(
    channels, height, breadth,
    act_in_ref, act_mid_ref, g_ref, xc_ref, out_ref,
    image1, image2, g, c, s1, s2, acc1, acc2, sum1, sum2, sem,
):
    ch = channels
    wide = breadth + 128
    core = slice(0, breadth)
    loads = [
        pltpu.make_async_copy(source, target, sem.at[at])
        for at, (source, target) in enumerate(
            ((g_ref.at[:, core], g), (xc_ref, c), (act_in_ref, image1), (act_mid_ref, image2))
        )
    ]
    for load in loads:
        load.start()
    for ref in (acc1, acc2, sum1, sum2):
        ref[...] = jnp.zeros_like(ref)
    empty = jnp.zeros((ch, wide - breadth), F32)

    def prepare(row, source, target, total):
        value = source[at_row(row, 1, ch), :].astype(F32)
        total[...] += value
        right, here, left = shifted(jnp.concatenate([value, empty], axis=1))
        for shift, moved in enumerate((left, here, right)):
            target[at_row(row * 3 + shift, 1, ch), :] = moved

    def add(pair, image, grads, acc):
        acc[...] += lax.dot_general(
            grads[at_row(pair * 6, 6, ch), :],
            image[at_row(pair * 2, 4, ch), :],
            NT,
            preferred_element_type=F32,
        )

    loads[0].wait()
    loads[1].wait()

    def step(row, _):
        prepare(row, g, s1, sum1)
        prepare(row, c, s2, sum2)
        return 0

    def products(pair, _):
        add(pair, image1, s1, acc1)
        add(pair, image2, s2, acc2)
        return 0

    lax.fori_loop(0, height, step, 0, unroll=4)
    loads[2].wait()
    loads[3].wait()
    lax.fori_loop(0, height // 2, products, 0, unroll=4)

    first, second = (
        acc[0 : 3 * ch, :] + pltpu.roll(acc[3 * ch : 6 * ch, :], 3 * ch, 1) for acc in (acc1, acc2)
    )
    second = pltpu.roll(second, ch, 1)
    low = lax.broadcasted_iota(jnp.int32, (3 * ch, 128), 1) < ch
    out_ref[0 : 3 * ch, :] = first[:, 0:128]
    out_ref[3 * ch : 6 * ch, :] = jnp.where(low, first[:, 128:256], second[:, 0:128])
    out_ref[6 * ch : 9 * ch, :] = second[:, 128:256]
    sums = jnp.concatenate(
        [jnp.sum(total[...], axis=1, keepdims=True) for total in (sum1, sum2)], axis=0
    )
    out_ref[9 * ch :, :] = jnp.broadcast_to(sums, (2 * ch, 2 * ch)).T[0:8, :]


def correlate(sizes, act_in, act_mid, g_mid, xc):
    channels, height, breadth = sizes
    wide = breadth + 128
    hbm = pl.BlockSpec(memory_space=pl.ANY)
    flops = 2 * 2 * 12 * channels * 2 * channels * breadth * (height // 2)
    return pl.pallas_call(
        functools.partial(correlate_kernel, channels, height, breadth),
        in_specs=[hbm] * 4,
        out_specs=pl.BlockSpec(memory_space=pltpu.VMEM),
        out_shape=jax.ShapeDtypeStruct((9 * channels + 8, 2 * channels), F32),
        scratch_shapes=[
            pltpu.VMEM(((height + 2) * channels, wide), BF16),
            pltpu.VMEM(((height + 2) * channels, wide), BF16),
            pltpu.VMEM((height * channels, breadth), BF16),
            pltpu.VMEM((height * channels, breadth), BF16),
            pltpu.VMEM((height * 3 * channels, wide), BF16),
            pltpu.VMEM((height * 3 * channels, wide), BF16),
            pltpu.VMEM((6 * channels, 4 * channels), F32),
            pltpu.VMEM((6 * channels, 4 * channels), F32),
            pltpu.VMEM((channels, breadth), F32),
            pltpu.VMEM((channels, breadth), F32),
            pltpu.SemaphoreType.DMA((4,)),
        ],
        compiler_params=params(),
        cost_estimate=pl.CostEstimate(flops=flops, bytes_accessed=10**7, transcendentals=0),
        name="correlate",
    )(act_in, act_mid, g_mid, xc)


def unpack_kernel(
    channels, breadth, arrived_ref, out_ref, arrived, label_rows, chosen, flat, frame, sem_in, sem_out
):
    devices = arrived.shape[0]
    halves, block_rows, part = out_ref.shape[2], out_ref.shape[1], out_ref.shape[3]
    rows_to = CAP * BLOCK
    depth = DEPTH * rows_to
    strip = depth // halves
    labels = pltpu.make_async_copy(arrived_ref.at[:, depth : depth + 16, :], label_rows, sem_in.at[0])
    labels.start()
    loads = [
        pltpu.make_async_copy(
            arrived_ref.at[:, at * strip : (at + 1) * strip, :],
            arrived.at[:, at * strip : (at + 1) * strip, :],
            sem_in.at[1 + at],
        )
        for at in range(halves)
    ]
    for load in loads:
        load.start()
    shape = (BLOCK, block_rows * breadth)
    place = lax.broadcasted_iota(jnp.int32, shape, 1) - lax.broadcasted_iota(jnp.int32, shape, 0)
    place = place.astype(F32)
    labels.wait()

    def select(source, _):
        label = label_rows[source].astype(F32) * BLOCK
        for rank in range(CAP):
            at = rank * (128 // CAP)
            hit = (place == label[:, at : at + 1]).astype(F32).astype(BF16)
            row = pl.multiple_of(source * rows_to + rank * BLOCK, BLOCK)
            chosen[pl.ds(row, BLOCK), :] = hit
        return 0

    lax.fori_loop(0, devices, select, 0, unroll=4)
    stores = []
    for half in range(halves):
        loads[half].wait()
        for at in range(strip // rows_to):
            row = half * strip + at * rows_to
            tile = arrived[:, row : row + rows_to, :]
            flat[at * 128 : (at + 1) * 128, :] = tile.reshape(devices * rows_to, 128).T
        for band in range(block_rows):
            summed = jnp.dot(
                flat[...], chosen[:, band * breadth : (band + 1) * breadth], preferred_element_type=F32
            )
            slot = half * block_rows + band
            frame[slot] = jnp.swapaxes(summed.reshape(part, channels, breadth), 0, 1)
            stores.append(
                pltpu.make_async_copy(frame.at[slot], out_ref.at[:, band, half], sem_out.at[slot])
            )
            stores[-1].start()
    for store in stores:
        store.wait()


def unpack(sizes, arrived):
    channels, height, breadth = sizes
    block_rows = height // BLOCK
    devices = arrived.shape[0]
    rows_to = CAP * BLOCK
    part = 8
    halves = BLOCK // part
    hbm = pl.BlockSpec(memory_space=pl.ANY)
    return pl.pallas_call(
        functools.partial(unpack_kernel, channels, breadth),
        in_specs=[hbm],
        out_specs=hbm,
        out_shape=jax.ShapeDtypeStruct((channels, block_rows, halves, part, breadth), F32),
        scratch_shapes=[
            pltpu.VMEM((devices, DEPTH * rows_to, 128), BF16),
            pltpu.VMEM((devices, 16, 128), BF16),
            pltpu.VMEM((devices * rows_to, block_rows * breadth), BF16),
            pltpu.VMEM((part * channels, devices * rows_to), BF16),
            pltpu.VMEM((halves * block_rows, channels, part, breadth), F32),
            pltpu.SemaphoreType.DMA((1 + halves,)),
            pltpu.SemaphoreType.DMA((halves * block_rows,)),
        ],
        compiler_params=params(),
        name="unpack",
    )(arrived)


def shift_pairs(axis, step):
    count = lax.axis_size(axis)
    return [(i, i + step) for i in range(count) if 0 <= i + step < count]


def finish_kernel(channels, factor, total_ref, other_ref, w1_ref, w2_ref, b1_ref, b2_ref, terms):
    ch = channels
    half = total_ref.shape[0]
    bit = lax.rem(lax.axis_index("rows") * lax.axis_size("cols") + lax.axis_index("cols"), 2)
    terms[pl.ds(pl.multiple_of(bit * half, 8), half), :] = total_ref[...] * factor
    terms[pl.ds(pl.multiple_of((1 - bit) * half, 8), half), :] = other_ref[...] * factor
    tile = lambda at: terms[at * 3 * ch : (at + 1) * 3 * ch, :]
    for out, parts in ((w1_ref, ((0, 0), (0, 1), (1, 0))), (w2_ref, ((1, 1), (2, 0), (2, 1)))):
        for row, (at, side) in enumerate(parts):
            value = pltpu.roll(tile(at), ch, 1) if side else tile(at)
            for col in range(3):
                out[row, col] = value[col * ch : (col + 1) * ch, 0:ch]
    bias = terms[9 * ch : 9 * ch + 8, :]
    b1_ref[...] = bias[0:1, 0:ch]
    b2_ref[...] = pltpu.roll(bias, ch, 1)[0:1, 0:ch]


def finish(channels, factor, total, other):
    vmem = pl.BlockSpec(memory_space=pltpu.VMEM)
    kernel = jax.ShapeDtypeStruct((3, 3, channels, channels), F32)
    bias = jax.ShapeDtypeStruct((1, channels), F32)
    w1, w2, b1, b2 = pl.pallas_call(
        functools.partial(finish_kernel, channels, factor),
        in_specs=[vmem, vmem],
        out_specs=[vmem] * 4,
        out_shape=[kernel, kernel, bias, bias],
        scratch_shapes=[pltpu.VMEM((2 * total.shape[0], 128), F32)],
        compiler_params=params(),
        name="finish",
    )(total, other)
    order = (2, 3, 0, 1)
    return jnp.transpose(w1, order), b1[0], jnp.transpose(w2, order), b2[0]


def total_over_devices(terms, devices, arrived, frame_of):
    me = lax.axis_index(AXES)
    swap = lambda value, step: lax.ppermute(value, AXES, [(i, i ^ step) for i in range(devices)])
    bit = me % 2
    half = terms.shape[0] // 2
    mine = lax.dynamic_slice_in_dim(terms, bit * half, half, 0)
    away = lax.dynamic_slice_in_dim(terms, (1 - bit) * half, half, 0)
    total = mine + swap(away, 1)
    step = 2
    while 2 * step < devices:
        total = total + swap(total, step)
        step *= 2
    total, arrived = lax.optimization_barrier((total, arrived))
    other = swap(total, step)
    frame = frame_of(arrived)
    other, frame = lax.optimization_barrier((other, frame))
    total = total + other
    return total, swap(total, 1), frame


def body(warped, cotangent, w_first, b_first, w_second, source_tile, source_block):
    sizes = warped.shape
    channels, height, breadth = sizes
    row_count = lax.axis_size("rows")
    col_count = lax.axis_size("cols")
    devices = row_count * col_count
    slots = devices * CAP
    factor = 1.0 / math.sqrt(height * row_count * breadth * col_count)
    me = lax.axis_index(AXES)

    block_rows = height // BLOCK
    count = source_tile.size
    target = source_tile.reshape(count)
    same = target[:, None] == target[None, :]
    earlier = jnp.arange(count)[None, :] < jnp.arange(count)[:, None]
    ranking = jnp.sum((same & earlier).astype(jnp.int32), axis=1)
    places = target * CAP + ranking
    target_row = (
        places.reshape(block_rows, -1, 1) * BLOCK + jnp.arange(BLOCK, dtype=jnp.int32)
    ).reshape(block_rows, breadth)
    hits = places[:, None] == jnp.arange(slots, dtype=jnp.int32)[None, :]
    labels = jnp.sum(jnp.where(hits, source_block.reshape(count, 1) + 1, 0), axis=0) - 1
    xw, xc, to_right, to_left, to_up, to_down, first, second_back, first_back, bias = reorder(
        warped, cotangent, w_first, w_second, b_first
    )
    rim = 2 * channels
    side = lax.ppermute(to_right, "cols", shift_pairs("cols", 1)) + lax.ppermute(
        to_left, "cols", shift_pairs("cols", -1)
    )
    to_down = lax.dynamic_update_slice(to_down, side[:, -rim:], (2 * rim, 0))
    to_up = lax.dynamic_update_slice(to_up, side[:, :rim], (2 * rim, 0))
    up = lax.ppermute(to_down, "rows", shift_pairs("rows", 1))
    down = lax.ppermute(to_up, "rows", shift_pairs("rows", -1))

    *state, gw_mid = inner(
        sizes, (xw, xc, side, first, second_back, first_back, bias, target_row, labels), slots
    )
    packed, act_in, act_mid, g_mid = outer(
        sizes,
        (
            xw, xc, up, down, side,
            first, second_back, first_back, bias, target_row, gw_mid,
        ),
        state,
        slots,
    )
    arrived = lax.all_to_all(packed, AXES, split_axis=0, concat_axis=0, tiled=True)

    terms = correlate(sizes, act_in, act_mid, g_mid, xc)
    fill = jnp.zeros((-terms.shape[0] % 16, 128), F32)
    total, other, frame = total_over_devices(
        jnp.concatenate([terms, fill], axis=0),
        devices,
        arrived,
        functools.partial(unpack, sizes),
    )
    return (frame.reshape(sizes), *finish(channels, factor, total, other))


def solution(mesh):
    in_specs = (
        P(None, "rows", "cols"),
        P(None, "rows", "cols"),
        P(),
        P(),
        P(),
        P("rows", "cols"),
        P("rows", "cols"),
    )
    out_specs = (P(None, "rows", "cols"), P(), P(), P(), P())
    return jax.shard_map(body, mesh=mesh, in_specs=in_specs, out_specs=out_specs, check_vma=False)
```

```python
import functools
import math

import jax
import jax.numpy as jnp
from jax import lax
from jax.experimental import pallas as pl
from jax.experimental.pallas import tpu as pltpu
from jax.sharding import PartitionSpec as P

BLOCK = 16
CAP = 2
AXES = ("rows", "cols")
BF16 = jnp.bfloat16
F32 = jnp.float32
NT = (((1,), (1,)), ((), ()))
TN = (((0,), (0,)), ((), ()))
VMEM_BYTES = 63 * 2**20


def params(**extra):
    return pltpu.CompilerParams(vmem_limit_bytes=VMEM_BYTES, **extra)


def sigmoid(value):
    return 0.5 * jnp.tanh(0.5 * value) + 0.5


def one_hot(shape, pairs):
    row = lax.broadcasted_iota(jnp.int32, shape, 0)
    col = lax.broadcasted_iota(jnp.int32, shape, 1)
    hit = jnp.zeros(shape, jnp.bool_)
    for at_row, at_col in pairs:
        hit = hit | ((row == at_row) & (col == at_col))
    return hit.astype(F32).astype(BF16)


def shifted(value):
    value = value.astype(BF16)
    return pltpu.roll(value, 1, 1), value, pltpu.roll(value, value.shape[1] - 1, 1)


def slope_of(value, sigma):
    return sigma + value * sigma * (1.0 - sigma)


def at_row(row, rows, channels):
    return pl.ds(pl.multiple_of(row * channels, channels), rows * channels)


def pair_weights(taps_ref, out_ref, flip):
    ch = taps_ref.shape[2]
    out_ref[...] = jnp.zeros_like(out_ref)
    for row in range(3):
        for col in range(3):
            if flip:
                tap = taps_ref[2 - row, 2 - col].astype(F32).T.astype(BF16)
            else:
                tap = taps_ref[row, col]
            at = (row * 3 + col) * ch
            out_ref[0:ch, at : at + ch] = tap
            out_ref[ch : 2 * ch, at + 3 * ch : at + 4 * ch] = tap


def reorder_kernel(
    w_ref, c_ref, first_ref, second_ref, b_ref,
    xw_ref, xc_ref, to_right_ref, to_left_ref, to_up_ref, to_down_ref,
    w1_ref, w2f_ref, w1f_ref, bias_ref,
):
    channels, rows, lanes = w_ref.shape

    @pl.when((pl.program_id(0) == 0) & (pl.program_id(1) == 1))
    def _():
        pair_weights(first_ref, w1_ref, False)
        pair_weights(second_ref, w2f_ref, True)
        pair_weights(first_ref, w1f_ref, True)
        column = jnp.broadcast_to(b_ref[...], (2 * channels, channels)).T
        bias_ref[0:channels, :] = column
        bias_ref[channels:, :] = column

    rim = 2 * channels
    kept = []
    for source, target in ((w_ref, xw_ref), (c_ref, xc_ref)):
        value = source[...].astype(F32)
        swapped = jnp.swapaxes(value, 0, 1).reshape(rows * channels, lanes).astype(BF16)
        target[...] = swapped
        kept.append(swapped)

    @pl.when(pl.program_id(1) == 0)
    def _():
        to_up_ref[0:rim, :] = kept[0][0:rim]
        to_up_ref[rim : 2 * rim, :] = kept[1][0:rim]
        to_up_ref[2 * rim :, :] = jnp.zeros((16, lanes), BF16)

    @pl.when(pl.program_id(1) == pl.num_programs(1) - 1)
    def _():
        to_down_ref[0:rim, :] = kept[0][rows * channels - rim :]
        to_down_ref[rim : 2 * rim, :] = kept[1][rows * channels - rim :]
        to_down_ref[2 * rim :, :] = jnp.zeros((16, lanes), BF16)

    here = pl.ds(pl.multiple_of(pl.program_id(1) * rows * channels, 128), rows * channels)

    def pick(tile, w_pairs, c_pairs):
        return sum(
            lax.dot_general(
                one_hot((16, 128), pairs), value[:, tile], NT, preferred_element_type=F32
            )
            for value, pairs in zip(kept, (w_pairs, c_pairs))
        ).astype(BF16)

    @pl.when(pl.program_id(0) == pl.num_programs(0) - 1)
    def _():
        final = slice(lanes - 128, lanes)
        to_right_ref[:, here] = pick(final, ((0, 126), (1, 127)), ((2, 126), (3, 127)))

    @pl.when(pl.program_id(0) == 0)
    def _():
        to_left_ref[:, here] = pick(slice(0, 128), ((4, 0), (5, 1)), ((6, 0), (7, 1)))


def reorder(warped, cotangent, w_first, w_second, b_first):
    channels, height, breadth = warped.shape
    whole = lambda shape: pl.BlockSpec(shape, lambda x, h: (0,) * len(shape))
    step = 16
    lanes = breadth
    spec_in = pl.BlockSpec((channels, step, lanes), lambda x, h: (0, h, x))
    spec_out = pl.BlockSpec((step * channels, lanes), lambda x, h: (h, x))
    spec_edge = pl.BlockSpec((16, height * channels), lambda x, h: (0, 0))
    spec_rim = pl.BlockSpec((4 * channels + 16, lanes), lambda x, h: (0, x))
    shape = jax.ShapeDtypeStruct((height * channels, breadth), BF16)
    edge = jax.ShapeDtypeStruct((16, height * channels), BF16)
    rim = jax.ShapeDtypeStruct((4 * channels + 16, breadth), BF16)
    weights = jax.ShapeDtypeStruct((2 * channels, 12 * channels), BF16)
    bias = jax.ShapeDtypeStruct((2 * channels, 2 * channels), F32)
    return pl.pallas_call(
        reorder_kernel,
        grid=(breadth // lanes, height // step),
        in_specs=[spec_in, spec_in]
        + [whole(w_first.shape[2:] + w_first.shape[:2])] * 2
        + [whole((1, channels))],
        out_specs=[spec_out, spec_out, spec_edge, spec_edge, spec_rim, spec_rim]
        + [whole(weights.shape)] * 3
        + [whole(bias.shape)],
        out_shape=[shape, shape, edge, edge, rim, rim, weights, weights, weights, bias],
        compiler_params=params(),
        name="reorder",
    )(
        warped,
        cotangent,
        jnp.transpose(w_first, (2, 3, 0, 1)),
        jnp.transpose(w_second, (2, 3, 0, 1)),
        b_first[None, :],
    )


def spread_sides(side, first):
    spread = one_hot((16, 128), ((first, 126), (first + 1, 127), (first + 4, 0), (first + 5, 1)))
    return lax.dot_general(side, spread, TN, preferred_element_type=F32).astype(BF16)


def rim_mask(channels):
    lane = lax.broadcasted_iota(jnp.int32, (2 * channels, 128), 1)
    col = lax.axis_index("cols")
    right = jnp.where(col < lax.axis_size("cols") - 1, 0, -1)
    left = jnp.where(col > 0, 127, -1)
    return (lane == right) | (lane == left)


def middle_step(w1_ref, w2f_ref, bias_ref, value, cot, act_window, cot_window):
    conv = jnp.dot(w1_ref[...], act_window, preferred_element_type=F32)
    back = jnp.dot(w2f_ref[...], cot_window, preferred_element_type=F32)
    a_mid = (value.astype(F32) + conv + bias_ref[:, 0:1]).astype(BF16).astype(F32)
    sigma = sigmoid(a_mid)
    return a_mid * sigma, cot.astype(F32) + slope_of(a_mid, sigma) * back


def rim_masked(value, rim_ok, breadth):
    return jnp.concatenate(
        [value[:, :breadth], jnp.where(rim_ok, value[:, breadth:], 0.0)], axis=1
    )


def chosen_blocks(target_ref, band, start, size, breadth):
    row_at = lax.broadcasted_iota(jnp.int32, (size, breadth), 0) + start
    return (row_at == target_ref[band : band + 1, :]).astype(F32).astype(BF16)


def inner_kernel(
    channels, height, breadth,
    xw_ref, xc_ref, side_ref, w1_ref, w2f_ref, w1f_ref, bias_ref, target_ref, label_ref,
    packed_ref, act_in_ref, act_mid_ref, g_ref, gw_mid_ref,
    wx, cx, sa, sc, sg, gw, act_in, act_mid, grads, packed, label_rows, sem_in, sem_out,
):
    ch = channels
    wide = breadth + 128
    core = slice(0, breadth)
    rim = slice(breadth, wide)
    step = height * ch // 4
    loads = [
        pltpu.make_async_copy(
            source.at[at * step : (at + 1) * step, :],
            target.at[at * step : (at + 1) * step, core],
            sem_in.at[2 * at + which],
        )
        for at in range(4)
        for which, (source, target) in enumerate(((xw_ref, wx), (xc_ref, cx)))
    ]
    stores = [
        pltpu.make_async_copy(act_in, act_in_ref.at[ch : ch + height * ch, :], sem_out.at[0]),
        pltpu.make_async_copy(act_mid, act_mid_ref.at[2 * ch : height * ch, :], sem_out.at[1]),
        pltpu.make_async_copy(grads, g_ref.at[ch : (height - 1) * ch, :], sem_out.at[2]),
        pltpu.make_async_copy(
            label_rows, packed_ref.at[:, DEPTH * CAP * BLOCK : DEPTH * CAP * BLOCK + 16, :], sem_out.at[3]
        ),
        pltpu.make_async_copy(
            gw.at[(BLOCK - 2) * ch : (BLOCK + 2) * ch, :], gw_mid_ref, sem_out.at[4]
        ),
    ]
    for load in loads:
        load.start()
    upper = lax.broadcasted_iota(jnp.int32, (16, 128), 1) >= 128 // CAP

    def label(device, _):
        owner = jnp.where(upper, label_ref[device * CAP + 1], label_ref[device * CAP])
        label_rows[device] = owner.astype(F32).astype(BF16)
        return 0

    lax.fori_loop(0, label_rows.shape[0], label, 0, unroll=4)
    stores[3].start()
    wx[:, rim] = spread_sides(side_ref[...], 0)
    cx[:, rim] = spread_sides(side_ref[...], 2)

    def prepare(row, _):
        here = at_row(row, 1, ch)
        out = pl.multiple_of(row * 3 * ch, ch)
        value = wx[here, :].astype(F32)
        moved = shifted(value * sigmoid(value))
        act_in[here, :] = moved[1]
        for shift in range(3):
            sa[pl.ds(out + shift * ch, ch), :] = moved[shift]
        moved = shifted(cx[here, :])
        for shift in range(3):
            sc[pl.ds(out + shift * ch, ch), :] = moved[shift]
        return 0

    rim_ok = rim_mask(ch)

    def middle(pair, _):
        row = pair * 2
        window = at_row(row * 3, 12, ch)
        here = at_row(row + 1, 2, ch)
        act, grad = middle_step(
            w1_ref, w2f_ref, bias_ref, wx[here, :], cx[here, :], sa[window, :], sc[window, :]
        )
        out = at_row(row, 2, ch)
        act_mid[out, :] = rim_masked(act, rim_ok, breadth).astype(BF16)
        moved = shifted(rim_masked(grad, rim_ok, breadth))
        grads[out, :] = moved[1]
        for shift in range(3):
            sg[at_row(row * 3 + shift, 1, ch), :] = moved[shift][:ch]
            sg[at_row(row * 3 + 3 + shift, 1, ch), :] = moved[shift][ch:]
        return 0

    quarter = height // 4
    done = 0
    for at in range(4):
        loads[2 * at].wait()
        loads[2 * at + 1].wait()
        lax.fori_loop(at * quarter, (at + 1) * quarter, prepare, 0, unroll=UNROLL_PREPARE)
        if at == 3:
            stores[0].start()
        ready = (at + 1) * quarter // 2 - 1
        lax.fori_loop(done, ready, middle, 0, unroll=True)
        done = ready
    stores[1].start()
    stores[2].start()

    def last(pair, _):
        row = pair * 2
        back = jnp.dot(w1f_ref[...], sg[at_row(row * 3, 12, ch), core], preferred_element_type=F32)
        here = at_row(row + 2, 2, ch)
        value = wx[here, core].astype(F32)
        mid = grads[at_row(row + 1, 2, ch), core].astype(F32)
        gw[here, :] = (mid + slope_of(value, sigmoid(value)) * back).astype(BF16)
        return 0

    lax.fori_loop(0, height // 2 - 2, last, 0, unroll=UNROLL_LAST)
    stores[4].start()

    size = 256
    strip = BLOCK * ch

    def pack(part, _):
        start = pl.multiple_of(part * size, size)
        total = None
        for band in range(height // BLOCK):
            chosen = chosen_blocks(target_ref, band, start, size, breadth)
            rows = slice(band * strip + 2 * ch, (band + 1) * strip - 2 * ch)
            term = lax.dot_general(chosen, gw[rows, :], NT, preferred_element_type=F32)
            total = term if total is None else total + term
        total = total.astype(BF16).reshape(size // rows_to, rows_to, total.shape[1])
        packed[pl.ds(part * (size // rows_to), size // rows_to), :, :] = total
        return 0

    rows_to = CAP * BLOCK
    lax.fori_loop(0, packed.shape[0] * rows_to // size, pack, 0, unroll=4)
    for at in range(1, DEPTH - 1):
        stores.append(
            pltpu.make_async_copy(
                packed.at[:, :, (at - 1) * 128 : at * 128],
                packed_ref.at[:, at * rows_to : (at + 1) * rows_to, :],
                sem_out.at[4 + at],
            )
        )
        stores[-1].start()
    for store in stores:
        store.wait()


DEPTH = 8
UNROLL_PREPARE = 8
UNROLL_MIDDLE = 5
UNROLL_LAST = 14


def inner(sizes, operands, slots):
    channels, height, breadth = sizes
    wide = breadth + 128
    vmem = pl.BlockSpec(memory_space=pltpu.VMEM)
    hbm = pl.BlockSpec(memory_space=pl.ANY)
    outs = [
        jax.ShapeDtypeStruct((slots // CAP, DEPTH * CAP * BLOCK + 16, 128), BF16),
        jax.ShapeDtypeStruct(((height + 2) * channels, wide), BF16),
        jax.ShapeDtypeStruct(((height + 2) * channels, wide), BF16),
        jax.ShapeDtypeStruct((height * channels, wide), BF16),
        jax.ShapeDtypeStruct((4 * channels, breadth), BF16),
    ]
    flops = 2 * 3 * 12 * channels * 2 * channels * wide * (height // 2)
    return pl.pallas_call(
        functools.partial(inner_kernel, channels, height, breadth),
        in_specs=[hbm, hbm]
        + [vmem] * (len(operands) - 3)
        + [pl.BlockSpec(memory_space=pltpu.SMEM)],
        out_specs=[hbm] * len(outs),
        out_shape=outs,
        scratch_shapes=[
            pltpu.VMEM((height * channels, wide), BF16),
            pltpu.VMEM((height * channels, wide), BF16),
            pltpu.VMEM((height * 3 * channels, wide), BF16),
            pltpu.VMEM((height * 3 * channels, wide), BF16),
            pltpu.VMEM(((height - 2) * 3 * channels, wide), BF16),
            pltpu.VMEM((height * channels, breadth), BF16),
            pltpu.VMEM((height * channels, wide), BF16),
            pltpu.VMEM(((height - 2) * channels, wide), BF16),
            pltpu.VMEM(((height - 2) * channels, wide), BF16),
            pltpu.VMEM((slots // CAP, CAP * BLOCK, (BLOCK - 4) * channels), BF16),
            pltpu.VMEM((slots // CAP, 16, 128), BF16),
            pltpu.SemaphoreType.DMA((8,)),
            pltpu.SemaphoreType.DMA((3 + DEPTH,)),
        ],
        compiler_params=params(),
        cost_estimate=pl.CostEstimate(flops=flops, bytes_accessed=2 * 10**7, transcendentals=10**6),
        name="inner",
    )(*operands)


def outer_kernel(
    channels, height, breadth,
    xw_ref, xc_ref, up_ref, down_ref, side_hbm,
    w1_hbm, w2f_hbm, w1f_hbm, bias_hbm, target_hbm, gw_mid_hbm,
    packed_in, act_in_in, act_mid_in, g_in,
    packed_ref, act_in_ref, act_mid_ref, g_ref,
    wx, cx, sa_both, sc_both, sg_both, near, gw, act_in, act_mid, grads, packed, chosen, corner,
    side_ref, w1_ref, w2f_ref, w1f_ref, bias_ref, target_ref, gw_mid_ref, sem_in, sem_out,
):
    ch = channels
    wide = breadth + 128
    core = slice(0, breadth)
    rim = slice(breadth, wide)
    body = height * ch
    rows2 = 2 * ch
    loads = []

    def load(source, target):
        copy = pltpu.make_async_copy(source, target, sem_in.at[len(loads)])
        copy.start()
        loads.append(copy)

    load(target_hbm, target_ref)
    load(side_hbm, side_ref)
    load(up_ref.at[2 * rows2 : 2 * rows2 + 16, 0:rows2], corner.at[0])
    load(down_ref.at[2 * rows2 : 2 * rows2 + 16, 0:rows2], corner.at[1])
    load(xw_ref.at[0:rows2, :], wx.at[rows2 : 2 * rows2, core])
    load(xc_ref.at[0:rows2, :], cx.at[rows2 : 2 * rows2, core])
    load(xw_ref.at[body - rows2 : body, :], wx.at[2 * rows2 : 3 * rows2, core])
    load(xc_ref.at[body - rows2 : body, :], cx.at[2 * rows2 : 3 * rows2, core])
    load(up_ref.at[0:rows2, :], wx.at[0:rows2, core])
    load(up_ref.at[rows2 : 2 * rows2, :], cx.at[0:rows2, core])
    load(down_ref.at[0:rows2, :], wx.at[3 * rows2 : 4 * rows2, core])
    load(down_ref.at[rows2 : 2 * rows2, :], cx.at[3 * rows2 : 4 * rows2, core])
    load(g_in.at[ch : 3 * ch, :], near.at[0:rows2, :])
    load(g_in.at[body - 3 * ch : body - ch, :], near.at[rows2 : 2 * rows2, :])
    load(w1_hbm, w1_ref)
    load(w2f_hbm, w2f_ref)
    load(bias_hbm, bias_ref)
    load(w1f_hbm, w1f_ref)
    load(gw_mid_hbm, gw_mid_ref)
    loads[0].wait()
    loads[1].wait()
    for target, first in ((wx, 0), (cx, 2)):
        target[rows2 : 2 * rows2, rim] = spread_sides(side_ref[:, 0:rows2], first)
        target[2 * rows2 : 3 * rows2, rim] = spread_sides(side_ref[:, body - rows2 : body], first)
    size = 256

    def choose(part, _):
        start = pl.multiple_of(part * size, size)
        for band in range(2):
            chosen[pl.ds(start, size), band * breadth : (band + 1) * breadth] = chosen_blocks(
                target_ref, band, start, size, breadth
            )
        return 0

    lax.fori_loop(0, chosen.shape[0] // size, choose, 0, unroll=4)
    for copy in loads[2:]:
        copy.wait()
    for target, first in ((wx, 0), (cx, 2)):
        target[0:rows2, rim] = spread_sides(corner[0], first)
        target[3 * rows2 : 4 * rows2, rim] = spread_sides(corner[1], first)
    rim_ok = rim_mask(ch)
    sub = lax.broadcasted_iota(jnp.int32, (2 * ch, wide), 0)

    for half in range(2):
        base = half * 2 * rows2
        sa, sc, sg = sa_both.at[half], sc_both.at[half], sg_both.at[half]
        for row in range(4):
            here = slice(base + row * ch, base + (row + 1) * ch)
            value = wx[here, :].astype(F32)
            moved = shifted(value * sigmoid(value))
            if row == 1 + half:
                act_in[half * ch : (half + 1) * ch, :] = moved[1]
            for shift in range(3):
                sa[(row * 3 + shift) * ch : (row * 3 + shift + 1) * ch, :] = moved[shift]
            moved = shifted(cx[here, :])
            for shift in range(3):
                sc[(row * 3 + shift) * ch : (row * 3 + shift + 1) * ch, :] = moved[shift]
        here = slice(base + ch, base + 3 * ch)
        act, grad = middle_step(
            w1_ref, w2f_ref, bias_ref, wx[here, :], cx[here, :], sa[...], sc[...]
        )
        inside_at = 0 if half == 0 else lax.axis_size("rows") - 1
        limit = jnp.where(lax.axis_index("rows") == inside_at, ch, 0 if half == 0 else 2 * ch)
        good = (sub >= limit) if half == 0 else (sub < limit)
        act = jnp.where(good, rim_masked(act, rim_ok, breadth), 0.0)
        grad = jnp.where(good, rim_masked(grad, rim_ok, breadth), 0.0)
        act_mid[half * rows2 : (half + 1) * rows2, :] = act.astype(BF16)
        mine = shifted(grad)
        other = shifted(near[half * rows2 : (half + 1) * rows2, :].astype(F32))
        own = mine[1][ch:] if half == 0 else mine[1][:ch]
        grads[half * ch : (half + 1) * ch, :] = own
        order = (mine, other) if half == 0 else (other, mine)
        for pair in range(2):
            for row in range(2):
                for shift in range(3):
                    out = ((pair * 2 + row) * 3 + shift) * ch
                    sg[out : out + ch, :] = order[pair][shift][row * ch : (row + 1) * ch]
        back = jnp.dot(w1f_ref[...], sg[:, core], preferred_element_type=F32)
        inside = slice(rows2, 2 * rows2) if half == 0 else slice(2 * rows2, 3 * rows2)
        value = wx[inside, core].astype(F32)
        mid = jnp.concatenate([order[0][1][ch:, core], order[1][1][:ch, core]], axis=0).astype(F32)
        gw[half * rows2 : (half + 1) * rows2, :] = (
            mid + slope_of(value, sigmoid(value)) * back
        ).astype(BF16)

    rows_to = CAP * BLOCK
    stores = [
        (act_in.at[0:ch, :], act_in_ref.at[0:ch, :]),
        (act_in.at[ch : 2 * ch, :], act_in_ref.at[body + ch : body + 2 * ch, :]),
        (act_mid.at[0:rows2, :], act_mid_ref.at[0:rows2, :]),
        (act_mid.at[rows2 : 2 * rows2, :], act_mid_ref.at[body : body + 2 * ch, :]),
        (grads.at[0:ch, :], g_ref.at[0:ch, :]),
        (grads.at[ch : 2 * ch, :], g_ref.at[body - ch : body, :]),
    ]
    stores = [
        pltpu.make_async_copy(source, target, sem_out.at[at])
        for at, (source, target) in enumerate(stores)
    ]
    for store in stores:
        store.start()
    both = (
        jnp.concatenate([gw[0:rows2, :], gw_mid_ref[0:rows2, :]], axis=0),
        jnp.concatenate([gw_mid_ref[rows2 : 2 * rows2, :], gw[rows2 : 2 * rows2, :]], axis=0),
    )

    def pack(part, _):
        rows = slice(part * size, (part + 1) * size)
        total = sum(
            lax.dot_general(
                chosen[rows, band * breadth : (band + 1) * breadth],
                both[band],
                NT,
                preferred_element_type=F32,
            )
            for band in range(2)
        ).astype(BF16)
        packed[pl.ds(part * (size // rows_to), size // rows_to), :, :] = total.reshape(
            size // rows_to, rows_to, total.shape[1]
        )
        return 0

    group = size // rows_to
    for part in range(packed.shape[0] // group):
        pack(part, 0)
        devices = slice(part * group, (part + 1) * group)
        for at, tile in enumerate((0, DEPTH - 1)):
            stores.append(
                pltpu.make_async_copy(
                    packed.at[devices, :, at * rows2 : (at + 1) * rows2],
                    packed_ref.at[devices, tile * rows_to : (tile + 1) * rows_to, :],
                    sem_out.at[len(stores)],
                )
            )
            stores[-1].start()
    for store in stores:
        store.wait()


def outer(sizes, operands, state, slots):
    channels, height, breadth = sizes
    wide = breadth + 128
    hbm = pl.BlockSpec(memory_space=pl.ANY)
    inputs = len(operands)
    return pl.pallas_call(
        functools.partial(outer_kernel, channels, height, breadth),
        in_specs=[hbm] * (inputs + len(state)),
        out_specs=[hbm] * len(state),
        out_shape=[jax.ShapeDtypeStruct(item.shape, item.dtype) for item in state],
        input_output_aliases={inputs + at: at for at in range(len(state))},
        scratch_shapes=[
            pltpu.VMEM((8 * channels, wide), BF16),
            pltpu.VMEM((8 * channels, wide), BF16),
            pltpu.VMEM((2, 12 * channels, wide), BF16),
            pltpu.VMEM((2, 12 * channels, wide), BF16),
            pltpu.VMEM((2, 12 * channels, wide), BF16),
            pltpu.VMEM((4 * channels, wide), BF16),
            pltpu.VMEM((4 * channels, breadth), BF16),
            pltpu.VMEM((2 * channels, wide), BF16),
            pltpu.VMEM((4 * channels, wide), BF16),
            pltpu.VMEM((2 * channels, wide), BF16),
            pltpu.VMEM((slots // CAP, CAP * BLOCK, 4 * channels), BF16),
            pltpu.VMEM((slots * BLOCK, 2 * breadth), BF16),
            pltpu.VMEM((2, 16, 2 * channels), BF16),
            *[pltpu.VMEM(item.shape, item.dtype) for item in operands[4:]],
            pltpu.SemaphoreType.DMA((19,)),
            pltpu.SemaphoreType.DMA((6 + 2 * slots * BLOCK // 256,)),
        ],
        compiler_params=params(),
        name="outer",
    )(*operands, *state)


def correlate_kernel(
    channels, height, breadth,
    act_in_ref, act_mid_ref, g_ref, xc_ref, out_ref,
    image1, image2, g, c, s1, s2, acc1, acc2, sum1, sum2, sem,
):
    ch = channels
    wide = breadth + 128
    core = slice(0, breadth)
    loads = [
        pltpu.make_async_copy(source, target, sem.at[at])
        for at, (source, target) in enumerate(
            ((g_ref.at[:, core], g), (xc_ref, c), (act_in_ref, image1), (act_mid_ref, image2))
        )
    ]
    for load in loads:
        load.start()
    for ref in (acc1, acc2, sum1, sum2):
        ref[...] = jnp.zeros_like(ref)
    empty = jnp.zeros((ch, wide - breadth), F32)

    def prepare(row, source, target, total):
        value = source[at_row(row, 1, ch), :].astype(F32)
        total[...] += value
        right, here, left = shifted(jnp.concatenate([value, empty], axis=1))
        for shift, moved in enumerate((left, here, right)):
            target[at_row(row * 3 + shift, 1, ch), :] = moved

    def add(pair, image, grads, acc):
        acc[...] += lax.dot_general(
            grads[at_row(pair * 6, 6, ch), :],
            image[at_row(pair * 2, 4, ch), :],
            NT,
            preferred_element_type=F32,
        )

    loads[0].wait()
    loads[1].wait()

    def step(row, _):
        prepare(row, g, s1, sum1)
        prepare(row, c, s2, sum2)
        return 0

    def products(pair, _):
        add(pair, image1, s1, acc1)
        add(pair, image2, s2, acc2)
        return 0

    lax.fori_loop(0, height, step, 0, unroll=4)
    loads[2].wait()
    loads[3].wait()
    lax.fori_loop(0, height // 2, products, 0, unroll=4)

    first, second = (
        acc[0 : 3 * ch, :] + pltpu.roll(acc[3 * ch : 6 * ch, :], 3 * ch, 1) for acc in (acc1, acc2)
    )
    second = pltpu.roll(second, ch, 1)
    low = lax.broadcasted_iota(jnp.int32, (3 * ch, 128), 1) < ch
    out_ref[0 : 3 * ch, :] = first[:, 0:128]
    out_ref[3 * ch : 6 * ch, :] = jnp.where(low, first[:, 128:256], second[:, 0:128])
    out_ref[6 * ch : 9 * ch, :] = second[:, 128:256]
    sums = jnp.concatenate(
        [jnp.sum(total[...], axis=1, keepdims=True) for total in (sum1, sum2)], axis=0
    )
    out_ref[9 * ch :, :] = jnp.broadcast_to(sums, (2 * ch, 2 * ch)).T[0:8, :]


def correlate(sizes, act_in, act_mid, g_mid, xc):
    channels, height, breadth = sizes
    wide = breadth + 128
    hbm = pl.BlockSpec(memory_space=pl.ANY)
    flops = 2 * 2 * 12 * channels * 2 * channels * breadth * (height // 2)
    return pl.pallas_call(
        functools.partial(correlate_kernel, channels, height, breadth),
        in_specs=[hbm] * 4,
        out_specs=pl.BlockSpec(memory_space=pltpu.VMEM),
        out_shape=jax.ShapeDtypeStruct((9 * channels + 8, 2 * channels), F32),
        scratch_shapes=[
            pltpu.VMEM(((height + 2) * channels, wide), BF16),
            pltpu.VMEM(((height + 2) * channels, wide), BF16),
            pltpu.VMEM((height * channels, breadth), BF16),
            pltpu.VMEM((height * channels, breadth), BF16),
            pltpu.VMEM((height * 3 * channels, wide), BF16),
            pltpu.VMEM((height * 3 * channels, wide), BF16),
            pltpu.VMEM((6 * channels, 4 * channels), F32),
            pltpu.VMEM((6 * channels, 4 * channels), F32),
            pltpu.VMEM((channels, breadth), F32),
            pltpu.VMEM((channels, breadth), F32),
            pltpu.SemaphoreType.DMA((4,)),
        ],
        compiler_params=params(),
        cost_estimate=pl.CostEstimate(flops=flops, bytes_accessed=10**7, transcendentals=0),
        name="correlate",
    )(act_in, act_mid, g_mid, xc)


def unpack_kernel(
    channels, breadth, arrived_ref, out_ref, arrived, label_rows, chosen, flat, frame, sem_in, sem_out
):
    devices = arrived.shape[0]
    halves, block_rows, part = out_ref.shape[2], out_ref.shape[1], out_ref.shape[3]
    rows_to = CAP * BLOCK
    depth = DEPTH * rows_to
    strip = depth // halves
    labels = pltpu.make_async_copy(arrived_ref.at[:, depth : depth + 16, :], label_rows, sem_in.at[0])
    labels.start()
    loads = [
        pltpu.make_async_copy(
            arrived_ref.at[:, at * strip : (at + 1) * strip, :],
            arrived.at[:, at * strip : (at + 1) * strip, :],
            sem_in.at[1 + at],
        )
        for at in range(halves)
    ]
    for load in loads:
        load.start()
    shape = (BLOCK, block_rows * breadth)
    place = lax.broadcasted_iota(jnp.int32, shape, 1) - lax.broadcasted_iota(jnp.int32, shape, 0)
    place = place.astype(F32)
    labels.wait()

    def select(source, _):
        label = label_rows[source].astype(F32) * BLOCK
        for rank in range(CAP):
            at = rank * (128 // CAP)
            hit = (place == label[:, at : at + 1]).astype(F32).astype(BF16)
            row = pl.multiple_of(source * rows_to + rank * BLOCK, BLOCK)
            chosen[pl.ds(row, BLOCK), :] = hit
        return 0

    lax.fori_loop(0, devices, select, 0, unroll=4)
    stores = []
    for half in range(halves):
        loads[half].wait()
        for at in range(strip // rows_to):
            row = half * strip + at * rows_to
            tile = arrived[:, row : row + rows_to, :]
            flat[at * 128 : (at + 1) * 128, :] = tile.reshape(devices * rows_to, 128).T
        for band in range(block_rows):
            summed = jnp.dot(
                flat[...], chosen[:, band * breadth : (band + 1) * breadth], preferred_element_type=F32
            )
            slot = half * block_rows + band
            frame[slot] = jnp.swapaxes(summed.reshape(part, channels, breadth), 0, 1)
            stores.append(
                pltpu.make_async_copy(frame.at[slot], out_ref.at[:, band, half], sem_out.at[slot])
            )
            stores[-1].start()
    for store in stores:
        store.wait()


def unpack(sizes, arrived):
    channels, height, breadth = sizes
    block_rows = height // BLOCK
    devices = arrived.shape[0]
    rows_to = CAP * BLOCK
    part = 8
    halves = BLOCK // part
    hbm = pl.BlockSpec(memory_space=pl.ANY)
    return pl.pallas_call(
        functools.partial(unpack_kernel, channels, breadth),
        in_specs=[hbm],
        out_specs=hbm,
        out_shape=jax.ShapeDtypeStruct((channels, block_rows, halves, part, breadth), F32),
        scratch_shapes=[
            pltpu.VMEM((devices, DEPTH * rows_to, 128), BF16),
            pltpu.VMEM((devices, 16, 128), BF16),
            pltpu.VMEM((devices * rows_to, block_rows * breadth), BF16),
            pltpu.VMEM((part * channels, devices * rows_to), BF16),
            pltpu.VMEM((halves * block_rows, channels, part, breadth), F32),
            pltpu.SemaphoreType.DMA((1 + halves,)),
            pltpu.SemaphoreType.DMA((halves * block_rows,)),
        ],
        compiler_params=params(),
        name="unpack",
    )(arrived)


def shift_pairs(axis, step):
    count = lax.axis_size(axis)
    return [(i, i + step) for i in range(count) if 0 <= i + step < count]


def finish_kernel(channels, factor, total_ref, other_ref, w1_ref, w2_ref, b1_ref, b2_ref, terms):
    ch = channels
    half = total_ref.shape[0]
    bit = lax.rem(lax.axis_index("rows") * lax.axis_size("cols") + lax.axis_index("cols"), 2)
    terms[pl.ds(pl.multiple_of(bit * half, 8), half), :] = total_ref[...] * factor
    terms[pl.ds(pl.multiple_of((1 - bit) * half, 8), half), :] = other_ref[...] * factor
    tile = lambda at: terms[at * 3 * ch : (at + 1) * 3 * ch, :]
    for out, parts in ((w1_ref, ((0, 0), (0, 1), (1, 0))), (w2_ref, ((1, 1), (2, 0), (2, 1)))):
        for row, (at, side) in enumerate(parts):
            value = pltpu.roll(tile(at), ch, 1) if side else tile(at)
            for col in range(3):
                out[row, col] = value[col * ch : (col + 1) * ch, 0:ch]
    bias = terms[9 * ch : 9 * ch + 8, :]
    b1_ref[...] = bias[0:1, 0:ch]
    b2_ref[...] = pltpu.roll(bias, ch, 1)[0:1, 0:ch]


def finish(channels, factor, total, other):
    vmem = pl.BlockSpec(memory_space=pltpu.VMEM)
    kernel = jax.ShapeDtypeStruct((3, 3, channels, channels), F32)
    bias = jax.ShapeDtypeStruct((1, channels), F32)
    w1, w2, b1, b2 = pl.pallas_call(
        functools.partial(finish_kernel, channels, factor),
        in_specs=[vmem, vmem],
        out_specs=[vmem] * 4,
        out_shape=[kernel, kernel, bias, bias],
        scratch_shapes=[pltpu.VMEM((2 * total.shape[0], 128), F32)],
        compiler_params=params(),
        name="finish",
    )(total, other)
    order = (2, 3, 0, 1)
    return jnp.transpose(w1, order), b1[0], jnp.transpose(w2, order), b2[0]


def total_over_devices(terms, devices, arrived, frame_of):
    me = lax.axis_index(AXES)
    swap = lambda value, step: lax.ppermute(value, AXES, [(i, i ^ step) for i in range(devices)])
    bit = me % 2
    half = terms.shape[0] // 2
    mine = lax.dynamic_slice_in_dim(terms, bit * half, half, 0)
    away = lax.dynamic_slice_in_dim(terms, (1 - bit) * half, half, 0)
    total = mine + swap(away, 1)
    step = 2
    while 2 * step < devices:
        total = total + swap(total, step)
        step *= 2
    other = swap(total, step)
    frame = frame_of(arrived)
    other, frame = lax.optimization_barrier((other, frame))
    total = total + other
    return total, swap(total, 1), frame


def body(warped, cotangent, w_first, b_first, w_second, source_tile, source_block):
    sizes = warped.shape
    channels, height, breadth = sizes
    row_count = lax.axis_size("rows")
    col_count = lax.axis_size("cols")
    devices = row_count * col_count
    slots = devices * CAP
    factor = 1.0 / math.sqrt(height * row_count * breadth * col_count)
    me = lax.axis_index(AXES)

    block_rows = height // BLOCK
    count = source_tile.size
    target = source_tile.reshape(count)
    same = target[:, None] == target[None, :]
    earlier = jnp.arange(count)[None, :] < jnp.arange(count)[:, None]
    ranking = jnp.sum((same & earlier).astype(jnp.int32), axis=1)
    places = target * CAP + ranking
    target_row = (
        places.reshape(block_rows, -1, 1) * BLOCK + jnp.arange(BLOCK, dtype=jnp.int32)
    ).reshape(block_rows, breadth)
    hits = places[:, None] == jnp.arange(slots, dtype=jnp.int32)[None, :]
    labels = jnp.sum(jnp.where(hits, source_block.reshape(count, 1) + 1, 0), axis=0) - 1
    xw, xc, to_right, to_left, to_up, to_down, first, second_back, first_back, bias = reorder(
        warped, cotangent, w_first, w_second, b_first
    )
    rim = 2 * channels
    side = lax.ppermute(to_right, "cols", shift_pairs("cols", 1)) + lax.ppermute(
        to_left, "cols", shift_pairs("cols", -1)
    )
    to_down = lax.dynamic_update_slice(to_down, side[:, -rim:], (2 * rim, 0))
    to_up = lax.dynamic_update_slice(to_up, side[:, :rim], (2 * rim, 0))
    up = lax.ppermute(to_down, "rows", shift_pairs("rows", 1))
    down = lax.ppermute(to_up, "rows", shift_pairs("rows", -1))

    *state, gw_mid = inner(
        sizes, (xw, xc, side, first, second_back, first_back, bias, target_row, labels), slots
    )
    packed, act_in, act_mid, g_mid = outer(
        sizes,
        (
            xw, xc, up, down, side,
            first, second_back, first_back, bias, target_row, gw_mid,
        ),
        state,
        slots,
    )
    arrived = lax.all_to_all(packed, AXES, split_axis=0, concat_axis=0, tiled=True)

    terms = correlate(sizes, act_in, act_mid, g_mid, xc)
    fill = jnp.zeros((-terms.shape[0] % 16, 128), F32)
    total, other, frame = total_over_devices(
        jnp.concatenate([terms, fill], axis=0),
        devices,
        arrived,
        functools.partial(unpack, sizes),
    )
    return (frame.reshape(sizes), *finish(channels, factor, total, other))


def solution(mesh):
    in_specs = (
        P(None, "rows", "cols"),
        P(None, "rows", "cols"),
        P(),
        P(),
        P(),
        P("rows", "cols"),
        P("rows", "cols"),
    )
    out_specs = (P(None, "rows", "cols"), P(), P(), P(), P())
    return jax.shard_map(body, mesh=mesh, in_specs=in_specs, out_specs=out_specs, check_vma=False)
```
